128 devices in a mesh: seq: 2 (over core), dp: 64 (over z, x, y).
Axes of the slice: x: 4, y: 4, z: 4, core: 2. Of those that a mesh axis runs over, the one named last changes fastest.
Arguments:
- tokens: bfloat16 [16384, 1536], P(('dp', 'seq')), may hold values from -6 to 6
- out_grad: bfloat16 [16384, 1536], P(('dp', 'seq')), may hold values from -6 to 6
- lengths: int32 [64, 4], P('dp'), may hold values from 1 to 192, 256 in all within a row
- routes: int32 [16384, 6], P(('dp', 'seq')), may hold values from 0 to 63, all different within a row; in each aligned block of 128 rows (0 to 127, 128 to 255, ...) at most 24 rows name the same one
- in_norm: bfloat16 [1536], P(('seq', 'dp')), may hold values from 0.5 to 1.5
- in_proj: bfloat16 [1536, 6448], P(('seq', 'dp')), may hold values from -0.15625 to 0.15625
- conv_weight: bfloat16 [3328, 4], P(('seq', 'dp')), may hold values from -3 to 3
- conv_bias: bfloat16 [3328], P(('seq', 'dp')), may hold values from -2 to 2
- head_params: bfloat16 [3, 48], replicated, may hold values from -5 to 1.5, as said below
- mixer_norm: bfloat16 [3072], P(('seq', 'dp')), may hold values from 0.5 to 1.5
- out_proj: bfloat16 [3072, 1536], P(('seq', 'dp')), may hold values from -0.109375 to 0.109375
- ffn_norm: bfloat16 [1536], P(('seq', 'dp')), may hold values from 0.5 to 1.5
- router: bfloat16 [1536, 64], P(('seq', 'dp')), may hold values from -0.078125 to 0.078125
- shared_gate_up: bfloat16 [1536, 2048], P(('seq', 'dp')), may hold values from -0.15625 to 0.15625
- shared_down: bfloat16 [1024, 1536], P(('seq', 'dp')), may hold values from -0.25 to 0.25
- expert_gate_up: bfloat16 [64, 1536, 1024], P('dp', 'seq'), may hold values from -0.15625 to 0.15625
- expert_down: bfloat16 [64, 512, 1536], P('dp', 'seq'), may hold values from -0.5 to 0.5
Outputs:
- block_out: bfloat16 [16384, 1536], P(('dp', 'seq'))
- token_grad: bfloat16 [16384, 1536], P(('dp', 'seq'))
- in_norm_grad: float32 [1536], P(('seq', 'dp'))
- in_proj_grad: float32 [1536, 6448], P(('seq', 'dp'))
- conv_weight_grad: float32 [3328, 4], P(('seq', 'dp'))
- conv_bias_grad: float32 [3328], P(('seq', 'dp'))
- head_grad: float32 [3, 48], replicated
- mixer_norm_grad: float32 [3072], P(('seq', 'dp'))
- out_proj_grad: float32 [3072, 1536], P(('seq', 'dp'))
- ffn_norm_grad: float32 [1536], P(('seq', 'dp'))
- router_grad: float32 [1536, 64], P(('seq', 'dp'))
- shared_gate_up_grad: float32 [1536, 2048], P(('seq', 'dp'))
- shared_down_grad: float32 [1024, 1536], P(('seq', 'dp'))
- expert_gate_up_grad: float32 [64, 1536, 1024], P('dp', 'seq')
- expert_down_grad: float32 [64, 512, 1536], P('dp', 'seq')
The draws below stay inside these ranges and needn't reach their ends.
Inputs may be any that keep to these rules, and one draw needn't show every extreme that they name: Row g holds the lengths of the 4 sequences packed in order into the 256 tokens of group g; each row sums to 256, and its longest sequence has exactly 192 tokens. `routes`: each row names 6 different experts. Among the rows of one device (aligned blocks of 128 rows) no expert is named more than 24 times, and 24 is reached. `head_params`: row 0 holds the logarithms of the heads' decay rates, row 1 the biases of their step sizes, row 2 their skip weights.
All inputs are finite; a program needn't handle non-finite values.
Results may differ from the reference program's by a relative error of at most 0.022.
Values may be sent and summed in bfloat16 or wider, within the bound.
A program may use at most 448 MiB of HBM per device.

```python
import math
import jax
import jax.numpy as jnp
import numpy as np
from jax import lax

D = 1536
HEADS = 48
HDIM = 64
CONV = 4
FE = 512
FS = 1024
TOPK = 6
TOK_DEV = 128
SEQS = 4
BLOCK = 128
INNER = 3072
XBC = 3328
PROJ = 6448
EXPERTS = 64
CAP = 24
TOKENS = 16384
LONGEST = 192
N_DP = 64


def draw_head_params(key, part):
    key = jax.random.fold_in(key, 11)
    uniform_rows = jax.random.uniform(key, (3, HEADS), jnp.float32)
    log_lower = math.log(0.05)
    log_upper = math.log(4.0)
    decay_log = log_lower + (log_upper - log_lower) * uniform_rows[0]
    step_bias = -5.0 + 2.0 * uniform_rows[1]
    skip_weight = 0.5 + uniform_rows[2]
    return jnp.stack([decay_log, step_bias, skip_weight]).astype(jnp.bfloat16)


def shard_levels(rng, extent, shards, smallest, top_value):
    loudness, own = 1.0, jax.random.fold_in(rng, 6)
    for position, shards_of in shards:
        heights = jnp.exp(jax.random.uniform(jax.random.fold_in(own, position), (shards_of,), jnp.float32, smallest / len(shards), top_value / len(shards)))
        loudness = loudness * jnp.repeat(heights, extent[position] // shards_of).reshape([-1 if axis == position else 1 for axis in range(len(extent))])
    return loudness


def length_profile(number_of, total, reach, skew):
    portions = [(1 << 20) // math.isqrt(grade ** skew) + 1 for grade in range(2, number_of + 1)]
    spare, holding = total - reach - (number_of - 1), [1] * (number_of - 1)
    while spare > 0:
        candidates = [i for i in range(number_of - 1) if holding[i] < reach]
        mass, remaining = sum([portions[i] for i in candidates]), spare
        for i in candidates:
            more = min(reach - holding[i], max(1, remaining * portions[i] // mass), spare)
            holding[i] = holding[i] + more
            spare = spare - more
    return np.array([reach] + holding)


def uneven_parts(rng, count, total, limit, lean):
    if count == 2:
        one = jax.random.randint(rng, (), max(1, total - limit), min(limit, total - 1) + 1)
        return jnp.stack([one, total - one])
    tallies = jnp.asarray(length_profile(count, total, limit, lean), jnp.int32)
    twos = (count - 1) // 2
    donor, taker = tallies[1:1 + 2 * twos:2], tallies[2:2 + 2 * twos:2]
    margin = jnp.minimum(donor - 1, limit - taker)
    moved = jax.random.randint(jax.random.fold_in(rng, 1), (twos,), 0, 1 << 20) % (margin + 1)
    tallies = tallies.at[1:1 + 2 * twos:2].set(donor - moved).at[2:2 + 2 * twos:2].set(taker + moved)
    return tallies[jax.random.permutation(jax.random.fold_in(rng, 2), count)]


def routed_block(stream_key, own, number, rows, amount, top, most, skew):
    order = jax.random.permutation(stream_key, amount)
    heavy_load, ordinary = load_shares(amount, rows * top, most, skew, True), load_shares(amount, rows * top, most, skew, False)
    places = jnp.arange(amount)

    def named(sizes, turn):
        used = int((sizes > 0).sum())
        fixed = max(1, used // 4)
        shifted = fixed + (places - fixed + turn * (used - fixed)) % max(1, amount - fixed)
        return jnp.zeros((amount,), jnp.int32).at[order[jnp.where(places < fixed, places, shifted)]].set(jnp.asarray(sizes, jnp.int32))

    sizes = jnp.where(number % 4 == 0, named(heavy_load, number // 4), named(ordinary, number - number // 4 - 1))
    mixed = jax.random.permutation(jax.random.fold_in(own, 3), amount)
    donor, sink = mixed[0:amount // 2 * 2:2], mixed[1:amount // 2 * 2:2]
    room = jnp.minimum(sizes[donor] - 1, most - sizes[sink]) // 2
    room = jnp.where((donor == order[0]) | (sink == order[0]) | (sizes[sink] == 0), 0, jnp.maximum(room, 0))
    shifted = jax.random.randint(jax.random.fold_in(own, 4), (amount // 2,), 0, 1 << 20) % (room + 1)
    sizes = sizes.at[donor].add(-shifted).at[sink].add(shifted)
    items = jnp.searchsorted(jnp.cumsum(sizes), jnp.arange(rows * top), side="right").astype(jnp.int32)
    grid = items.reshape(top, rows).T
    grid = grid[jax.random.permutation(jax.random.fold_in(own, 1), rows)]
    turn = jax.random.randint(jax.random.fold_in(own, 2), (rows, 1), 0, top)
    return jnp.take_along_axis(grid, (jnp.arange(top)[None, :] + turn) % top, axis=1)


def load_shares(count, total, bound, slope, full):
    loads = [(1 << 20) // math.isqrt(rank ** slope) + 1 for rank in range(1, count + 1)]
    largest = bound if full else min(bound, max(-(-total // count), total * loads[0] // sum(loads)))
    least = 1 if total - largest >= count - 1 else 0
    counts, rest = [largest] + [least] * (count - 1), total - largest - least * (count - 1)
    while rest > 0:
        free = [i for i in range(1, count) if counts[i] < largest] or [i for i in range(1, count) if counts[i] < bound]
        mass, budget = sum([loads[i] for i in free]), rest
        for i in free:
            more = min(bound - counts[i], max(1, budget * loads[i] // mass), rest)
            counts[i] = counts[i] + more
            rest = rest - more
    return np.array(counts)


def centred(stream_key, extent, scale, most, cuts=(), kind=jnp.bfloat16):
    result = jax.random.normal(stream_key, extent, jnp.float32) * scale
    if len(cuts) > 0:
        result = shard_levels(stream_key, extent, cuts, -0.22, 0.18) * result
    return jnp.clip(result, min=-most, max=most).astype(kind)


def setup_inputs(seed: int = 0) -> dict:
    streams_of = jax.random.split(jax.random.key(seed), 18)
    tokens = centred(streams_of[0], (TOKENS, D), 1.0, 6.0, ((0, 128),))
    out_grad = centred(streams_of[1], (TOKENS, D), 1.0, 6.0, ((0, 128),))
    lengths = jax.vmap(lambda own: uneven_parts(own, SEQS, 2 * TOK_DEV, LONGEST, 2))(jax.random.split(streams_of[2], N_DP)).reshape((N_DP, SEQS)).astype(jnp.int32)
    routes_keys = jax.random.split(jax.random.fold_in(streams_of[3], 1), TOKENS // TOK_DEV)
    routes_turns = jax.random.permutation(jax.random.fold_in(streams_of[3], 3), TOKENS // TOK_DEV)
    routes = jax.vmap(lambda own, number: routed_block(jax.random.fold_in(streams_of[3], 2), own, number, TOK_DEV, EXPERTS, TOPK, CAP, 2))(routes_keys, routes_turns).reshape((TOKENS, TOPK))
    in_norm = jnp.clip(1.0 + 0.1 * jax.random.normal(streams_of[4], (D,), jnp.float32), 0.5, 1.5).astype(jnp.bfloat16)
    in_proj = centred(streams_of[5], (D, PROJ), D ** -0.5, 0.15625, ((0, 128),))
    conv_weight = centred(streams_of[6], (XBC, CONV), CONV ** -0.5, 3.0, ((0, 128),))
    conv_bias = centred(streams_of[7], (XBC,), 0.3, 2.0, ((0, 128),))
    head_params = draw_head_params(jax.random.fold_in(streams_of[17], 71), 0)
    mixer_norm = jnp.clip(1.0 + 0.1 * jax.random.normal(streams_of[9], (INNER,), jnp.float32), 0.5, 1.5).astype(jnp.bfloat16)
    out_proj = centred(streams_of[10], (INNER, D), INNER ** -0.5, 0.109375, ((0, 128),))
    ffn_norm = jnp.clip(1.0 + 0.1 * jax.random.normal(streams_of[11], (D,), jnp.float32), 0.5, 1.5).astype(jnp.bfloat16)
    router = centred(streams_of[12], (D, EXPERTS), (4 * D) ** -0.5, 0.078125, ((0, 128),))
    shared_gate_up = centred(streams_of[13], (D, 2 * FS), D ** -0.5, 0.15625, ((0, 128),))
    shared_down = centred(streams_of[14], (FS, D), (FS // 2) ** -0.5, 0.25, ((0, 128),))
    expert_gate_up = centred(streams_of[15], (EXPERTS, D, 2 * FE), D ** -0.5, 0.15625, ((0, 64), (1, 2)))
    expert_down = centred(streams_of[16], (EXPERTS, FE, D), (FE // 4) ** -0.5, 0.5, ((0, 64), (1, 2)))
    return dict(tokens=tokens, out_grad=out_grad, lengths=lengths, routes=routes, in_norm=in_norm, in_proj=in_proj, conv_weight=conv_weight, conv_bias=conv_bias, head_params=head_params, mixer_norm=mixer_norm, out_proj=out_proj, ffn_norm=ffn_norm, router=router, shared_gate_up=shared_gate_up, shared_down=shared_down, expert_gate_up=expert_gate_up, expert_down=expert_down)


epsilon = 1e-05
highest = lax.Precision.HIGHEST

@jax.custom_vjp
def low(v):
    return lax.optimization_barrier(v.astype(jnp.bfloat16)).astype(jnp.float32)

@jax.custom_vjp
def low_back(v):
    return v

def low_keep(v):
    return (low(v), None)

def low_pass(kept, grad):
    return (grad,)

def back_keep(v):
    return (v, None)

def back_low(kept, grad):
    return (low(grad),)
low.defvjp(low_keep, low_pass)
low_back.defvjp(back_keep, back_low)

def matmul_high(left_op, right_op):
    return jnp.dot(left_op, right_op, precision=highest, preferred_element_type=jnp.float32)

def rms_scale(values, gain_vec):
    return values * lax.rsqrt(lax.optimization_barrier(jnp.mean(values * values, axis=-1, keepdims=True)) + epsilon) * gain_vec

def swish_product(gate_up):
    half_width = gate_up.shape[-1] // 2
    return jax.nn.silu(gate_up[..., :half_width]) * gate_up[..., half_width:]

def conv_taps(padded, pad_segment, segment, conv_w, conv_b):
    length = segment.shape[0]
    running = jnp.zeros((length, conv_w.shape[0]), jnp.float32) + conv_b[None, :]
    for tap_index in range(conv_w.shape[1]):
        same_doc = (pad_segment[tap_index:tap_index + length] == segment).astype(jnp.float32)
        running = running + conv_w[:, tap_index][None, :] * padded[tap_index:tap_index + length] * same_doc[:, None]
    return jax.nn.silu(running)

def ssd_blocks(x_heads, b_mat, c_mat, rate_vals, step_vals, skip_vals, segment):
    length, head_count, head_dim = x_heads.shape
    state_dim = b_mat.shape[1]
    blocks = length // BLOCK
    positions = jnp.arange(BLOCK, dtype=jnp.int32)
    causal = positions[:, None] >= positions[None, :]

    def one_block(carry_in, pieces):
        held_state, held_segment = carry_in
        x_blk, b_blk, c_blk, r_blk, s_blk, g_blk = pieces
        cum_rate = jnp.cumsum(r_blk, axis=0)
        inside = (g_blk[:, None] == g_blk[None, :]) & causal
        inside_f = inside.astype(jnp.float32)[:, :, None]
        spread = cum_rate[:, None, :] - cum_rate[None, :, :]
        decays = jnp.exp(jnp.where(inside[:, :, None], spread, -80.0)) * inside_f
        scores = matmul_high(c_blk, b_blk.T)
        mixing = decays * scores[:, :, None] * s_blk[None, :, :]
        inner_part = jnp.einsum('tsh,shp->thp', mixing, x_blk, precision=highest)
        carried = (g_blk == held_segment).astype(jnp.float32)[:, None] * jnp.exp(cum_rate)
        outer_part = jnp.einsum('tn,hpn->thp', c_blk, held_state, precision=highest) * carried[:, :, None]
        outputs = inner_part + outer_part + skip_vals[None, :, None] * x_blk
        last_segment = g_blk[-1]
        tail_w = jnp.exp(cum_rate[-1][None, :] - cum_rate) * (g_blk == last_segment).astype(jnp.float32)[:, None] * s_blk
        keep_old = (last_segment == held_segment).astype(jnp.float32) * jnp.exp(cum_rate[-1])
        new_state = keep_old[:, None, None] * held_state + jnp.einsum('sh,shp,sn->hpn', tail_w, x_blk, b_blk, precision=highest)
        return ((new_state, last_segment), outputs)
    pieces = (x_heads.reshape(blocks, BLOCK, head_count, head_dim), b_mat.reshape(blocks, BLOCK, state_dim), c_mat.reshape(blocks, BLOCK, state_dim), rate_vals.reshape(blocks, BLOCK, head_count), step_vals.reshape(blocks, BLOCK, head_count), segment.reshape(blocks, BLOCK))
    initial = (jnp.zeros((head_count, head_dim, state_dim), jnp.float32), jnp.array(-1, jnp.int32))
    final_carry, outputs = lax.scan(jax.checkpoint(one_block), initial, pieces)
    return (outputs.reshape(length, head_count, head_dim), final_carry[0])

def mixer_group(group_x, segment, g_in, w_in, w_conv, b_conv, heads_p, g_mix, w_out):
    length = group_x.shape[0]
    inner_w = g_mix.shape[0]
    xbc_width = w_conv.shape[0]
    kernel = w_conv.shape[1]
    state_dim = (xbc_width - inner_w) // 2
    normed = low(rms_scale(group_x, g_in))
    projected = low_back(low(matmul_high(normed, w_in)))
    gate_z = projected[:, :inner_w]
    xbc_rows = projected[:, inner_w:inner_w + xbc_width]
    step_raw = projected[:, inner_w + xbc_width:]
    padded = jnp.concatenate([jnp.zeros((kernel - 1, xbc_width), jnp.float32), xbc_rows], axis=0)
    pad_segment = jnp.concatenate([jnp.full((kernel - 1,), -1, jnp.int32), segment])
    conv_out = conv_taps(padded, pad_segment, segment, w_conv, b_conv)
    step_vals = jax.nn.softplus(step_raw + heads_p[1][None, :])
    rate_vals = -step_vals * jnp.exp(heads_p[0])[None, :]
    x_heads = conv_out[:, :inner_w].reshape(length, HEADS, HDIM)
    mixer_y, _ = ssd_blocks(x_heads, conv_out[:, inner_w:inner_w + state_dim], conv_out[:, inner_w + state_dim:], rate_vals, step_vals, heads_p[2], segment)
    gated = mixer_y.reshape(length, inner_w) * jax.nn.silu(gate_z)
    mixer_out = low(rms_scale(gated, g_mix))
    return group_x + low_back(matmul_high(mixer_out, w_out))

def expert_rows(ffn_rows, gate_vals, gate_up, down_w, route_ids, valid_rows):
    picked = low_back(ffn_rows[route_ids // TOPK] * valid_rows[:, None])
    expert_gu = low_back(matmul_high(picked, gate_up))
    expert_act = low(swish_product(expert_gu))
    expert_out = low_back(low(matmul_high(expert_act, down_w)))
    return expert_out * (gate_vals[route_ids] * valid_rows)[:, None]

def reference(tokens, out_grad, lengths, routes, in_norm, in_proj, conv_weight, conv_bias, head_params, mixer_norm, out_proj, ffn_norm, router, shared_gate_up, shared_down, expert_gate_up, expert_down):
    groups = lengths.shape[0]
    span = tokens.shape[0] // groups
    seq_ends = jnp.cumsum(lengths, axis=1).astype(jnp.int32)
    positions = jnp.arange(span, dtype=jnp.int32)
    segments = lax.optimization_barrier(jnp.sum((positions[None, :, None] >= seq_ends[:, None, :]).astype(jnp.int32), axis=2)).astype(jnp.int32)
    route_count = routes.shape[0] * routes.shape[1]
    flat_routes = routes.reshape(route_count)
    sorted_ids = jnp.argsort(flat_routes, stable=True).astype(jnp.int32)
    expert_ids = jnp.arange(EXPERTS, dtype=jnp.int32)
    per_expert = lax.optimization_barrier(jnp.sum((flat_routes[None, :] == expert_ids[:, None]).astype(jnp.int32), axis=1)).astype(jnp.int32)
    starts = (jnp.cumsum(per_expert) - per_expert).astype(jnp.int32)
    most_rows = CAP * (tokens.shape[0] // TOK_DEV)
    slots = jnp.arange(most_rows, dtype=jnp.int32)
    valid = slots[None, :] < per_expert[:, None]
    where_sorted = jnp.minimum(starts[:, None] + slots[None, :], route_count - 1).astype(jnp.int32)
    route_table = jnp.where(valid, sorted_ids[where_sorted], 0).astype(jnp.int32)
    valid_table = valid.astype(jnp.float32)

    def forward(block_in, g_in, w_in, w_conv, b_conv, heads_p, g_mix, w_out, g_ffn, w_router, w_sgu, w_sdown, w_egu, w_edown):

        def group_step(unused, pieces):
            return (unused, jax.checkpoint(mixer_group)(pieces[0], pieces[1], g_in, w_in, w_conv, b_conv, heads_p, g_mix, w_out))
        _, residual = lax.scan(group_step, None, (block_in.reshape(groups, span, block_in.shape[1]), segments))
        residual = residual.reshape(block_in.shape)
        ffn_in = low(rms_scale(residual, g_ffn))
        logits = matmul_high(ffn_in, w_router)
        chosen = jnp.take_along_axis(logits, routes, axis=1)
        gating = jax.nn.softmax(chosen, axis=-1)
        gate_flat = gating.reshape(route_count)
        shared_gu = low_back(matmul_high(ffn_in, w_sgu))
        shared_act = low(swish_product(shared_gu))
        shared_out = low_back(matmul_high(shared_act, w_sdown))

        def add_expert(running, pieces):
            gate_up, down_w, route_ids, valid_rows = pieces
            contrib = jax.checkpoint(expert_rows)(ffn_in, gate_flat, gate_up, down_w, route_ids, valid_rows)
            return (running.at[route_ids // TOPK].add(contrib), None)
        routed, _ = lax.scan(add_expert, jnp.zeros_like(residual), (w_egu, w_edown, route_table, valid_table))
        return residual + shared_out + routed
    floats = tuple((array_in.astype(jnp.float32) for array_in in (tokens, in_norm, in_proj, conv_weight, conv_bias, head_params, mixer_norm, out_proj, ffn_norm, router, shared_gate_up, shared_down, expert_gate_up, expert_down)))
    block_out, pullback = jax.vjp(forward, *floats)
    gradients = pullback(out_grad.astype(jnp.float32))
    return (block_out.astype(jnp.bfloat16), gradients[0].astype(jnp.bfloat16), gradients[1], gradients[2], gradients[3], gradients[4], gradients[5], gradients[6], gradients[7], gradients[8], gradients[9], gradients[10], gradients[11], gradients[12], gradients[13])
```

```python
import functools

import jax
import jax.numpy as jnp
import numpy as np
from jax import lax
from jax.experimental import pallas as pl
from jax.experimental.pallas import tpu as pltpu
from jax.sharding import Mesh
from jax.sharding import PartitionSpec as P

DP = ("z", "x", "y")
ALL = ("seq", "z", "x", "y")
DP_SEQ = ("z", "x", "y", "seq")
ORDER = (("z", "x", "y"), ("x", "y", "z"), ("y", "z", "x"))
REM = (("z", "x"), ("y", "x"), ("y", "z"))
MESH_ID = pl.DeviceIdType.MESH
EPS = 1e-05
f32 = jnp.float32
bf16 = jnp.bfloat16

ROWS_FIRST = (("y", "s", "z", "x"), "rows")
CHANNELS = (("y", "z", "x", "s"), "cols")
SPECS = (ROWS_FIRST, ROWS_FIRST, CHANNELS, CHANNELS)


def dot(a, b, dims=((1,), (0,))):
    return lax.dot_general(a, b, (dims, ((), ())), preferred_element_type=f32)


def neighbours():
    pos = {a: lax.axis_index(a) for a in DP}
    right = {a: lax.rem(pos[a] + 1, 4) for a in DP}
    left = {a: lax.rem(pos[a] + 3, 4) for a in DP}
    opp = {a: lax.rem(pos[a] + 2, 4) for a in DP}
    return pos, right, left, opp


def greet(right, left):
    barrier = pltpu.get_barrier_semaphore()
    for a in DP:
        for n in (right[a], left[a]):
            pl.semaphore_signal(barrier, inc=1, device_id={a: n}, device_id_type=MESH_ID)
    pl.semaphore_wait(barrier, 6)


def third(shape, split, a):
    rows, cols = shape[-2:]
    if split == "rows":
        return (pl.ds(rows // 3 * a, rows // 3), slice(None))
    return (slice(None), pl.ds(cols // 3 * a, cols // 3))


def third_shape(shape, split):
    rows, cols = shape[-2:]
    return (rows // 3, cols) if split == "rows" else (rows, cols // 3)


def region(ref, spec, free, fixed, a, s=None):
    order, split = spec
    ix = []
    for d in order:
        if d == "s":
            ix.append(slice(None) if s is None else s)
        else:
            ix.append(slice(None) if d in free else fixed[d])
    return ref.at[tuple(ix) + third(ref.shape, split, a)]


def gather_kernel(specs, *refs):
    n = len(specs)
    ins, outs, (send, recv, loc) = refs[:n], refs[n : 2 * n], refs[2 * n :]
    pos, right, left, opp = neighbours()
    own = []
    for i in range(n):
        ix = tuple(slice(None) if d == "s" else pos[d] for d in specs[i][0])
        c = pltpu.make_async_copy(ins[i], outs[i].at[ix], loc.at[i])
        c.start()
        own.append(c)
    greet(right, left)
    sends = []

    def remote(i, st, a, k, src, dst, ax, to):
        c = pltpu.make_async_remote_copy(
            src_ref=src,
            dst_ref=dst,
            send_sem=send.at[i, st, a, k],
            recv_sem=recv.at[i, st, a, k],
            device_id={ax: to},
            device_id_type=MESH_ID,
        )
        c.start()
        sends.append(c)
        return c

    for st in range(3):
        first, later = {}, []
        for i in range(n):
            for a in range(3):
                ax, free = ORDER[a][st], ORDER[a][:st]
                dst = region(outs[i], specs[i], free, pos, a)
                src = dst
                if st == 0:
                    src = ins[i].at[(slice(None),) + third(ins[i].shape, specs[i][1], a)]
                for d, to in enumerate((right[ax], left[ax])):
                    first[i, a, d] = remote(i, st, a, d, src, dst, ax, to)
        for i in range(n):
            for a in range(3):
                ax, free = ORDER[a][st], ORDER[a][:st]
                for d, (to, frm) in enumerate(((right[ax], left[ax]), (left[ax], right[ax]))):
                    first[i, a, d].wait_recv()
                    r = region(outs[i], specs[i], free, {**pos, ax: frm}, a, s=d)
                    later.append(remote(i, st, a, 2 + d, r, r, ax, to))
        for c in later:
            c.wait_recv()
        if st == 0:
            for c in own:
                c.wait()
    for c in sends:
        c.wait_send()


def gather(arrays, specs, collective_id):
    n = len(arrays)
    sizes = {"y": 4, "z": 4, "x": 4, "s": 2}
    outs = [
        jax.ShapeDtypeStruct(tuple(sizes[d] for d in spec[0]) + v.shape[1:], v.dtype)
        for v, spec in zip(arrays, specs)
    ]
    moved = sum(int(np.prod(o.shape)) for o in outs) * 2
    return pl.pallas_call(
        functools.partial(gather_kernel, specs),
        out_shape=outs,
        in_specs=[pl.BlockSpec(memory_space=pl.ANY)] * n,
        out_specs=[pl.BlockSpec(memory_space=pl.ANY)] * n,
        scratch_shapes=[
            pltpu.SemaphoreType.DMA((n, 3, 3, 4)),
            pltpu.SemaphoreType.DMA((n, 3, 3, 4)),
            pltpu.SemaphoreType.DMA((n,)),
        ],
        compiler_params=pltpu.CompilerParams(collective_id=collective_id, has_side_effects=True),
        cost_estimate=pl.CostEstimate(flops=0, bytes_accessed=2 * moved, transcendentals=0),
        name="gather_weights",
    )(*arrays)


def each(lead, fn):
    if not lead:
        fn((Ellipsis,))
        return

    @pl.loop(0, int(np.prod(lead)))
    def _(i):
        ix = []
        for d in reversed(lead):
            ix.append(lax.rem(i, d))
            i = lax.div(i, d)
        fn(tuple(reversed(ix)))


def scatter_kernel(specs, *refs):
    n = len(specs)
    gs, outs = refs[:n], refs[n : 2 * n]
    held, got = refs[2 * n : 3 * n], [refs[3 * n + 3 * i : 3 * n + 3 * i + 3] for i in range(n)]
    send, recv, loc = refs[6 * n :]
    pos, right, left, opp = neighbours()

    def source(i, st, a, idx, s):
        ax = ORDER[a][2 - st]
        if st == 0:
            return region(gs[i], specs[i], [d for d in DP if d != ax], {ax: idx}, a, s)
        part = held[i].at[a, 2 + s]
        if st == 1:
            return part.at[:, idx] if REM[a][1] == ax else part.at[idx]
        me = pos[ORDER[a][1]]
        return part.at[me, idx] if REM[a][1] == ax else part.at[idx, me]

    local = {}
    for i in range(n):
        for a in range(3):
            ax = ORDER[a][2]
            for k, (idx, s) in enumerate(((right[ax], 0), (left[ax], 1), (pos[ax], 0), (pos[ax], 1))):
                c = pltpu.make_async_copy(source(i, 0, a, idx, s), held[i].at[a, k], loc.at[i, a, k])
                c.start()
                local[i, a, k] = c
    greet(right, left)
    sends = []

    def remote(i, st, a, k, src, ax, to):
        c = pltpu.make_async_remote_copy(
            src_ref=src,
            dst_ref=got[i][st].at[a, k],
            send_sem=send.at[i, st, a, k],
            recv_sem=recv.at[i, st, a, k],
            device_id={ax: to},
            device_id_type=MESH_ID,
        )
        c.start()
        sends.append(c)
        return c

    every = [(i, a) for i in range(n) for a in range(3)]
    for st in range(3):
        lead = ((4, 4), (4,), ())[st]
        cp = {}
        for i, a in every:
            ax = ORDER[a][2 - st]
            cp[i, a, 0] = remote(i, st, a, 0, source(i, st, a, opp[ax], 0), ax, right[ax])
            cp[i, a, 1] = remote(i, st, a, 1, source(i, st, a, opp[ax], 1), ax, left[ax])
        for i, a in every:
            ax = ORDER[a][2 - st]
            cp[i, a, 2] = remote(i, st, a, 2, source(i, st, a, right[ax], 1), ax, right[ax])
            cp[i, a, 3] = remote(i, st, a, 3, source(i, st, a, left[ax], 0), ax, left[ax])
        for i, a in every:
            ax = ORDER[a][2 - st]
            for d, to in enumerate((right[ax], left[ax])):
                cp[i, a, d].wait_recv()
                if st == 0:
                    local[i, a, d].wait()
                    acc = held[i].at[a, d]
                else:
                    acc = source(i, st, a, to, d)
                more = got[i][st].at[a, d]

                def add(ix, acc=acc, more=more):
                    acc[ix] = (acc[ix].astype(f32) + more[ix].astype(f32)).astype(acc.dtype)

                each(lead, add)
                cp[i, a, 4 + d] = remote(i, st, a, 4 + d, acc, ax, to)
        for i, a in every:
            ax = ORDER[a][2 - st]
            if st == 0:
                local[i, a, 2].wait()
                local[i, a, 3].wait()
            for s, (p, q) in enumerate(((4, 3), (2, 5))):
                cp[i, a, p].wait_recv()
                cp[i, a, q].wait_recv()
                acc = held[i].at[a, 2 + s] if st == 0 else source(i, st, a, pos[ax], s)
                one, two = got[i][st].at[a, p], got[i][st].at[a, q]
                if st == 2:
                    ix = (s,) + third(outs[i].shape, specs[i][1], a)
                    outs[i][ix] = acc[...].astype(f32) + one[...].astype(f32) + two[...].astype(f32)
                else:

                    def finish(ix, acc=acc, one=one, two=two):
                        total = acc[ix].astype(f32) + one[ix].astype(f32) + two[ix].astype(f32)
                        acc[ix] = total.astype(acc.dtype)

                    each(lead, finish)
    for c in sends:
        c.wait_send()


def scatter(arrays, specs, collective_id):
    n = len(arrays)
    outs = [jax.ShapeDtypeStruct((2,) + v.shape[4:], f32) for v in arrays]
    pieces = [third_shape(v.shape, spec[1]) for v, spec in zip(arrays, specs)]
    moved = sum(int(np.prod(v.shape)) for v in arrays) * 2
    return pl.pallas_call(
        functools.partial(scatter_kernel, specs),
        out_shape=outs,
        in_specs=[pl.BlockSpec(memory_space=pl.ANY)] * n,
        out_specs=[pl.BlockSpec(memory_space=pltpu.VMEM)] * n,
        scratch_shapes=[pltpu.VMEM((3, 4, 4, 4) + p, bf16) for p in pieces]
        + [pltpu.VMEM((3, 6) + lead + p, bf16) for p in pieces for lead in ((4, 4), (4,), ())]
        + [
            pltpu.SemaphoreType.DMA((n, 3, 3, 6)),
            pltpu.SemaphoreType.DMA((n, 3, 3, 6)),
            pltpu.SemaphoreType.DMA((n, 3, 4)),
        ],
        compiler_params=pltpu.CompilerParams(
            collective_id=collective_id, has_side_effects=True, vmem_limit_bytes=56 * 2**20
        ),
        cost_estimate=pl.CostEstimate(flops=0, bytes_accessed=2 * moved, transcendentals=0),
        name="scatter_grads",
    )(*arrays)


def swap(v):
    return lax.ppermute(v, "seq", [(0, 1), (1, 0)])


def both_halves(own, other, s):
    first = jnp.where(s == 0, own, other)
    second = jnp.where(s == 0, other, own)
    return jnp.concatenate([first, second], axis=0)


def halves(v, s):
    rows = v.shape[0] // 2
    return (
        lax.dynamic_slice_in_dim(v, s * rows, rows, 0),
        lax.dynamic_slice_in_dim(v, (1 - s) * rows, rows, 0),
    )


def hi_lo(v):
    hi = v.astype(bf16)
    return hi, (v - hi.astype(f32)).astype(bf16)


def rms(v):
    return lax.rsqrt(jnp.mean(v * v, axis=-1, keepdims=True) + EPS)


def silu_grad(v):
    sig = jax.nn.sigmoid(v)
    return sig * (1.0 + v * (1.0 - sig))


def shift_down(v, d):
    return jnp.pad(v, [(0, 0)] * (v.ndim - 2) + [(d, 0), (0, 0)])[..., : v.shape[-2], :] if d else v


def shift_up(v, d):
    return jnp.pad(v, [(0, 0)] * (v.ndim - 2) + [(0, d), (0, 0)])[..., d:, :] if d else v


def conv_pre(v, same, w, b):
    total = b
    for k in range(4):
        d = 3 - k
        total = total + w[k] * (shift_down(v, d) * same[d])
    return total


def conv_back(d_pre, v, same, w):
    d_w = [jnp.sum(d_pre * (shift_down(v, 3 - k) * same[3 - k]), axis=-2) for k in range(4)]
    d_b = jnp.sum(d_pre, axis=-2)
    d_v = 0.0
    for k in range(4):
        d = 3 - k
        d_v = d_v + w[k] * shift_up(d_pre * same[d], d)
    return d_v, jnp.stack(d_w + [d_b], axis=0)


def local(
    tokens,
    out_grad,
    lengths,
    routes,
    in_norm,
    in_proj,
    conv_weight,
    conv_bias,
    head_params,
    mixer_norm,
    out_proj,
    ffn_norm,
    router,
    shared_gate_up,
    shared_down,
    expert_gate_up,
    expert_down,
):
    s = lax.axis_index("seq")
    dp = lax.axis_index(DP)
    device = s * 64 + dp
    experts, slots = 64, 24
    n_slots = experts * slots

    pieces = []
    for c in range(2):
        for j in range(4):
            at = c * 1536 + j * 384
            misc = jnp.concatenate(
                [
                    in_proj[:, 6144 + j * 64 : 6208 + j * 64],
                    router[:, j * 16 : j * 16 + 16],
                    in_proj[:, 6400 + c * 24 + j * 6 : 6406 + c * 24 + j * 6],
                    jnp.zeros((12, 42), bf16),
                ],
                axis=1,
            )
            up = 1024 + c * 512 + j * 128
            pieces.append(
                jnp.concatenate(
                    [
                        in_proj[:, at : at + 384],
                        in_proj[:, 3072 + at : 3456 + at],
                        misc,
                        shared_gate_up[:, up - 1024 : up - 896],
                        shared_gate_up[:, up : up + 128],
                    ],
                    axis=1,
                )
            )
    rows_in = lax.all_to_all(jnp.stack(pieces), ("seq", "y"), 0, 0, tiled=True).reshape(2, 48, 1152)
    out_rows = jnp.concatenate(
        [out_proj.reshape(24, 4, 384), shared_down.reshape(8, 4, 384)], axis=0
    ).transpose(1, 0, 2)
    out_rows = lax.all_to_all(out_rows, "y", 0, 0, tiled=True)
    vec = jnp.concatenate(
        [
            in_norm,
            ffn_norm,
            mixer_norm,
            conv_weight.T.reshape(-1),
            conv_bias,
            jnp.zeros((78,), bf16),
        ]
    )
    vecs = lax.all_gather(vec[None], ALL, axis=0, tiled=True)
    other_tokens = swap(tokens)
    other_grad = swap(out_grad)
    other_gate_up = swap(expert_gate_up[0])
    other_down = swap(expert_down[0])

    w_in, w_sgu, w_out, w_sdown = gather(
        (
            rows_in[:, :, :896],
            rows_in[:, :, 896:],
            out_rows[:, :24].reshape(2, 48, 384),
            out_rows[:, 24:].reshape(2, 16, 384),
        ),
        SPECS,
        1,
    )
    w_in = w_in.reshape(4, 1536, 896)
    w_sgu = w_sgu.reshape(4, 1536, 256)
    w_out = w_out.reshape(4, 1536, 384)
    w_sdown = w_sdown.reshape(4, 512, 384)

    vecs = vecs.astype(f32)
    g_in = vecs[:, :12].reshape(1536)
    g_ffn = vecs[:, 12:24].reshape(1536)
    g_mix = lax.dynamic_slice_in_dim(vecs[:, 24:48].reshape(3072), s * 1536, 1536)
    conv = vecs[:, 48:178].reshape(128, 5, 26).transpose(1, 0, 2).reshape(5, 3328)
    conv_x = lax.dynamic_slice_in_dim(conv[:, :3072], s * 1536, 1536, 1).reshape(5, 4, 1, 384)
    conv_bc = conv[:, 3072:].reshape(5, 4, 1, 64)
    heads = lax.dynamic_slice_in_dim(head_params.astype(f32), s * 24, 24, 1)
    w_eg = both_halves(expert_gate_up[0], other_gate_up, s)
    w_ed = both_halves(expert_down[0], other_down, s)

    ids = jnp.arange(experts, dtype=jnp.int32)
    named = jnp.sum((routes[:, :, None] == ids).astype(f32), axis=1)
    t128 = jnp.arange(128)
    before = (t128[:, None] > t128[None, :]).astype(bf16)
    rank = dot(before, named.astype(bf16))
    slot = jnp.arange(n_slots, dtype=jnp.int32)
    spread = (slot[None, :] // slots == ids[:, None]).astype(bf16)
    is_named = dot(named.astype(bf16), spread) > 0.5
    in_slot = dot(rank.astype(bf16), spread) == (slot % slots).astype(f32)[None, :]
    place = (is_named & in_slot).astype(bf16)

    def to_slots(v):
        return dot(place, v, ((0,), (0,))).astype(bf16).reshape(experts, slots, v.shape[1])

    grad_rows = lax.all_to_all(to_slots(out_grad), DP, 0, 0, tiled=True).reshape(n_slots, 1536)

    ends = jnp.cumsum(lengths[0])
    t256 = jnp.arange(256, dtype=jnp.int32)
    segment = jnp.sum((t256[:, None] >= ends[None, :]).astype(jnp.int32), axis=1)
    same = [
        (jnp.pad(segment, (d, 0), constant_values=-1)[:256] == segment).astype(f32)[:, None]
        for d in range(4)
    ]
    inside = (segment[:, None] == segment[None, :]) & (t256[:, None] >= t256[None, :])
    x_full = both_halves(tokens, other_tokens, s).astype(f32)
    normed = (x_full * rms(x_full) * g_in).astype(bf16)
    proj = jnp.stack([dot(normed, w_in[j]) for j in range(4)]).astype(bf16).astype(f32)
    z, x_raw, bc_raw, dt = (
        proj[..., :384],
        proj[..., 384:768],
        proj[..., 768:832],
        proj[..., 848:854],
    )
    x_pre = conv_pre(x_raw, same, conv_x[:4], conv_x[4])
    bc_pre = conv_pre(bc_raw, same, conv_bc[:4], conv_bc[4])
    x = jax.nn.silu(x_pre)
    bc = jax.nn.silu(bc_pre)
    b_mat = jnp.concatenate([bc[0], bc[1]], axis=1)
    c_mat = jnp.concatenate([bc[2], bc[3]], axis=1)
    raw = dt.transpose(1, 0, 2).reshape(256, 24) + heads[1]
    step = jax.nn.softplus(raw)
    decay = jnp.exp(heads[0])
    rate = -step * decay
    tri = (t256[:, None] >= t256[None, :]).astype(f32)
    cum = jnp.dot(tri, rate, precision=lax.Precision.HIGHEST, preferred_element_type=f32).T
    scores = dot(c_mat.astype(bf16), b_mat.astype(bf16), ((1,), (1,)))
    fade = jnp.where(inside, jnp.exp(jnp.where(inside, cum[:, :, None] - cum[:, None, :], 0.0)), 0.0)
    mixing = fade * scores * step.T[:, None, :]
    x_heads = x.reshape(4, 256, 6, 64).transpose(0, 2, 1, 3).reshape(24, 256, 64)
    x_low = x_heads.astype(bf16)
    y_heads = jnp.einsum("hts,hsp->htp", mixing.astype(bf16), x_low, preferred_element_type=f32)
    y_heads = y_heads + heads[2][:, None, None] * x_heads
    y = y_heads.reshape(4, 6, 256, 64).transpose(0, 2, 1, 3).reshape(4, 256, 384)
    gate = jax.nn.silu(z)
    gated = y * gate
    g_mix = g_mix.reshape(4, 1, 384)
    scaled = (gated * g_mix).astype(bf16)
    squares = jnp.sum(gated * gated, axis=(0, 2))[:, None]
    scaled_flat = scaled.transpose(1, 0, 2).reshape(256, 1536)
    part = jnp.concatenate([dot(scaled_flat, w_out[j]) for j in range(4)], axis=1)
    part_own, part_other = halves(part, s)
    sq_own, sq_other = halves(squares, s)
    part = part_own + swap(part_other)
    q = lax.rsqrt((sq_own + swap(sq_other)) / 3072.0 + EPS)
    residual = tokens.astype(f32) + q * part

    r = rms(residual)
    ffn_in = (residual * r * g_ffn).astype(bf16)
    w_router = w_in[:, :, 832:848].transpose(1, 0, 2).reshape(1536, 64)
    logits = dot(ffn_in, w_router)
    logits = jnp.where(named > 0.5, logits, -1e30)
    top = jnp.max(logits, axis=1, keepdims=True)
    weights = jnp.where(named > 0.5, jnp.exp(logits - top), 0.0)
    gating = weights / jnp.sum(weights, axis=1, keepdims=True)
    gate_hi, gate_lo = hi_lo(gating)
    sent = to_slots(jnp.concatenate([ffn_in, gate_hi, gate_lo], axis=1))
    arrived = lax.all_to_all(sent, DP, 0, 0, tiled=True).reshape(n_slots, 1664)

    ffn_full = both_halves(ffn_in, swap(ffn_in), s)
    og_full = both_halves(out_grad, other_grad, s)
    sgu = jnp.stack([dot(ffn_full, w_sgu[j]) for j in range(4)])
    sg, su = sgu[..., :128], sgu[..., 128:]
    s_act = (jax.nn.silu(sg) * su).astype(bf16)
    s_flat = s_act.transpose(1, 0, 2).reshape(256, 512)
    s_out = jnp.concatenate([dot(s_flat, w_sdown[j]) for j in range(4)], axis=1)
    s_own, s_other = halves(s_out, s)
    s_out = s_own + swap(s_other.astype(bf16)).astype(f32)
    og_cols = og_full.reshape(256, 4, 384).transpose(1, 0, 2)
    d_s_act = sum(dot(og_cols[j], w_sdown[j], ((1,), (1,))) for j in range(4))
    d_s_act = d_s_act.reshape(256, 4, 128).transpose(1, 0, 2)
    d_sgu = jnp.concatenate([d_s_act * su * silu_grad(sg), d_s_act * jax.nn.silu(sg)], axis=-1)
    d_sgu = d_sgu.astype(bf16)
    grad_sdown = jnp.stack([dot(s_flat, og_cols[j], ((0,), (0,))) for j in range(4)]).astype(bf16)
    grad_sgu = jnp.stack([dot(ffn_full, d_sgu[j], ((0,), (0,))) for j in range(4)]).astype(bf16)
    d_ffn = sum(dot(d_sgu[j], w_sgu[j], ((1,), (1,))) for j in range(4))
    df_own, df_other = halves(d_ffn, s)
    d_ffn = df_own + swap(df_other.astype(bf16)).astype(f32)

    rows = arrived[:, :1536]
    lane = jnp.arange(128, dtype=jnp.int32) % 64
    slot_gate = jnp.sum(
        jnp.where(lane == dp, arrived[:, 1536:].astype(f32), 0.0), axis=1, keepdims=True
    )
    e_gu = dot(rows, w_eg)
    eg, eu = e_gu[:, :512], e_gu[:, 512:]
    e_act32 = jax.nn.silu(eg) * eu
    e_act = e_act32.astype(bf16)
    e_out = dot(e_act, w_ed).astype(bf16)
    d_act = dot(grad_rows, w_ed, ((1,), (1,)))
    d_gate = jnp.sum(e_act.astype(f32) * d_act, axis=1, keepdims=True)
    d_gu32 = jnp.concatenate([d_act * eu * silu_grad(eg), d_act * jax.nn.silu(eg)], axis=1)
    d_gu = d_gu32.astype(bf16)
    d_rows = dot(d_gu, w_eg, ((1,), (1,))).astype(bf16)
    dg_hi, dg_lo = hi_lo(d_gate)
    d_rows = jnp.concatenate([d_rows, dg_hi, dg_lo, jnp.zeros((n_slots, 126), bf16)], axis=1)
    d_back = lax.all_to_all(d_rows.reshape(experts, slots, 1664), DP, 0, 0, tiled=True)
    d_back = d_back.reshape(n_slots, 1664)
    out_back = lax.all_to_all(e_out.reshape(experts, slots, 1536), DP, 0, 0, tiled=True)
    out_back = out_back.reshape(n_slots, 1536)
    grad_ed = dot((e_act.astype(f32) * slot_gate).astype(bf16), grad_rows, ((0,), (0,)))
    grad_eg = dot(rows, (d_gu32 * slot_gate).astype(bf16), ((0,), (0,)))
    ge_own, ge_other = halves(grad_eg, s)
    grad_eg = ge_own + swap(ge_other.astype(bf16)).astype(f32)
    gd_own, gd_other = halves(grad_ed, s)
    grad_ed = gd_own + swap(gd_other.astype(bf16)).astype(f32)

    wide_gate = dot(gate_hi, spread) + dot(gate_lo, spread)
    weighted = (place.astype(f32) * wide_gate).astype(bf16)
    routed = dot(weighted, out_back)
    block_out = (residual + s_out + routed).astype(bf16)
    d_route = dot(weighted, d_back[:, :1536])
    dg = d_back[:, 1536:1538].T
    d_gating = dot(place * dg[0:1], spread, ((1,), (1,))) + dot(
        place * dg[1:2], spread, ((1,), (1,))
    )
    d_logits = gating * (d_gating - jnp.sum(gating * d_gating, axis=1, keepdims=True))
    d_logits_low = d_logits.astype(bf16)
    d_ffn = d_ffn + dot(d_logits_low, w_router, ((1,), (1,))) + d_route
    ffn_norm_grad = jnp.sum(d_ffn * residual * r, axis=0)
    u = d_ffn * g_ffn
    d_residual = (
        out_grad.astype(f32)
        + r * u
        - r * r * r * residual * jnp.mean(u * residual, axis=1, keepdims=True)
    )

    d_mixed = (q * d_residual).astype(bf16)
    kappa = q * q / 3072.0 * jnp.sum(d_mixed.astype(f32) * part, axis=1, keepdims=True)
    d_mixed_full = both_halves(d_mixed, swap(d_mixed), s)
    kappa = both_halves(kappa, swap(kappa), s)
    dm_cols = d_mixed_full.reshape(256, 4, 384).transpose(1, 0, 2)
    grad_out = jnp.stack([dot(scaled_flat, dm_cols[j], ((0,), (0,))) for j in range(4)])
    grad_out = grad_out.astype(bf16)
    d_scaled = sum(dot(dm_cols[j], w_out[j], ((1,), (1,))) for j in range(4))
    d_scaled = d_scaled.reshape(256, 4, 384).transpose(1, 0, 2)
    mixer_norm_grad = jnp.sum(d_scaled * gated, axis=1)
    d_gated = d_scaled * g_mix - kappa * gated
    d_y = d_gated * gate
    d_z = d_gated * y * silu_grad(z)
    dy_heads = d_y.reshape(4, 256, 6, 64).transpose(0, 2, 1, 3).reshape(24, 256, 64)
    dy_low = dy_heads.astype(bf16)
    d_skip = jnp.sum(x_heads * dy_heads, axis=(1, 2))
    dx_heads = jnp.einsum("hts,htp->hsp", mixing.astype(bf16), dy_low, preferred_element_type=f32)
    dx_heads = dx_heads + heads[2][:, None, None] * dy_heads
    pair = jnp.einsum("htp,hsp->hts", dy_low, x_low, preferred_element_type=f32)
    pair_fade = pair * fade
    d_scores = jnp.sum(pair_fade * step.T[:, None, :], axis=0).astype(bf16)
    q_pair = pair_fade * scores
    d_step = jnp.sum(q_pair, axis=1).T
    w_pair = q_pair * step.T[:, None, :]
    d_cum = (jnp.sum(w_pair, axis=2) - jnp.sum(w_pair, axis=1)).T
    d_rate = jnp.dot(tri.T, d_cum, precision=lax.Precision.HIGHEST, preferred_element_type=f32)
    d_c = dot(d_scores, b_mat.astype(bf16))
    d_b = dot(d_scores, c_mat.astype(bf16), ((0,), (0,)))
    d_raw = (d_step - d_rate * decay) * jax.nn.sigmoid(raw)
    head_grad = jnp.stack([jnp.sum(d_rate * rate, axis=0), jnp.sum(d_raw, axis=0), d_skip])
    dx = dx_heads.reshape(4, 6, 256, 64).transpose(0, 2, 1, 3).reshape(4, 256, 384)
    d_bc = jnp.stack([d_b[:, :64], d_b[:, 64:], d_c[:, :64], d_c[:, 64:]])
    d_x_raw, conv_x_grad = conv_back(dx * silu_grad(x_pre), x_raw, same, conv_x[:4])
    d_bc_raw, conv_bc_grad = conv_back(d_bc * silu_grad(bc_pre), bc_raw, same, conv_bc[:4])
    d_dt = d_raw.reshape(256, 4, 6).transpose(1, 0, 2)
    d_proj = jnp.concatenate(
        [d_z, d_x_raw, d_bc_raw, jnp.zeros((4, 256, 16), f32), d_dt, jnp.zeros((4, 256, 42), f32)],
        axis=2,
    ).astype(bf16)
    d_normed = sum(dot(d_proj[j], w_in[j], ((1,), (1,))) for j in range(4))
    dn_own, dn_other = halves(d_normed, s)
    d_normed = dn_own + swap(dn_other.astype(bf16)).astype(f32)
    x_own = tokens.astype(f32)
    p = rms(x_own)
    in_norm_grad = jnp.sum(d_normed * x_own * p, axis=0)
    v = d_normed * g_in
    token_grad = (
        d_residual + p * v - p * p * p * x_own * jnp.mean(v * x_own, axis=1, keepdims=True)
    ).astype(bf16)

    lhs = jnp.concatenate([normed, ffn_in], axis=0)
    d_route_cols = jnp.pad(
        d_logits_low.reshape(128, 4, 16).transpose(1, 0, 2), ((0, 0), (0, 0), (832, 48))
    )
    rhs = jnp.concatenate([d_proj, d_route_cols], axis=1)
    grad_in = jnp.stack([dot(lhs, rhs[j], ((0,), (0,))) for j in range(4)]).astype(bf16)
    small = jnp.concatenate(
        [
            in_norm_grad,
            ffn_norm_grad,
            lax.dynamic_update_slice(
                jnp.zeros((3072,), f32), mixer_norm_grad.reshape(1536), (s * 1536,)
            ),
            lax.dynamic_update_slice(
                jnp.zeros((5, 3328), f32), conv_x_grad.reshape(5, 1536), (0, s * 1536)
            )
            .at[:, 3072:]
            .add(conv_bc_grad.reshape(5, 256))
            .reshape(-1),
            lax.dynamic_update_slice(jnp.zeros((3, 48), f32), head_grad, (0, s * 24)).reshape(-1),
        ]
    )
    small = lax.psum(small, ALL)
    sum_in, sum_sgu, sum_out, sum_sdown = scatter(
        (
            grad_in.reshape(4, 2, 4, 4, 48, 896),
            grad_sgu.reshape(4, 2, 4, 4, 48, 256),
            grad_out.reshape(4, 4, 4, 2, 48, 384),
            grad_sdown.reshape(4, 4, 4, 2, 16, 384),
        ),
        SPECS,
        2,
    )
    back = jnp.concatenate([sum_in, sum_sgu], axis=2).reshape(8, 12, 1152)
    back = lax.all_to_all(back, ("seq", "y"), 0, 0, tiled=True).reshape(2, 4, 12, 1152)
    back = back.transpose(2, 0, 1, 3)
    bc_dt = back[..., 768:896]
    both_cores = bc_dt[:, 0] + bc_dt[:, 1]
    in_proj_grad = jnp.concatenate(
        [
            back[..., :384].reshape(12, 3072),
            back[..., 384:768].reshape(12, 3072),
            both_cores[..., :64].reshape(12, 256),
            bc_dt[..., 80:86].reshape(12, 48),
        ],
        axis=1,
    )
    router_grad = both_cores[..., 64:80].reshape(12, 64)
    sgu_grad = jnp.concatenate(
        [back[..., 896:1024].reshape(12, 1024), back[..., 1024:].reshape(12, 1024)], axis=1
    )
    rows_out = jnp.concatenate(
        [sum_out.reshape(4, 24, 384), sum_sdown.reshape(4, 8, 384)], axis=1
    )
    rows_out = lax.all_to_all(rows_out, "y", 0, 0, tiled=True).transpose(1, 0, 2).reshape(32, 1536)

    def mine(at, width):
        return lax.dynamic_slice_in_dim(small, at + device * width, width)

    conv_grad = lax.dynamic_slice_in_dim(small[6144:22784].reshape(5, 3328), device * 26, 26, 1)
    return (
        block_out,
        token_grad,
        mine(0, 12),
        in_proj_grad,
        conv_grad[:4].T,
        conv_grad[4],
        small[22784:].reshape(3, 48),
        mine(3072, 24),
        rows_out[:24],
        mine(1536, 12),
        router_grad,
        sgu_grad,
        rows_out[24:],
        grad_eg[None],
        grad_ed[None],
    )


def solution(mesh):
    finer = Mesh(mesh.devices.reshape(2, 4, 4, 4), ALL)
    placed = (
        P(DP_SEQ, None),
        P(DP_SEQ, None),
        P(DP, None),
        P(DP_SEQ, None),
        P(ALL),
        P(ALL, None),
        P(ALL, None),
        P(ALL),
        P(),
        P(ALL),
        P(ALL, None),
        P(ALL),
        P(ALL, None),
        P(ALL, None),
        P(ALL, None),
        P(DP, "seq", None),
        P(DP, "seq", None),
    )
    return jax.shard_map(
        local,
        mesh=finer,
        in_specs=placed,
        out_specs=(
            P(DP_SEQ, None),
            P(DP_SEQ, None),
            P(ALL),
            P(ALL, None),
            P(ALL, None),
            P(ALL),
            P(),
            P(ALL),
            P(ALL, None),
            P(ALL),
            P(ALL, None),
            P(ALL, None),
            P(ALL, None),
            P(DP, "seq", None),
            P(DP, "seq", None),
        ),
        check_vma=False,
    )
```

```python
import functools

import jax
import jax.numpy as jnp
import numpy as np
from jax import lax
from jax.experimental import pallas as pl
from jax.experimental.pallas import tpu as pltpu
from jax.sharding import Mesh
from jax.sharding import PartitionSpec as P

DP = ("z", "x", "y")
ALL = ("seq", "z", "x", "y")
DP_SEQ = ("z", "x", "y", "seq")
ORDER = (("z", "x", "y"), ("x", "y", "z"), ("y", "z", "x"))
REM = (("z", "x"), ("y", "x"), ("y", "z"))
MESH_ID = pl.DeviceIdType.MESH
EPS = 1e-05
f32 = jnp.float32
bf16 = jnp.bfloat16

ROWS_FIRST = (("y", "s", "z", "x"), "rows")
CHANNELS = (("y", "z", "x", "s"), "cols")
SPECS = (ROWS_FIRST, ROWS_FIRST, CHANNELS, CHANNELS)


def dot(a, b, dims=((1,), (0,))):
    return lax.dot_general(a, b, (dims, ((), ())), preferred_element_type=f32)


def neighbours():
    pos = {a: lax.axis_index(a) for a in DP}
    right = {a: lax.rem(pos[a] + 1, 4) for a in DP}
    left = {a: lax.rem(pos[a] + 3, 4) for a in DP}
    opp = {a: lax.rem(pos[a] + 2, 4) for a in DP}
    return pos, right, left, opp


def greet(right, left):
    barrier = pltpu.get_barrier_semaphore()
    for a in DP:
        for n in (right[a], left[a]):
            pl.semaphore_signal(barrier, inc=1, device_id={a: n}, device_id_type=MESH_ID)
    pl.semaphore_wait(barrier, 6)


def third(shape, split, a):
    rows, cols = shape[-2:]
    if split == "rows":
        return (pl.ds(rows // 3 * a, rows // 3), slice(None))
    return (slice(None), pl.ds(cols // 3 * a, cols // 3))


def third_shape(shape, split):
    rows, cols = shape[-2:]
    return (rows // 3, cols) if split == "rows" else (rows, cols // 3)


def region(ref, spec, free, fixed, a, s=None):
    order, split = spec
    ix = []
    for d in order:
        if d == "s":
            ix.append(slice(None) if s is None else s)
        else:
            ix.append(slice(None) if d in free else fixed[d])
    return ref.at[tuple(ix) + third(ref.shape, split, a)]


def gather_kernel(specs, *refs):
    n = len(specs)
    ins, outs, (send, recv, loc) = refs[:n], refs[n : 2 * n], refs[2 * n :]
    pos, right, left, opp = neighbours()
    own = []
    for i in range(n):
        ix = tuple(slice(None) if d == "s" else pos[d] for d in specs[i][0])
        c = pltpu.make_async_copy(ins[i], outs[i].at[ix], loc.at[i])
        c.start()
        own.append(c)
    greet(right, left)
    sends = []

    def remote(i, st, a, k, src, dst, ax, to):
        c = pltpu.make_async_remote_copy(
            src_ref=src,
            dst_ref=dst,
            send_sem=send.at[i, st, a, k],
            recv_sem=recv.at[i, st, a, k],
            device_id={ax: to},
            device_id_type=MESH_ID,
        )
        c.start()
        sends.append(c)
        return c

    for st in range(3):
        first, later = {}, []
        for i in range(n):
            for a in range(3):
                ax, free = ORDER[a][st], ORDER[a][:st]
                dst = region(outs[i], specs[i], free, pos, a)
                src = dst
                if st == 0:
                    src = ins[i].at[(slice(None),) + third(ins[i].shape, specs[i][1], a)]
                for d, to in enumerate((right[ax], left[ax])):
                    first[i, a, d] = remote(i, st, a, d, src, dst, ax, to)
        for i in range(n):
            for a in range(3):
                ax, free = ORDER[a][st], ORDER[a][:st]
                for d, (to, frm) in enumerate(((right[ax], left[ax]), (left[ax], right[ax]))):
                    first[i, a, d].wait_recv()
                    r = region(outs[i], specs[i], free, {**pos, ax: frm}, a, s=d)
                    later.append(remote(i, st, a, 2 + d, r, r, ax, to))
        for c in later:
            c.wait_recv()
        if st == 0:
            for c in own:
                c.wait()
    for c in sends:
        c.wait_send()


def gather(arrays, specs, collective_id):
    n = len(arrays)
    sizes = {"y": 4, "z": 4, "x": 4, "s": 2}
    outs = [
        jax.ShapeDtypeStruct(tuple(sizes[d] for d in spec[0]) + v.shape[1:], v.dtype)
        for v, spec in zip(arrays, specs)
    ]
    moved = sum(int(np.prod(o.shape)) for o in outs) * 2
    return pl.pallas_call(
        functools.partial(gather_kernel, specs),
        out_shape=outs,
        in_specs=[pl.BlockSpec(memory_space=pl.ANY)] * n,
        out_specs=[pl.BlockSpec(memory_space=pl.ANY)] * n,
        scratch_shapes=[
            pltpu.SemaphoreType.DMA((n, 3, 3, 4)),
            pltpu.SemaphoreType.DMA((n, 3, 3, 4)),
            pltpu.SemaphoreType.DMA((n,)),
        ],
        compiler_params=pltpu.CompilerParams(collective_id=collective_id, has_side_effects=True),
        cost_estimate=pl.CostEstimate(flops=0, bytes_accessed=2 * moved, transcendentals=0),
        name="gather_weights",
    )(*arrays)


def each(lead, fn):
    if not lead:
        fn((Ellipsis,))
        return

    @pl.loop(0, int(np.prod(lead)))
    def _(i):
        ix = []
        for d in reversed(lead):
            ix.append(lax.rem(i, d))
            i = lax.div(i, d)
        fn(tuple(reversed(ix)))


def scatter_kernel(specs, *refs):
    n = len(specs)
    gs, outs = refs[:n], refs[n : 2 * n]
    held, got = refs[2 * n : 3 * n], [refs[3 * n + 3 * i : 3 * n + 3 * i + 3] for i in range(n)]
    send, recv, loc = refs[6 * n :]
    pos, right, left, opp = neighbours()

    def source(i, st, a, idx, s):
        ax = ORDER[a][2 - st]
        if st == 0:
            return region(gs[i], specs[i], [d for d in DP if d != ax], {ax: idx}, a, s)
        part = held[i].at[a, 2 + s]
        if st == 1:
            return part.at[:, idx] if REM[a][1] == ax else part.at[idx]
        me = pos[ORDER[a][1]]
        return part.at[me, idx] if REM[a][1] == ax else part.at[idx, me]

    local = {}
    for i in range(n):
        for a in range(3):
            ax = ORDER[a][2]
            for k, (idx, s) in enumerate(((right[ax], 0), (left[ax], 1), (pos[ax], 0), (pos[ax], 1))):
                c = pltpu.make_async_copy(source(i, 0, a, idx, s), held[i].at[a, k], loc.at[i, a, k])
                c.start()
                local[i, a, k] = c
    greet(right, left)
    sends = []

    def remote(i, st, a, k, src, ax, to):
        c = pltpu.make_async_remote_copy(
            src_ref=src,
            dst_ref=got[i][st].at[a, k],
            send_sem=send.at[i, st, a, k],
            recv_sem=recv.at[i, st, a, k],
            device_id={ax: to},
            device_id_type=MESH_ID,
        )
        c.start()
        sends.append(c)
        return c

    every = [(i, a) for i in range(n) for a in range(3)]
    for st in range(3):
        lead = ((4, 4), (4,), ())[st]
        cp = {}
        for i, a in every:
            ax = ORDER[a][2 - st]
            cp[i, a, 0] = remote(i, st, a, 0, source(i, st, a, opp[ax], 0), ax, right[ax])
            cp[i, a, 1] = remote(i, st, a, 1, source(i, st, a, opp[ax], 1), ax, left[ax])
        for i, a in every:
            ax = ORDER[a][2 - st]
            cp[i, a, 2] = remote(i, st, a, 2, source(i, st, a, right[ax], 1), ax, right[ax])
            cp[i, a, 3] = remote(i, st, a, 3, source(i, st, a, left[ax], 0), ax, left[ax])
        for i, a in every:
            ax = ORDER[a][2 - st]
            for d, to in enumerate((right[ax], left[ax])):
                cp[i, a, d].wait_recv()
                if st == 0:
                    local[i, a, d].wait()
                    acc = held[i].at[a, d]
                else:
                    acc = source(i, st, a, to, d)
                more = got[i][st].at[a, d]

                def add(ix, acc=acc, more=more):
                    acc[ix] = (acc[ix].astype(f32) + more[ix].astype(f32)).astype(acc.dtype)

                each(lead, add)
                cp[i, a, 4 + d] = remote(i, st, a, 4 + d, acc, ax, to)
        for i, a in every:
            ax = ORDER[a][2 - st]
            if st == 0:
                local[i, a, 2].wait()
                local[i, a, 3].wait()
            for s, (p, q) in enumerate(((4, 3), (2, 5))):
                cp[i, a, p].wait_recv()
                cp[i, a, q].wait_recv()
                acc = held[i].at[a, 2 + s] if st == 0 else source(i, st, a, pos[ax], s)
                one, two = got[i][st].at[a, p], got[i][st].at[a, q]
                if st == 2:
                    ix = (s,) + third(outs[i].shape, specs[i][1], a)
                    outs[i][ix] = acc[...].astype(f32) + one[...].astype(f32) + two[...].astype(f32)
                else:

                    def finish(ix, acc=acc, one=one, two=two):
                        total = acc[ix].astype(f32) + one[ix].astype(f32) + two[ix].astype(f32)
                        acc[ix] = total.astype(acc.dtype)

                    each(lead, finish)
    for c in sends:
        c.wait_send()


def scatter(arrays, specs, collective_id):
    n = len(arrays)
    outs = [jax.ShapeDtypeStruct((2,) + v.shape[4:], f32) for v in arrays]
    pieces = [third_shape(v.shape, spec[1]) for v, spec in zip(arrays, specs)]
    moved = sum(int(np.prod(v.shape)) for v in arrays) * 2
    return pl.pallas_call(
        functools.partial(scatter_kernel, specs),
        out_shape=outs,
        in_specs=[pl.BlockSpec(memory_space=pl.ANY)] * n,
        out_specs=[pl.BlockSpec(memory_space=pltpu.VMEM)] * n,
        scratch_shapes=[pltpu.VMEM((3, 4, 4, 4) + p, bf16) for p in pieces]
        + [pltpu.VMEM((3, 6) + lead + p, bf16) for p in pieces for lead in ((4, 4), (4,), ())]
        + [
            pltpu.SemaphoreType.DMA((n, 3, 3, 6)),
            pltpu.SemaphoreType.DMA((n, 3, 3, 6)),
            pltpu.SemaphoreType.DMA((n, 3, 4)),
        ],
        compiler_params=pltpu.CompilerParams(
            collective_id=collective_id, has_side_effects=True, vmem_limit_bytes=56 * 2**20
        ),
        cost_estimate=pl.CostEstimate(flops=0, bytes_accessed=2 * moved, transcendentals=0),
        name="scatter_grads",
    )(*arrays)


def expert_kernel(rows_ref, grad_ref, gu_ref, down_ref, pick_ref, back_ref, act_ref, wact_ref, wgu_ref):
    e_gu = dot(rows_ref[:, :1536], gu_ref[...])
    eg, eu = e_gu[:, :512], e_gu[:, 512:]
    sig = jax.nn.sigmoid(eg)
    silu = eg * sig
    act32 = silu * eu
    act = act32.astype(bf16)
    slot_gate = jnp.sum(rows_ref[:, 1536:].astype(f32) * pick_ref[...], axis=1, keepdims=True)
    d_act = dot(grad_ref[...], down_ref[...], ((1,), (1,)))
    d_gate = jnp.sum(act.astype(f32) * d_act, axis=1, keepdims=True)
    d_eg = d_act * eu * (sig + silu * (1.0 - sig))
    d_eu = d_act * silu
    d_gu = jnp.concatenate([d_eg.astype(bf16), d_eu.astype(bf16)], axis=1)
    back_ref[:, :1536] = dot(d_gu, gu_ref[...], ((1,), (1,))).astype(bf16)
    hi = d_gate.astype(bf16).astype(f32)
    lane = lax.broadcasted_iota(jnp.int32, (rows_ref.shape[0], 128), 1)
    tail = jnp.where(lane == 0, hi, jnp.where(lane == 1, d_gate - hi, 0.0))
    back_ref[:, 1536:] = tail.astype(bf16)
    act_ref[...] = act
    wact_ref[...] = (act32 * slot_gate).astype(bf16)
    wgu_ref[:, :512] = (d_eg * slot_gate).astype(bf16)
    wgu_ref[:, 512:] = (d_eu * slot_gate).astype(bf16)


def expert_grads(rows, grad_rows, gate_up, down, pick):
    n, block = rows.shape[0], 256
    widths = (1664, 512, 512, 1024)

    def blocked(w):
        return pl.BlockSpec((block, w), lambda i: (i, 0))

    def whole(v):
        return pl.BlockSpec(v.shape, lambda i: (0, 0))

    return pl.pallas_call(
        expert_kernel,
        grid=(n // block,),
        out_shape=[jax.ShapeDtypeStruct((n, w), bf16) for w in widths],
        in_specs=[blocked(1664), blocked(1536), whole(gate_up), whole(down), whole(pick)],
        out_specs=[blocked(w) for w in widths],
        compiler_params=pltpu.CompilerParams(vmem_limit_bytes=48 * 2**20),
        cost_estimate=pl.CostEstimate(
            flops=2 * n * 1536 * (1024 + 512 + 1024), bytes_accessed=26 * 2**20, transcendentals=0
        ),
        name="expert_grads",
    )(rows, grad_rows, gate_up, down, pick)


HEAD_AT = 80


def split3(v):
    hi = v.astype(bf16)
    rest = v - hi.astype(f32)
    mid = rest.astype(bf16)
    return hi, mid, (rest - mid.astype(f32)).astype(bf16)


def roll(v, by, axis):
    return pltpu.roll(v, by, axis) if by else v


def taps_pre(v, marks, w):
    total = w[4:5] + w[3:4] * v
    for d in (1, 2, 3):
        total = total + w[3 - d : 4 - d] * (roll(v, d, 0) * marks[:, d : d + 1])
    return total


def taps_back(d_pre, v, marks, w):
    d_v = w[3:4] * d_pre
    d_w = [jnp.sum(d_pre * v, axis=0, keepdims=True)]
    for d in (1, 2, 3):
        masked = d_pre * marks[:, d : d + 1]
        d_w.insert(0, jnp.sum(masked * roll(v, d, 0), axis=0, keepdims=True))
        d_v = d_v + w[3 - d : 4 - d] * roll(masked, 256 - d, 0)
    zero = jnp.zeros((3, v.shape[1]), f32)
    return d_v, jnp.concatenate(d_w + [jnp.sum(d_pre, axis=0, keepdims=True), zero], axis=0)


def lanes(shape):
    return lax.broadcasted_iota(jnp.int32, shape, len(shape) - 1)


def joined(first, second):
    return jnp.where(lanes(first.shape) < 64, first, roll(second, 64, 1))


def bc_raw(proj_ref, k):
    return joined(
        proj_ref[2 * k, :, 768:896].astype(f32), proj_ref[2 * k + 1, :, 768:896].astype(f32)
    )


def head_steps(proj_ref, hp_ref, j, tri):
    raw = proj_ref[j, :, 768:896].astype(f32) + hp_ref[j, 1:2]
    step = jnp.maximum(raw, 0.0) + jnp.log1p(jnp.exp(-jnp.abs(raw)))
    rate = -step * hp_ref[j, 0:1]
    cum = sum(dot(tri, part) for part in split3(rate))
    return raw, step, rate, cum


def triangle():
    t = lax.broadcasted_iota(jnp.int32, (256, 256), 0)
    return t >= lanes((256, 256))


def pair_of(cols, p):
    at = HEAD_AT + 2 * p
    first = jnp.broadcast_to(cols[:, at : at + 1], (256, 128))
    return jnp.where(lanes((256, 128)) < 64, first, cols[:, at + 1 : at + 2])


def fade_of(cum, cum_rows, h, inside):
    at = HEAD_AT + h
    return jnp.exp(jnp.where(inside, cum[:, at : at + 1] - cum_rows[at : at + 1], -1e30))


def forward_kernel(
    x_ref, g_ref, w_in_ref, w_out_ref, cx_ref, cbc_ref, hp_ref, marks_ref, seg_ref,
    normed_ref, proj_ref, y_ref, scaled_ref, part_ref, squares_ref, scores_ref,
):
    i = pl.program_id(0)

    @pl.when(i == 0)
    def _():
        x = x_ref[...].astype(f32)
        normed_ref[...] = (x * rms(x) * g_ref[0:1]).astype(bf16)

    @pl.when(i < 4)
    def _():
        proj_ref[i] = dot(normed_ref[...], w_in_ref[0]).astype(bf16)

    @pl.when(i == 4)
    def _():
        marks = marks_ref[...]
        b_mat, c_mat = [jax.nn.silu(taps_pre(bc_raw(proj_ref, k), marks, cbc_ref[k])) for k in (0, 1)]
        scores_ref[...] = dot(c_mat.astype(bf16), b_mat.astype(bf16), ((1,), (1,)))
        part_ref[...] = jnp.zeros_like(part_ref)
        squares_ref[...] = jnp.zeros_like(squares_ref)

    @pl.when(i >= 4)
    def _():
        j = i - 4
        marks, cx = marks_ref[...], cx_ref[j]
        causal = triangle()
        inside = causal & (marks[:, 4:5] == seg_ref[0:1])
        _, step, _, cum = head_steps(proj_ref, hp_ref, j, causal.astype(bf16))
        cum_rows = cum.T
        x = jax.nn.silu(taps_pre(proj_ref[j, :, 384:768].astype(f32), marks, cx))
        scores = scores_ref[...]
        ys = []
        for p in range(3):
            xp = x[:, 128 * p : 128 * p + 128]
            xs = (xp * pair_of(step, p)).astype(bf16)
            y0, y1 = [
                dot((fade_of(cum, cum_rows, 2 * p + k, inside) * scores).astype(bf16), xs)
                for k in (0, 1)
            ]
            ys.append(jnp.where(lanes((256, 128)) < 64, y0, y1))
        y = jnp.concatenate(ys, axis=1) + cx[5:6] * x
        z = proj_ref[j, :, :384].astype(f32)
        gated = y * jax.nn.silu(z)
        scaled = (gated * cx[6:7]).astype(bf16)
        y_ref[j] = y
        scaled_ref[j] = scaled
        squares_ref[...] += jnp.broadcast_to(
            jnp.sum(gated * gated, axis=1, keepdims=True), squares_ref.shape
        )
        for c in range(4):
            part_ref[:, c * 384 : c * 384 + 384] += dot(scaled, w_out_ref[c])


def fixed(v):
    return pl.BlockSpec(v.shape, lambda i: (0,) * len(v.shape))


def mixer_forward(x, g, w_in, w_out, cx, cbc, hp, marks, seg):
    outs = [
        jax.ShapeDtypeStruct((256, 1536), bf16),
        jax.ShapeDtypeStruct((4, 256, 896), bf16),
        jax.ShapeDtypeStruct((4, 256, 384), f32),
        jax.ShapeDtypeStruct((4, 256, 384), bf16),
        jax.ShapeDtypeStruct((256, 1536), f32),
        jax.ShapeDtypeStruct((256, 128), f32),
    ]
    return pl.pallas_call(
        forward_kernel,
        grid=(8,),
        out_shape=outs,
        in_specs=[
            fixed(x),
            fixed(g),
            pl.BlockSpec((1, 1536, 896), lambda i: (jnp.minimum(i, 3), 0, 0)),
            pl.BlockSpec((4, 384, 384), lambda i: (0, jnp.maximum(i - 4, 0), 0)),
            *[fixed(v) for v in (cx, cbc, hp, marks, seg)],
        ],
        out_specs=[fixed(o) for o in outs],
        scratch_shapes=[pltpu.VMEM((256, 256), f32)],
        compiler_params=pltpu.CompilerParams(vmem_limit_bytes=48 * 2**20),
        cost_estimate=pl.CostEstimate(
            flops=2 * 256 * 1536 * (3584 + 1536), bytes_accessed=22 * 2**20, transcendentals=2**21
        ),
        name="mixer_forward",
    )(x, g, w_in, w_out, cx, cbc, hp, marks, seg)


def backward_kernel(
    dm_ref, kappa_ref, w_out_ref, w_in_ref, normed_ref, ffn_ref, drout_ref, proj_ref, y_ref,
    scaled_ref, cx_ref, cbc_ref, hp_ref, marks_ref, seg_ref,
    gout_ref, gin_ref, dn_ref, gcx_ref, gcbc_ref, gheads_ref,
    dproj_ref, scores_ref, dscores_ref, bc_ref,
):
    i = pl.program_id(0)

    @pl.when(i == 0)
    def _():
        marks = marks_ref[...]
        for k in (0, 1):
            bc_ref[k] = jax.nn.silu(taps_pre(bc_raw(proj_ref, k), marks, cbc_ref[k])).astype(bf16)
        scores_ref[...] = dot(bc_ref[1], bc_ref[0], ((1,), (1,)))
        dscores_ref[...] = jnp.zeros_like(dscores_ref)

    @pl.when(i < 4)
    def _():
        j = i
        marks, cx = marks_ref[...], cx_ref[j]
        scaled = scaled_ref[j]
        d_scaled = jnp.zeros((256, 384), f32)
        for c in range(4):
            dm = dm_ref[:, c * 384 : c * 384 + 384]
            d_scaled = d_scaled + dot(dm, w_out_ref[c], ((1,), (1,)))
            gout_ref[c] = dot(scaled, dm, ((0,), (0,))).astype(bf16)
        y = y_ref[j]
        z = proj_ref[j, :, :384].astype(f32)
        sig = jax.nn.sigmoid(z)
        gate = z * sig
        gated = y * gate
        d_gated = d_scaled * cx[6:7] - kappa_ref[:, 0:1] * gated
        dy = d_gated * gate
        dproj_ref[j, :, :384] = (d_gated * y * (sig + gate * (1.0 - sig))).astype(bf16)
        norm_grad = jnp.sum(d_scaled * gated, axis=0, keepdims=True)

        causal = triangle()
        inside = causal & (marks[:, 4:5] == seg_ref[0:1])
        raw, step, rate, cum = head_steps(proj_ref, hp_ref, j, causal.astype(bf16))
        cum_rows = cum.T
        x_raw = proj_ref[j, :, 384:768].astype(f32)
        x_pre = taps_pre(x_raw, marks, cx)
        x_sig = jax.nn.sigmoid(x_pre)
        x = x_pre * x_sig
        scores = scores_ref[...]
        d_scores = dscores_ref[...]
        lane = lanes((256, 128))
        low_half = lane < 64
        row = lax.broadcasted_iota(jnp.int32, (128, 256), 0)
        d_cum = jnp.zeros((256, 128), f32)
        d_cum_rows = jnp.zeros((128, 256), f32)
        d_step = jnp.zeros((256, 128), f32)
        dxs = []
        for p in range(3):
            xp = x[:, 128 * p : 128 * p + 128]
            dyp = dy[:, 128 * p : 128 * p + 128]
            steps = pair_of(step, p)
            xs = (xp * steps).astype(bf16)
            dy_low = dyp.astype(bf16)
            back = []
            for k in (0, 1):
                at = HEAD_AT + 2 * p + k
                fade = fade_of(cum, cum_rows, 2 * p + k, inside)
                mine = jnp.where(low_half if k == 0 else ~low_half, dyp, 0.0).astype(bf16)
                pair = dot(mine, xs, ((1,), (1,)))
                mixing = fade * scores
                w = mixing * pair
                d_scores = d_scores + fade * pair
                d_cum = jnp.where(lane == at, jnp.sum(w, axis=1, keepdims=True), d_cum)
                d_cum_rows = jnp.where(row == at, jnp.sum(w, axis=0, keepdims=True), d_cum_rows)
                back.append(dot(mixing.astype(bf16), dy_low, ((0,), (0,))))
            d_xs = jnp.where(low_half, back[0], back[1])
            prod = xp * d_xs
            first = jnp.sum(jnp.where(low_half, prod, 0.0), axis=1, keepdims=True)
            second = jnp.sum(jnp.where(low_half, 0.0, prod), axis=1, keepdims=True)
            at = HEAD_AT + 2 * p
            d_step = jnp.where(lane == at, first, jnp.where(lane == at + 1, second, d_step))
            dxs.append(d_xs * steps)
        dscores_ref[...] = d_scores
        dx = jnp.concatenate(dxs, axis=1) + cx[5:6] * dy
        skip_grad = jnp.sum(x * dy, axis=0, keepdims=True)
        d_x_pre = dx * (x_sig + x * (1.0 - x_sig))
        d_x_raw, conv_grad = taps_back(d_x_pre, x_raw, marks, cx)
        dproj_ref[j, :, 384:768] = d_x_raw.astype(bf16)
        rowid = lax.broadcasted_iota(jnp.int32, (8, 384), 0)
        gcx_ref[j] = jnp.where(rowid == 5, skip_grad, jnp.where(rowid == 6, norm_grad, conv_grad))
        d_cum = d_cum - d_cum_rows.T
        d_rate = sum(dot(causal.astype(bf16), part, ((0,), (0,))) for part in split3(d_cum))
        d_raw = (d_step - d_rate * hp_ref[j, 0:1]) * jax.nn.sigmoid(raw)
        dproj_ref[j, :, 768:896] = d_raw.astype(bf16)
        rowid = lax.broadcasted_iota(jnp.int32, (8, 128), 0)
        gheads_ref[j] = jnp.where(
            rowid == 0,
            jnp.sum(d_rate * rate, axis=0, keepdims=True),
            jnp.where(rowid == 1, jnp.sum(d_raw, axis=0, keepdims=True), 0.0),
        )

    @pl.when(i == 4)
    def _():
        marks = marks_ref[...]
        d_scores = dscores_ref[...].astype(bf16)
        d_bc = (dot(d_scores, bc_ref[1], ((0,), (0,))), dot(d_scores, bc_ref[0]))
        low_half = lanes((256, 128)) < 64
        for k in (0, 1):
            raw = bc_raw(proj_ref, k)
            pre = taps_pre(raw, marks, cbc_ref[k])
            sig = jax.nn.sigmoid(pre)
            d_pre = d_bc[k] * (sig + pre * sig * (1.0 - sig))
            d_raw, conv_grad = taps_back(d_pre, raw, marks, cbc_ref[k])
            gcbc_ref[k] = conv_grad
            for h, moved in enumerate((d_raw, roll(d_raw, 64, 1))):
                steps = dproj_ref[2 * k + h, :, 768:896].astype(f32)
                dproj_ref[2 * k + h, :, 768:896] = jnp.where(low_half, moved, steps).astype(bf16)
        dn_ref[...] = jnp.zeros_like(dn_ref)

    @pl.when(i >= 4)
    def _():
        j = i - 4
        d_proj = dproj_ref[j]
        dn_ref[...] += dot(d_proj, w_in_ref[0], ((1,), (1,)))
        gin_ref[0, :, :768] = dot(normed_ref[...], d_proj[:, :768], ((0,), (0,))).astype(bf16)
        last = dot(normed_ref[...], d_proj[:, 768:], ((0,), (0,)))
        last = last + dot(ffn_ref[...], drout_ref[j], ((0,), (0,)))
        gin_ref[0, :, 768:] = last.astype(bf16)


def mixer_backward(dm, kappa, w_out, w_in, normed, ffn_in, drout, proj, y, scaled, cx, cbc, hp, marks, seg):
    def late(i):
        return jnp.maximum(i - 4, 0)

    def early(i):
        return jnp.minimum(i, 3)

    small = [
        jax.ShapeDtypeStruct((256, 1536), f32),
        jax.ShapeDtypeStruct((4, 8, 384), f32),
        jax.ShapeDtypeStruct((2, 8, 128), f32),
        jax.ShapeDtypeStruct((4, 8, 128), f32),
    ]
    w_out_spec = pl.BlockSpec((4, 384, 384), lambda i: (0, early(i), 0))
    w_in_spec = pl.BlockSpec((1, 1536, 896), lambda i: (late(i), 0, 0))
    return pl.pallas_call(
        backward_kernel,
        grid=(8,),
        out_shape=[
            jax.ShapeDtypeStruct((4, 1536, 384), bf16),
            jax.ShapeDtypeStruct((4, 1536, 896), bf16),
            *small,
        ],
        in_specs=[
            fixed(dm),
            fixed(kappa),
            w_out_spec,
            w_in_spec,
            *[fixed(v) for v in (normed, ffn_in, drout, proj, y, scaled, cx, cbc, hp, marks, seg)],
        ],
        out_specs=[w_out_spec, w_in_spec, *[fixed(o) for o in small]],
        scratch_shapes=[
            pltpu.VMEM((4, 256, 896), bf16),
            pltpu.VMEM((256, 256), f32),
            pltpu.VMEM((256, 256), f32),
            pltpu.VMEM((2, 256, 128), bf16),
        ],
        compiler_params=pltpu.CompilerParams(vmem_limit_bytes=56 * 2**20),
        cost_estimate=pl.CostEstimate(
            flops=4 * 256 * 1536 * (3584 + 1536), bytes_accessed=40 * 2**20, transcendentals=2**21
        ),
        name="mixer_backward",
    )(dm, kappa, w_out, w_in, normed, ffn_in, drout, proj, y, scaled, cx, cbc, hp, marks, seg)


def swap(v):
    return lax.ppermute(v, "seq", [(0, 1), (1, 0)])


def both_halves(own, other, s):
    first = jnp.where(s == 0, own, other)
    second = jnp.where(s == 0, other, own)
    return jnp.concatenate([first, second], axis=0)


def halves(v, s):
    rows = v.shape[0] // 2
    return (
        lax.dynamic_slice_in_dim(v, s * rows, rows, 0),
        lax.dynamic_slice_in_dim(v, (1 - s) * rows, rows, 0),
    )


def hi_lo(v):
    hi = v.astype(bf16)
    return hi, (v - hi.astype(f32)).astype(bf16)


def rms(v):
    return lax.rsqrt(jnp.mean(v * v, axis=-1, keepdims=True) + EPS)


def silu_grad(v):
    sig = jax.nn.sigmoid(v)
    return sig * (1.0 + v * (1.0 - sig))


def local(
    tokens,
    out_grad,
    lengths,
    routes,
    in_norm,
    in_proj,
    conv_weight,
    conv_bias,
    head_params,
    mixer_norm,
    out_proj,
    ffn_norm,
    router,
    shared_gate_up,
    shared_down,
    expert_gate_up,
    expert_down,
):
    s = lax.axis_index("seq")
    dp = lax.axis_index(DP)
    device = s * 64 + dp
    experts, slots = 64, 24
    n_slots = experts * slots

    pieces = []
    for c in range(2):
        for j in range(4):
            at = c * 1536 + j * 384
            misc = jnp.concatenate(
                [
                    in_proj[:, 6144 + j * 64 : 6208 + j * 64],
                    router[:, j * 16 : j * 16 + 16],
                    in_proj[:, 6400 + c * 24 + j * 6 : 6406 + c * 24 + j * 6],
                    jnp.zeros((12, 42), bf16),
                ],
                axis=1,
            )
            up = 1024 + c * 512 + j * 128
            pieces.append(
                jnp.concatenate(
                    [
                        in_proj[:, at : at + 384],
                        in_proj[:, 3072 + at : 3456 + at],
                        misc,
                        shared_gate_up[:, up - 1024 : up - 896],
                        shared_gate_up[:, up : up + 128],
                    ],
                    axis=1,
                )
            )
    rows_in = lax.all_to_all(jnp.stack(pieces), ("seq", "y"), 0, 0, tiled=True).reshape(2, 48, 1152)
    out_rows = jnp.concatenate(
        [out_proj.reshape(24, 4, 384), shared_down.reshape(8, 4, 384)], axis=0
    ).transpose(1, 0, 2)
    out_rows = lax.all_to_all(out_rows, "y", 0, 0, tiled=True)
    vec = jnp.concatenate(
        [
            in_norm,
            ffn_norm,
            mixer_norm,
            conv_weight.T.reshape(-1),
            conv_bias,
            jnp.zeros((78,), bf16),
        ]
    )
    vecs = lax.all_to_all(jnp.broadcast_to(vec, (128, 256)), ALL, 0, 0, tiled=True)
    other_tokens = swap(tokens)
    other_grad = swap(out_grad)
    other_gate_up = swap(expert_gate_up[0])
    other_down = swap(expert_down[0])

    w_in, w_sgu, w_out, w_sdown = gather(
        (
            rows_in[:, :, :896],
            rows_in[:, :, 896:],
            out_rows[:, :24].reshape(2, 48, 384),
            out_rows[:, 24:].reshape(2, 16, 384),
        ),
        SPECS,
        1,
    )
    w_in = w_in.reshape(4, 1536, 896)
    w_sgu = w_sgu.reshape(4, 1536, 256)
    w_out = w_out.reshape(4, 1536, 384)
    w_sdown = w_sdown.reshape(4, 512, 384)

    vecs = vecs.astype(f32)
    g_in = vecs[:, :12].reshape(1, 1536)
    g_ffn = vecs[:, 12:24].reshape(1536)
    g_mix = lax.dynamic_slice_in_dim(vecs[:, 24:48].reshape(1, 3072), s * 1536, 1536, 1)
    conv = vecs[:, 48:178].reshape(128, 5, 26).transpose(1, 0, 2).reshape(5, 3328)
    heads = lax.dynamic_slice_in_dim(head_params.astype(f32), s * 24, 24, 1)
    cx = jnp.concatenate(
        [
            lax.dynamic_slice_in_dim(conv[:, :3072], s * 1536, 1536, 1),
            jnp.broadcast_to(heads[2][:, None], (24, 64)).reshape(1, 1536),
            g_mix,
            jnp.zeros((1, 1536), f32),
        ],
        axis=0,
    )
    cx = cx.reshape(8, 4, 384).transpose(1, 0, 2)
    cbc = jnp.pad(conv[:, 3072:], ((0, 3), (0, 0))).reshape(8, 2, 128).transpose(1, 0, 2)
    hp = jnp.stack([jnp.exp(heads[0]), heads[1]]).reshape(2, 4, 6).transpose(1, 0, 2)
    hp = jnp.pad(hp, ((0, 0), (0, 6), (HEAD_AT, 122 - HEAD_AT)))
    w_eg = both_halves(expert_gate_up[0], other_gate_up, s)
    w_ed = both_halves(expert_down[0], other_down, s)

    ids = jnp.arange(experts, dtype=jnp.int32)
    named = jnp.sum((routes[:, :, None] == ids).astype(f32), axis=1)
    t128 = jnp.arange(128)
    before = (t128[:, None] > t128[None, :]).astype(bf16)
    rank = dot(before, named.astype(bf16))
    slot = jnp.arange(n_slots, dtype=jnp.int32)
    spread = (slot[None, :] // slots == ids[:, None]).astype(bf16)
    is_named = dot(named.astype(bf16), spread) > 0.5
    in_slot = dot(rank.astype(bf16), spread) == (slot % slots).astype(f32)[None, :]
    place = (is_named & in_slot).astype(bf16)

    def to_slots(v):
        return dot(place, v, ((0,), (0,))).astype(bf16).reshape(experts, slots, v.shape[1])

    grad_slots, w_in = lax.optimization_barrier((to_slots(out_grad), w_in))
    grad_rows = lax.all_to_all(grad_slots, DP, 0, 0, tiled=True).reshape(n_slots, 1536)

    ends = jnp.cumsum(lengths[0])
    t256 = jnp.arange(256, dtype=jnp.int32)
    segment = jnp.sum((t256[:, None] >= ends[None, :]).astype(jnp.int32), axis=1)
    seg = segment.astype(f32)
    same = [
        (jnp.pad(segment, (d, 0), constant_values=-1)[:256] == segment).astype(f32)
        for d in range(4)
    ]
    marks = jnp.pad(jnp.stack(same + [seg], axis=1), ((0, 0), (0, 123)))
    seg = jnp.broadcast_to(seg, (8, 256))
    x_full = both_halves(tokens, other_tokens, s)
    normed, proj, y, scaled, part, squares = mixer_forward(
        x_full, jnp.broadcast_to(g_in, (8, 1536)), w_in, w_out, cx, cbc, hp, marks, seg
    )
    squares = squares[:, :1]
    part_own, part_other = halves(part, s)
    sq_own, sq_other = halves(squares, s)
    part = part_own + swap(part_other)
    q = lax.rsqrt((sq_own + swap(sq_other)) / 3072.0 + EPS)
    residual = tokens.astype(f32) + q * part

    r = rms(residual)
    ffn_in = (residual * r * g_ffn).astype(bf16)
    w_router = w_in[:, :, 832:848].transpose(1, 0, 2).reshape(1536, 64)
    logits = dot(ffn_in, w_router)
    logits = jnp.where(named > 0.5, logits, -1e30)
    top = jnp.max(logits, axis=1, keepdims=True)
    weights = jnp.where(named > 0.5, jnp.exp(logits - top), 0.0)
    gating = weights / jnp.sum(weights, axis=1, keepdims=True)
    gate_hi, gate_lo = hi_lo(gating)
    sent = to_slots(jnp.concatenate([ffn_in, gate_hi, gate_lo], axis=1))
    sent, grad_rows = lax.optimization_barrier((sent, grad_rows))
    arrived = lax.all_to_all(sent, DP, 0, 0, tiled=True).reshape(n_slots, 1664)

    ffn_full = both_halves(ffn_in, swap(ffn_in), s)
    og_full = both_halves(out_grad, other_grad, s)
    sgu = jnp.stack([dot(ffn_full, w_sgu[j]) for j in range(4)])
    sg, su = sgu[..., :128], sgu[..., 128:]
    s_act = (jax.nn.silu(sg) * su).astype(bf16)
    s_flat = s_act.transpose(1, 0, 2).reshape(256, 512)
    s_out = jnp.concatenate([dot(s_flat, w_sdown[j]) for j in range(4)], axis=1)
    s_own, s_other = halves(s_out, s)
    s_out = s_own + swap(s_other.astype(bf16)).astype(f32)
    og_cols = og_full.reshape(256, 4, 384).transpose(1, 0, 2)
    d_s_act = sum(dot(og_cols[j], w_sdown[j], ((1,), (1,))) for j in range(4))
    d_s_act = d_s_act.reshape(256, 4, 128).transpose(1, 0, 2)
    d_sgu = jnp.concatenate([d_s_act * su * silu_grad(sg), d_s_act * jax.nn.silu(sg)], axis=-1)
    d_sgu = d_sgu.astype(bf16)
    grad_sdown = jnp.stack([dot(s_flat, og_cols[j], ((0,), (0,))) for j in range(4)]).astype(bf16)
    grad_sgu = jnp.stack([dot(ffn_full, d_sgu[j], ((0,), (0,))) for j in range(4)]).astype(bf16)
    d_ffn = sum(dot(d_sgu[j], w_sgu[j], ((1,), (1,))) for j in range(4))
    df_own, df_other = halves(d_ffn, s)
    d_ffn = df_own + swap(df_other.astype(bf16)).astype(f32)

    lane = jnp.arange(128, dtype=jnp.int32) % 64
    pick = (lane == dp).astype(f32)[None, :]
    d_rows, e_act, w_act, w_gu = expert_grads(arrived, grad_rows, w_eg, w_ed, pick)
    d_back = lax.all_to_all(d_rows.reshape(experts, slots, 1664), DP, 0, 0, tiled=True)
    d_back = d_back.reshape(n_slots, 1664)
    e_out = dot(e_act, w_ed).astype(bf16)
    e_out, d_back = lax.optimization_barrier((e_out, d_back))
    out_back = lax.all_to_all(e_out.reshape(experts, slots, 1536), DP, 0, 0, tiled=True)
    out_back = out_back.reshape(n_slots, 1536)
    grad_ed = dot(w_act, grad_rows, ((0,), (0,)))
    grad_eg = dot(arrived[:, :1536], w_gu, ((0,), (0,)))
    ge_own, ge_other = halves(grad_eg, s)
    grad_eg = ge_own + swap(ge_other.astype(bf16)).astype(f32)
    gd_own, gd_other = halves(grad_ed, s)
    grad_ed = gd_own + swap(gd_other.astype(bf16)).astype(f32)

    wide_gate = dot(gate_hi, spread) + dot(gate_lo, spread)
    weighted = (place.astype(f32) * wide_gate).astype(bf16)
    d_route = dot(weighted, d_back[:, :1536])
    dg = d_back[:, 1536:1538].T
    d_gating = dot(place * dg[0:1], spread, ((1,), (1,))) + dot(
        place * dg[1:2], spread, ((1,), (1,))
    )
    d_logits = gating * (d_gating - jnp.sum(gating * d_gating, axis=1, keepdims=True))
    d_logits_low = d_logits.astype(bf16)
    d_ffn = d_ffn + dot(d_logits_low, w_router, ((1,), (1,))) + d_route
    ffn_norm_grad = jnp.sum(d_ffn * residual * r, axis=0)
    u = d_ffn * g_ffn
    d_residual = (
        out_grad.astype(f32)
        + r * u
        - r * r * r * residual * jnp.mean(u * residual, axis=1, keepdims=True)
    )

    d_mixed = (q * d_residual).astype(bf16)
    kappa = q * q / 3072.0 * jnp.sum(d_mixed.astype(f32) * part, axis=1, keepdims=True)
    d_mixed_full = both_halves(d_mixed, swap(d_mixed), s)
    kappa = both_halves(kappa, swap(kappa), s)
    drout = jnp.pad(d_logits_low.reshape(128, 4, 16).transpose(1, 0, 2), ((0, 0), (0, 0), (64, 48)))
    grad_out, grad_in, d_normed, g_cx, g_cbc, g_heads = mixer_backward(
        d_mixed_full, kappa, w_out, w_in, normed, ffn_in, drout, proj, y, scaled, cx, cbc, hp, marks, seg
    )
    conv_x_grad = g_cx[:, :5].transpose(1, 0, 2).reshape(5, 1536)
    conv_bc_grad = g_cbc[:, :5].transpose(1, 0, 2).reshape(5, 256)
    mixer_norm_grad = g_cx[:, 6].reshape(1536)
    head_grad = g_heads[:, :2, HEAD_AT : HEAD_AT + 6].transpose(1, 0, 2).reshape(2, 24)
    d_skip = jnp.sum(g_cx[:, 5].reshape(24, 64), axis=1)
    head_grad = jnp.concatenate([head_grad, d_skip[None]], axis=0)
    dn_own, dn_other = halves(d_normed, s)
    d_normed = dn_own + swap(dn_other.astype(bf16)).astype(f32)
    x_own = tokens.astype(f32)
    p = rms(x_own)
    in_norm_grad = jnp.sum(d_normed * x_own * p, axis=0)
    v = d_normed * g_in
    token_grad = (
        d_residual + p * v - p * p * p * x_own * jnp.mean(v * x_own, axis=1, keepdims=True)
    ).astype(bf16)

    conv_grad = lax.dynamic_update_slice(
        jnp.zeros((5, 3328), f32), conv_x_grad, (0, s * 1536)
    )
    conv_grad = lax.dynamic_update_slice(conv_grad, conv_bc_grad, (0, 3072))
    mixer_norm_grad = lax.dynamic_update_slice(
        jnp.zeros((128, 24), f32), mixer_norm_grad.reshape(64, 24), (s * 64, 0)
    )
    head_grad = lax.dynamic_update_slice(jnp.zeros((3, 48), f32), head_grad, (0, s * 24))
    small = jnp.concatenate(
        [
            in_norm_grad.reshape(128, 12),
            ffn_norm_grad.reshape(128, 12),
            mixer_norm_grad,
            conv_grad.reshape(5, 128, 26).transpose(1, 0, 2).reshape(128, 130),
            jnp.broadcast_to(head_grad.reshape(1, 144), (128, 144)),
            jnp.zeros((128, 62), f32),
        ],
        axis=1,
    )
    weighted_late, small, grad_in = lax.optimization_barrier((weighted, small, grad_in))
    small = jnp.sum(lax.all_to_all(small, ALL, 0, 0, tiled=True), axis=0)
    routed = dot(weighted_late, out_back)
    block_out = (residual + s_out + routed).astype(bf16)
    sum_in, sum_sgu, sum_out, sum_sdown = scatter(
        (
            grad_in.reshape(4, 2, 4, 4, 48, 896),
            grad_sgu.reshape(4, 2, 4, 4, 48, 256),
            grad_out.reshape(4, 4, 4, 2, 48, 384),
            grad_sdown.reshape(4, 4, 4, 2, 16, 384),
        ),
        SPECS,
        2,
    )
    back = jnp.concatenate([sum_in, sum_sgu], axis=2).reshape(8, 12, 1152)
    back = lax.all_to_all(back, ("seq", "y"), 0, 0, tiled=True).reshape(2, 4, 12, 1152)
    back = back.transpose(2, 0, 1, 3)
    bc_dt = back[..., 768:896]
    both_cores = bc_dt[:, 0] + bc_dt[:, 1]
    in_proj_grad = jnp.concatenate(
        [
            back[..., :384].reshape(12, 3072),
            back[..., 384:768].reshape(12, 3072),
            both_cores[..., :64].reshape(12, 256),
            bc_dt[..., 80:86].reshape(12, 48),
        ],
        axis=1,
    )
    router_grad = both_cores[..., 64:80].reshape(12, 64)
    sgu_grad = jnp.concatenate(
        [back[..., 896:1024].reshape(12, 1024), back[..., 1024:].reshape(12, 1024)], axis=1
    )
    rows_out = jnp.concatenate(
        [sum_out.reshape(4, 24, 384), sum_sdown.reshape(4, 8, 384)], axis=1
    )
    rows_out = lax.all_to_all(rows_out, "y", 0, 0, tiled=True).transpose(1, 0, 2).reshape(32, 1536)

    conv_grad = small[48:178].reshape(5, 26)
    return (
        block_out,
        token_grad,
        small[:12],
        in_proj_grad,
        conv_grad[:4].T,
        conv_grad[4],
        small[178:322].reshape(3, 48),
        small[24:48],
        rows_out[:24],
        small[12:24],
        router_grad,
        sgu_grad,
        rows_out[24:],
        grad_eg[None],
        grad_ed[None],
    )


def solution(mesh):
    finer = Mesh(mesh.devices.reshape(2, 4, 4, 4), ALL)
    placed = (
        P(DP_SEQ, None),
        P(DP_SEQ, None),
        P(DP, None),
        P(DP_SEQ, None),
        P(ALL),
        P(ALL, None),
        P(ALL, None),
        P(ALL),
        P(),
        P(ALL),
        P(ALL, None),
        P(ALL),
        P(ALL, None),
        P(ALL, None),
        P(ALL, None),
        P(DP, "seq", None),
        P(DP, "seq", None),
    )
    return jax.shard_map(
        local,
        mesh=finer,
        in_specs=placed,
        out_specs=(
            P(DP_SEQ, None),
            P(DP_SEQ, None),
            P(ALL),
            P(ALL, None),
            P(ALL, None),
            P(ALL),
            P(),
            P(ALL),
            P(ALL, None),
            P(ALL),
            P(ALL, None),
            P(ALL, None),
            P(ALL, None),
            P(DP, "seq", None),
            P(DP, "seq", None),
        ),
        check_vma=False,
    )
```

```python
import functools

import jax
import jax.numpy as jnp
import numpy as np
from jax import lax
from jax.experimental import pallas as pl
from jax.experimental.pallas import tpu as pltpu
from jax.sharding import Mesh
from jax.sharding import PartitionSpec as P

DP = ("z", "x", "y")
ALL = ("seq", "z", "x", "y")
DP_SEQ = ("z", "x", "y", "seq")
ORDER = (("z", "x", "y"), ("x", "y", "z"), ("y", "z", "x"))
REM = (("z", "x"), ("y", "x"), ("y", "z"))
MESH_ID = pl.DeviceIdType.MESH
EPS = 1e-05
f32 = jnp.float32
bf16 = jnp.bfloat16

ROWS_FIRST = (("y", "s", "z", "x"), "rows")
CHANNELS = (("y", "z", "x", "s"), "cols")
VECTORS = (("s", "z", "x", "y"), "one")
SPECS = (ROWS_FIRST, ROWS_FIRST, CHANNELS, CHANNELS, VECTORS)
HEAD_AT = 80
SIZES = {"y": 4, "z": 4, "x": 4, "s": 2}


def dot(a, b, dims=((1,), (0,))):
    return lax.dot_general(a, b, (dims, ((), ())), preferred_element_type=f32)


def neighbours():
    pos = {a: lax.axis_index(a) for a in DP}
    right = {a: lax.rem(pos[a] + 1, 4) for a in DP}
    left = {a: lax.rem(pos[a] + 3, 4) for a in DP}
    opp = {a: lax.rem(pos[a] + 2, 4) for a in DP}
    return pos, right, left, opp


def chip_row():
    core, y = lax.axis_index("seq"), lax.axis_index("y")
    return [(lax.rem(core + c, 2), lax.rem(y + d, 4)) for c in range(2) for d in range(4)]


def greet(right, left):
    barrier = pltpu.get_barrier_semaphore()

    def signal(device_id):
        pl.semaphore_signal(barrier, inc=1, device_id=device_id, device_id_type=MESH_ID)

    for a in ("z", "x"):
        signal({a: right[a]})
        signal({a: left[a]})
    for core, y in chip_row()[1:]:
        signal({"seq": core, "y": y})
    pl.semaphore_wait(barrier, 11)


def cuts(spec):
    return range(1 if spec[1] == "one" else 3)


def third(shape, split, a):
    rows, cols = shape[-2:]
    if split == "one":
        return (slice(None), slice(None))
    if split == "rows":
        return (pl.ds(rows // 3 * a, rows // 3), slice(None))
    return (slice(None), pl.ds(cols // 3 * a, cols // 3))


def third_shape(shape, split):
    rows, cols = shape[-2:]
    return {"one": (rows, cols), "rows": (rows // 3, cols), "cols": (rows, cols // 3)}[split]


def region(ref, spec, free, fixed, a, s=None):
    order, split = spec
    ix = []
    for d in order:
        if d == "s":
            ix.append(slice(None) if s is None else s)
        else:
            ix.append(slice(None) if d in free else fixed[d])
    return ref.at[tuple(ix) + third(ref.shape, split, a)]


def roll(v, by, axis):
    by = by % v.shape[axis]
    return pltpu.roll(v, by, axis) if by else v


def lanes(shape):
    return lax.broadcasted_iota(jnp.int32, shape, len(shape) - 1)


def moved(v, at, to, width):
    lane = lanes(v.shape)
    return jnp.where((lane >= to) & (lane < to + width), roll(v, to - at, 1), 0.0)


def gather_kernel(in_ref, gu_ref, router_ref, rows_ref, vec_ref, *refs):
    specs, n = SPECS, len(SPECS)
    outs, blocks = refs[:n], refs[n : 2 * n]
    pin, pout, bin_, bout, send0, recv0, send, recv, loc = refs[2 * n :]
    pos, right, left, opp = neighbours()
    row = chip_row()
    (core, y) = row[0]
    bc = [in_ref[:, 6144 + 128 * k : 6272 + 128 * k].astype(f32) for k in range(2)]
    router, steps = router_ref[...].astype(f32), in_ref[:, 6400:6528].astype(f32)
    for c in range(2):
        for j in range(4):
            k, at = 4 * c + j, c * 1536 + j * 384
            misc = (
                moved(bc[j // 2], 64 * (j % 2), 0, 64)
                + moved(router, 16 * j, 64, 16)
                + moved(steps, 24 * c + 6 * j, HEAD_AT, 6)
            )
            pin[k, :, :384] = in_ref[:, at : at + 384]
            pin[k, :, 384:768] = in_ref[:, 3072 + at : 3456 + at]
            pin[k, :, 768:896] = misc.astype(bf16)
            pin[k, :, 896:1024] = gu_ref[:, 128 * k : 128 * k + 128]
            pin[k, :, 1024:] = gu_ref[:, 1024 + 128 * k : 1152 + 128 * k]
    for j in range(4):
        pout[j] = rows_ref[:, 384 * j : 384 * j + 384]
    greet(right, left)
    sends, first = [], []

    def push(src, dst, k, device_id):
        c = pltpu.make_async_remote_copy(
            src_ref=src,
            dst_ref=dst,
            send_sem=send0.at[k],
            recv_sem=recv0.at[k],
            device_id=device_id,
            device_id_type=MESH_ID,
        )
        c.start()
        sends.append(c)
        first.append(c)

    for k, (c, d) in enumerate(row):
        if k:
            push(pin.at[4 * c + d], bin_.at[4 * core + y], k, {"seq": c, "y": d})
    for k, (_, d) in enumerate(row[:4]):
        if k:
            push(pout.at[d], bout.at[y], 8 + k, {"y": d})
    push(vec_ref, blocks[4].at[core], 0, {"seq": 1 - core})
    blocks[4][core] = vec_ref[...]
    bin_[4 * core + y] = pin[4 * core + y]
    bout[y] = pout[y]
    for c in first:
        c.wait_recv()
    for c in range(2):
        v = jnp.concatenate([bin_[4 * c + d].astype(f32)[:12] for d in range(4)], axis=0)
        blocks[0][c] = v[:, :896].astype(bf16)
        blocks[1][c] = v[:, 896:].astype(bf16)
    v = [bout[d].astype(f32) for d in range(4)]
    for h in range(2):
        blocks[2][h] = jnp.concatenate([v[2 * h][:24], v[2 * h + 1][:24]], axis=0).astype(bf16)
        blocks[3][h] = jnp.concatenate([v[2 * h][24:], v[2 * h + 1][24:]], axis=0).astype(bf16)

    own = []
    for i in range(n):
        ix = tuple(slice(None) if d == "s" else pos[d] for d in specs[i][0])
        c = pltpu.make_async_copy(blocks[i], outs[i].at[ix], loc.at[i])
        c.start()
        own.append(c)

    def remote(i, st, a, k, src, dst, ax, to):
        c = pltpu.make_async_remote_copy(
            src_ref=src,
            dst_ref=dst,
            send_sem=send.at[i, st, a, k],
            recv_sem=recv.at[i, st, a, k],
            device_id={ax: to},
            device_id_type=MESH_ID,
        )
        c.start()
        sends.append(c)
        return c

    every = [(i, a) for i in range(n) for a in cuts(specs[i])]
    for st in range(3):
        first, later = {}, []
        for i, a in every:
            ax, free = ORDER[a][st], ORDER[a][:st]
            dst = region(outs[i], specs[i], free, pos, a)
            src = dst
            if st == 0:
                src = blocks[i].at[(slice(None),) + third(blocks[i].shape, specs[i][1], a)]
            for d, to in enumerate((right[ax], left[ax])):
                first[i, a, d] = remote(i, st, a, d, src, dst, ax, to)
        for i, a in every:
            ax, free = ORDER[a][st], ORDER[a][:st]
            for d, (to, frm) in enumerate(((right[ax], left[ax]), (left[ax], right[ax]))):
                first[i, a, d].wait_recv()
                r = region(outs[i], specs[i], free, {**pos, ax: frm}, a, s=d)
                later.append(remote(i, st, a, 2 + d, r, r, ax, to))
        for c in later:
            c.wait_recv()
        if st == 0:
            for c in own:
                c.wait()
    for c in sends:
        c.wait_send()


def gather(in_rows, gu_rows, router_rows, rows, vec):
    n = len(SPECS)
    blocks = [(2, 48, 896), (2, 48, 256), (2, 48, 384), (2, 16, 384), (2, 16, 128)]
    outs = [
        jax.ShapeDtypeStruct(tuple(SIZES[d] for d in spec[0]) + v[1:], bf16)
        for v, spec in zip(blocks, SPECS)
    ]
    total = sum(int(np.prod(o.shape)) for o in outs) * 2
    return pl.pallas_call(
        gather_kernel,
        out_shape=outs,
        in_specs=[pl.BlockSpec(memory_space=pltpu.VMEM)] * 5,
        out_specs=[pl.BlockSpec(memory_space=pl.ANY)] * n,
        scratch_shapes=[pltpu.VMEM(v, bf16) for v in blocks]
        + [
            pltpu.VMEM((8, 16, 1152), bf16),
            pltpu.VMEM((4, 32, 384), bf16),
            pltpu.VMEM((8, 16, 1152), bf16),
            pltpu.VMEM((4, 32, 384), bf16),
            pltpu.SemaphoreType.DMA((12,)),
            pltpu.SemaphoreType.DMA((12,)),
            pltpu.SemaphoreType.DMA((n, 3, 3, 4)),
            pltpu.SemaphoreType.DMA((n, 3, 3, 4)),
            pltpu.SemaphoreType.DMA((n,)),
        ],
        compiler_params=pltpu.CompilerParams(
            collective_id=1, has_side_effects=True, vmem_limit_bytes=60 * 2**20
        ),
        cost_estimate=pl.CostEstimate(flops=0, bytes_accessed=2 * total, transcendentals=0),
        name="gather_weights",
    )(in_rows, gu_rows, router_rows, rows, vec)


def each(lead, fn):
    if not lead:
        fn((Ellipsis,))
        return

    @pl.loop(0, int(np.prod(lead)))
    def _(i):
        ix = []
        for d in reversed(lead):
            ix.append(lax.rem(i, d))
            i = lax.div(i, d)
        fn(tuple(reversed(ix)))


def scatter_kernel(*refs):
    specs, n = SPECS, len(SPECS)
    gs, (in_out, router_out, gu_out, out_out, down_out, small_out) = refs[:n], refs[n : n + 6]
    outs, refs = refs[n + 6 : 2 * n + 6], refs[2 * n + 6 :]
    held, got = refs[:n], [refs[n + 3 * i : n + 3 * i + 3] for i in range(n)]
    pin, pout, bin_, bout, other, send0, recv0, send, recv, loc = refs[4 * n :]
    pos, right, left, opp = neighbours()
    row = chip_row()
    (core, y) = row[0]

    def source(i, st, a, idx, s):
        ax = ORDER[a][2 - st]
        if st == 0:
            return region(gs[i], specs[i], [d for d in DP if d != ax], {ax: idx}, a, s)
        part = held[i].at[a, 2 + s]
        if st == 1:
            return part.at[:, idx] if REM[a][1] == ax else part.at[idx]
        me = pos[ORDER[a][1]]
        return part.at[me, idx] if REM[a][1] == ax else part.at[idx, me]

    local = {}
    for i in range(n):
        for a in cuts(specs[i]):
            ax = ORDER[a][2]
            for k, (idx, s) in enumerate(((right[ax], 0), (left[ax], 1), (pos[ax], 0), (pos[ax], 1))):
                c = pltpu.make_async_copy(source(i, 0, a, idx, s), held[i].at[a, k], loc.at[i, a, k])
                c.start()
                local[i, a, k] = c
    greet(right, left)
    sends = []

    def remote(i, st, a, k, src, ax, to):
        c = pltpu.make_async_remote_copy(
            src_ref=src,
            dst_ref=got[i][st].at[a, k],
            send_sem=send.at[i, st, a, k],
            recv_sem=recv.at[i, st, a, k],
            device_id={ax: to},
            device_id_type=MESH_ID,
        )
        c.start()
        sends.append(c)
        return c

    every = [(i, a) for i in range(n) for a in cuts(specs[i])]
    for st in range(3):
        lead = ((4, 4), (4,), ())[st]
        cp = {}
        for i, a in every:
            ax = ORDER[a][2 - st]
            cp[i, a, 0] = remote(i, st, a, 0, source(i, st, a, opp[ax], 0), ax, right[ax])
            cp[i, a, 1] = remote(i, st, a, 1, source(i, st, a, opp[ax], 1), ax, left[ax])
        for i, a in every:
            ax = ORDER[a][2 - st]
            cp[i, a, 2] = remote(i, st, a, 2, source(i, st, a, right[ax], 1), ax, right[ax])
            cp[i, a, 3] = remote(i, st, a, 3, source(i, st, a, left[ax], 0), ax, left[ax])
        for i, a in every:
            ax = ORDER[a][2 - st]
            for d, to in enumerate((right[ax], left[ax])):
                cp[i, a, d].wait_recv()
                if st == 0:
                    local[i, a, d].wait()
                    acc = held[i].at[a, d]
                else:
                    acc = source(i, st, a, to, d)
                more = got[i][st].at[a, d]

                def add(ix, acc=acc, more=more):
                    acc[ix] = (acc[ix].astype(f32) + more[ix].astype(f32)).astype(acc.dtype)

                each(lead, add)
                cp[i, a, 4 + d] = remote(i, st, a, 4 + d, acc, ax, to)
        for i, a in every:
            ax = ORDER[a][2 - st]
            if st == 0:
                local[i, a, 2].wait()
                local[i, a, 3].wait()
            for s, (p, q) in enumerate(((4, 3), (2, 5))):
                cp[i, a, p].wait_recv()
                cp[i, a, q].wait_recv()
                acc = held[i].at[a, 2 + s] if st == 0 else source(i, st, a, pos[ax], s)
                one, two = got[i][st].at[a, p], got[i][st].at[a, q]
                if st == 2:
                    ix = (s,) + third(outs[i].shape, specs[i][1], a)
                    outs[i][ix] = acc[...].astype(f32) + one[...].astype(f32) + two[...].astype(f32)
                else:

                    def finish(ix, acc=acc, one=one, two=two):
                        total = acc[ix].astype(f32) + one[ix].astype(f32) + two[ix].astype(f32)
                        acc[ix] = total.astype(acc.dtype)

                    each(lead, finish)

    for k in range(8):
        c, d = divmod(k, 4)
        pin[k, :12, :896] = outs[0][c, 12 * d : 12 * d + 12, :]
        pin[k, :12, 896:] = outs[1][c, 12 * d : 12 * d + 12, :]
    for d in range(4):
        h, at = divmod(d, 2)
        pout[d, :24] = outs[2][h, 24 * at : 24 * at + 24, :]
        pout[d, 24:] = outs[3][h, 8 * at : 8 * at + 8, :]
    last = []

    def push(src, dst, k, device_id):
        c = pltpu.make_async_remote_copy(
            src_ref=src,
            dst_ref=dst,
            send_sem=send0.at[k],
            recv_sem=recv0.at[k],
            device_id=device_id,
            device_id_type=MESH_ID,
        )
        c.start()
        sends.append(c)
        last.append(c)

    for k, (c, d) in enumerate(row):
        if k:
            push(pin.at[4 * c + d], bin_.at[4 * core + y], k, {"seq": c, "y": d})
    for k, (_, d) in enumerate(row[:4]):
        if k:
            push(pout.at[d], bout.at[y], 8 + k, {"y": d})
    push(outs[4].at[1 - core], other, 0, {"seq": 1 - core})
    bin_[4 * core + y] = pin[4 * core + y]
    bout[y] = pout[y]
    for c in last:
        c.wait_recv()
    small_out[...] = outs[4][core] + other[...]
    misc = []
    for k in range(8):
        got_k = bin_[k]
        in_out[:, 384 * k : 384 * k + 384] = got_k[:12, :384]
        in_out[:, 3072 + 384 * k : 3456 + 384 * k] = got_k[:12, 384:768]
        gu_out[:, 128 * k : 128 * k + 128] = got_k[:12, 896:1024]
        gu_out[:, 1024 + 128 * k : 1152 + 128 * k] = got_k[:12, 1024:]
        misc.append(got_k[:, 768:896])
    both = [misc[j] + misc[4 + j] for j in range(4)]
    for h in range(2):
        pair = moved(both[2 * h], 0, 0, 64) + moved(both[2 * h + 1], 0, 64, 64)
        in_out[:, 6144 + 128 * h : 6272 + 128 * h] = pair[:12]
    steps = sum(moved(misc[k], HEAD_AT, 6 * k, 6) for k in range(8))
    in_out[:, 6400:] = steps[:12, :48]
    router = sum(moved(both[j], 64, 16 * j, 16) for j in range(4))
    router_out[...] = router[:12, :64]
    for j in range(4):
        out_out[:, 384 * j : 384 * j + 384] = bout[j, :24]
        down_out[:, 384 * j : 384 * j + 384] = bout[j, 24:]
    for c in sends:
        c.wait_send()


def scatter(arrays):
    n = len(arrays)
    results = [(12, 6448), (12, 64), (12, 2048), (24, 1536), (8, 1536), (8, 128)]
    pieces = [(third_shape(v.shape, spec[1]), v.dtype) for v, spec in zip(arrays, SPECS)]
    cut = [len(cuts(spec)) for spec in SPECS]
    total = sum(int(np.prod(v.shape)) for v in arrays) * 2
    return pl.pallas_call(
        scatter_kernel,
        out_shape=[jax.ShapeDtypeStruct(v, f32) for v in results],
        in_specs=[pl.BlockSpec(memory_space=pl.ANY)] * n,
        out_specs=[pl.BlockSpec(memory_space=pltpu.VMEM)] * len(results),
        scratch_shapes=[pltpu.VMEM((2,) + v.shape[4:], f32) for v in arrays]
        + [pltpu.VMEM((k, 4, 4, 4) + p, t) for k, (p, t) in zip(cut, pieces)]
        + [
            pltpu.VMEM((k, 6) + lead + p, t)
            for k, (p, t) in zip(cut, pieces)
            for lead in ((4, 4), (4,), ())
        ]
        + [
            pltpu.VMEM((8, 16, 1152), f32),
            pltpu.VMEM((4, 32, 384), f32),
            pltpu.VMEM((8, 16, 1152), f32),
            pltpu.VMEM((4, 32, 384), f32),
            pltpu.VMEM((8, 128), f32),
            pltpu.SemaphoreType.DMA((12,)),
            pltpu.SemaphoreType.DMA((12,)),
            pltpu.SemaphoreType.DMA((n, 3, 3, 6)),
            pltpu.SemaphoreType.DMA((n, 3, 3, 6)),
            pltpu.SemaphoreType.DMA((n, 3, 4)),
        ],
        compiler_params=pltpu.CompilerParams(
            collective_id=2, has_side_effects=True, vmem_limit_bytes=56 * 2**20
        ),
        cost_estimate=pl.CostEstimate(flops=0, bytes_accessed=2 * total, transcendentals=0),
        name="scatter_grads",
    )(*arrays)


def expert_kernel(rows_ref, grad_ref, gu_ref, down_ref, pick_ref, back_ref, act_ref, wact_ref, wgu_ref):
    e_gu = dot(rows_ref[:, :1536], gu_ref[...])
    eg, eu = e_gu[:, :512], e_gu[:, 512:]
    sig = jax.nn.sigmoid(eg)
    silu = eg * sig
    act32 = silu * eu
    act = act32.astype(bf16)
    slot_gate = jnp.sum(rows_ref[:, 1536:].astype(f32) * pick_ref[...], axis=1, keepdims=True)
    d_act = dot(grad_ref[...], down_ref[...], ((1,), (1,)))
    d_gate = jnp.sum(act.astype(f32) * d_act, axis=1, keepdims=True)
    d_eg = d_act * eu * (sig + silu * (1.0 - sig))
    d_eu = d_act * silu
    d_gu = jnp.concatenate([d_eg.astype(bf16), d_eu.astype(bf16)], axis=1)
    back_ref[:, :1536] = dot(d_gu, gu_ref[...], ((1,), (1,))).astype(bf16)
    hi = d_gate.astype(bf16).astype(f32)
    lane = lax.broadcasted_iota(jnp.int32, (rows_ref.shape[0], 128), 1)
    tail = jnp.where(lane == 0, hi, jnp.where(lane == 1, d_gate - hi, 0.0))
    back_ref[:, 1536:] = tail.astype(bf16)
    act_ref[...] = act
    wact_ref[...] = (act32 * slot_gate).astype(bf16)
    wgu_ref[:, :512] = (d_eg * slot_gate).astype(bf16)
    wgu_ref[:, 512:] = (d_eu * slot_gate).astype(bf16)


def expert_grads(rows, grad_rows, gate_up, down, pick):
    n, block = rows.shape[0], 256
    widths = (1664, 512, 512, 1024)

    def blocked(w):
        return pl.BlockSpec((block, w), lambda i: (i, 0))

    def whole(v):
        return pl.BlockSpec(v.shape, lambda i: (0, 0))

    return pl.pallas_call(
        expert_kernel,
        grid=(n // block,),
        out_shape=[jax.ShapeDtypeStruct((n, w), bf16) for w in widths],
        in_specs=[blocked(1664), blocked(1536), whole(gate_up), whole(down), whole(pick)],
        out_specs=[blocked(w) for w in widths],
        compiler_params=pltpu.CompilerParams(vmem_limit_bytes=48 * 2**20),
        cost_estimate=pl.CostEstimate(
            flops=2 * n * 1536 * (1024 + 512 + 1024), bytes_accessed=26 * 2**20, transcendentals=0
        ),
        name="expert_grads",
    )(rows, grad_rows, gate_up, down, pick)


def split3(v):
    hi = v.astype(bf16)
    rest = v - hi.astype(f32)
    mid = rest.astype(bf16)
    return hi, mid, (rest - mid.astype(f32)).astype(bf16)


def taps_pre(v, marks, w):
    total = w[4:5] + w[3:4] * v
    for d in (1, 2, 3):
        total = total + w[3 - d : 4 - d] * (roll(v, d, 0) * marks[:, d : d + 1])
    return total


def taps_back(d_pre, v, marks, w):
    d_v = w[3:4] * d_pre
    d_w = [jnp.sum(d_pre * v, axis=0, keepdims=True)]
    for d in (1, 2, 3):
        masked = d_pre * marks[:, d : d + 1]
        d_w.insert(0, jnp.sum(masked * roll(v, d, 0), axis=0, keepdims=True))
        d_v = d_v + w[3 - d : 4 - d] * roll(masked, 256 - d, 0)
    zero = jnp.zeros((3, v.shape[1]), f32)
    return d_v, jnp.concatenate(d_w + [jnp.sum(d_pre, axis=0, keepdims=True), zero], axis=0)


def joined(first, second):
    return jnp.where(lanes(first.shape) < 64, first, roll(second, 64, 1))


def bc_raw(proj_ref, k):
    return joined(
        proj_ref[2 * k, :, 768:896].astype(f32), proj_ref[2 * k + 1, :, 768:896].astype(f32)
    )


def head_steps(proj_ref, hp_ref, j, tri):
    raw = proj_ref[j, :, 768:896].astype(f32) + hp_ref[j, 1:2]
    step = jnp.maximum(raw, 0.0) + jnp.log1p(jnp.exp(-jnp.abs(raw)))
    rate = -step * hp_ref[j, 0:1]
    cum = sum(dot(tri, part) for part in split3(rate))
    return raw, step, rate, cum


def triangle():
    t = lax.broadcasted_iota(jnp.int32, (256, 256), 0)
    return t >= lanes((256, 256))


def pair_of(cols, p):
    at = HEAD_AT + 2 * p
    first = jnp.broadcast_to(cols[:, at : at + 1], (256, 128))
    return jnp.where(lanes((256, 128)) < 64, first, cols[:, at + 1 : at + 2])


def fade_of(cum, cum_rows, h, inside):
    at = HEAD_AT + h
    return jnp.exp(jnp.where(inside, cum[:, at : at + 1] - cum_rows[at : at + 1], -1e30))


def forward_kernel(
    x_ref, g_ref, w_in_ref, w_out_ref, cx_ref, cbc_ref, hp_ref, marks_ref, seg_ref,
    normed_ref, proj_ref, y_ref, scaled_ref, part_ref, squares_ref, scores_ref,
):
    i = pl.program_id(0)

    @pl.when(i == 0)
    def _():
        x = x_ref[...].astype(f32)
        normed_ref[...] = (x * rms(x) * g_ref[0:1]).astype(bf16)

    @pl.when(i < 4)
    def _():
        proj_ref[i] = dot(normed_ref[...], w_in_ref[0]).astype(bf16)

    @pl.when(i == 4)
    def _():
        marks = marks_ref[...]
        b_mat, c_mat = [jax.nn.silu(taps_pre(bc_raw(proj_ref, k), marks, cbc_ref[k])) for k in (0, 1)]
        scores_ref[...] = dot(c_mat.astype(bf16), b_mat.astype(bf16), ((1,), (1,)))
        part_ref[...] = jnp.zeros_like(part_ref)
        squares_ref[...] = jnp.zeros_like(squares_ref)

    @pl.when(i >= 4)
    def _():
        j = i - 4
        marks, cx = marks_ref[...], cx_ref[j]
        causal = triangle()
        inside = causal & (marks[:, 4:5] == seg_ref[0:1])
        _, step, _, cum = head_steps(proj_ref, hp_ref, j, causal.astype(bf16))
        cum_rows = cum.T
        x = jax.nn.silu(taps_pre(proj_ref[j, :, 384:768].astype(f32), marks, cx))
        scores = scores_ref[...]
        ys = []
        for p in range(3):
            xp = x[:, 128 * p : 128 * p + 128]
            xs = (xp * pair_of(step, p)).astype(bf16)
            y0, y1 = [
                dot((fade_of(cum, cum_rows, 2 * p + k, inside) * scores).astype(bf16), xs)
                for k in (0, 1)
            ]
            ys.append(jnp.where(lanes((256, 128)) < 64, y0, y1))
        y = jnp.concatenate(ys, axis=1) + cx[5:6] * x
        z = proj_ref[j, :, :384].astype(f32)
        gated = y * jax.nn.silu(z)
        scaled = (gated * cx[6:7]).astype(bf16)
        y_ref[j] = y
        scaled_ref[j] = scaled
        squares_ref[...] += jnp.broadcast_to(
            jnp.sum(gated * gated, axis=1, keepdims=True), squares_ref.shape
        )
        for c in range(4):
            part_ref[:, c * 384 : c * 384 + 384] += dot(scaled, w_out_ref[c])


def fixed(v):
    return pl.BlockSpec(v.shape, lambda i: (0,) * len(v.shape))


def mixer_forward(x, g, w_in, w_out, cx, cbc, hp, marks, seg):
    outs = [
        jax.ShapeDtypeStruct((256, 1536), bf16),
        jax.ShapeDtypeStruct((4, 256, 896), bf16),
        jax.ShapeDtypeStruct((4, 256, 384), f32),
        jax.ShapeDtypeStruct((4, 256, 384), bf16),
        jax.ShapeDtypeStruct((256, 1536), f32),
        jax.ShapeDtypeStruct((256, 128), f32),
    ]
    return pl.pallas_call(
        forward_kernel,
        grid=(8,),
        out_shape=outs,
        in_specs=[
            fixed(x),
            fixed(g),
            pl.BlockSpec((1, 1536, 896), lambda i: (jnp.minimum(i, 3), 0, 0)),
            pl.BlockSpec((4, 384, 384), lambda i: (0, jnp.maximum(i - 4, 0), 0)),
            *[fixed(v) for v in (cx, cbc, hp, marks, seg)],
        ],
        out_specs=[fixed(o) for o in outs],
        scratch_shapes=[pltpu.VMEM((256, 256), f32)],
        compiler_params=pltpu.CompilerParams(vmem_limit_bytes=48 * 2**20),
        cost_estimate=pl.CostEstimate(
            flops=2 * 256 * 1536 * (3584 + 1536), bytes_accessed=22 * 2**20, transcendentals=2**21
        ),
        name="mixer_forward",
    )(x, g, w_in, w_out, cx, cbc, hp, marks, seg)


def backward_kernel(
    dm_ref, kappa_ref, w_out_ref, w_in_ref, normed_ref, ffn_ref, drout_ref, proj_ref, y_ref,
    scaled_ref, cx_ref, cbc_ref, hp_ref, marks_ref, seg_ref,
    gout_ref, gin_ref, dn_ref, gcx_ref, gcbc_ref, gheads_ref,
    dproj_ref, scores_ref, dscores_ref, bc_ref,
):
    i = pl.program_id(0)

    @pl.when(i == 0)
    def _():
        marks = marks_ref[...]
        for k in (0, 1):
            bc_ref[k] = jax.nn.silu(taps_pre(bc_raw(proj_ref, k), marks, cbc_ref[k])).astype(bf16)
        scores_ref[...] = dot(bc_ref[1], bc_ref[0], ((1,), (1,)))
        dscores_ref[...] = jnp.zeros_like(dscores_ref)

    @pl.when(i < 4)
    def _():
        j = i
        marks, cx = marks_ref[...], cx_ref[j]
        scaled = scaled_ref[j]
        d_scaled = jnp.zeros((256, 384), f32)
        for c in range(4):
            dm = dm_ref[:, c * 384 : c * 384 + 384]
            d_scaled = d_scaled + dot(dm, w_out_ref[c], ((1,), (1,)))
            gout_ref[c] = dot(scaled, dm, ((0,), (0,))).astype(bf16)
        y = y_ref[j]
        z = proj_ref[j, :, :384].astype(f32)
        sig = jax.nn.sigmoid(z)
        gate = z * sig
        gated = y * gate
        d_gated = d_scaled * cx[6:7] - kappa_ref[:, 0:1] * gated
        dy = d_gated * gate
        dproj_ref[j, :, :384] = (d_gated * y * (sig + gate * (1.0 - sig))).astype(bf16)
        norm_grad = jnp.sum(d_scaled * gated, axis=0, keepdims=True)

        causal = triangle()
        inside = causal & (marks[:, 4:5] == seg_ref[0:1])
        raw, step, rate, cum = head_steps(proj_ref, hp_ref, j, causal.astype(bf16))
        cum_rows = cum.T
        x_raw = proj_ref[j, :, 384:768].astype(f32)
        x_pre = taps_pre(x_raw, marks, cx)
        x_sig = jax.nn.sigmoid(x_pre)
        x = x_pre * x_sig
        scores = scores_ref[...]
        d_scores = dscores_ref[...]
        lane = lanes((256, 128))
        low_half = lane < 64
        row = lax.broadcasted_iota(jnp.int32, (128, 256), 0)
        d_cum = jnp.zeros((256, 128), f32)
        d_cum_rows = jnp.zeros((128, 256), f32)
        d_step = jnp.zeros((256, 128), f32)
        dxs = []
        for p in range(3):
            xp = x[:, 128 * p : 128 * p + 128]
            dyp = dy[:, 128 * p : 128 * p + 128]
            steps = pair_of(step, p)
            xs = (xp * steps).astype(bf16)
            dy_low = dyp.astype(bf16)
            back = []
            for k in (0, 1):
                at = HEAD_AT + 2 * p + k
                fade = fade_of(cum, cum_rows, 2 * p + k, inside)
                mine = jnp.where(low_half if k == 0 else ~low_half, dyp, 0.0).astype(bf16)
                pair = dot(mine, xs, ((1,), (1,)))
                mixing = fade * scores
                w = mixing * pair
                d_scores = d_scores + fade * pair
                d_cum = jnp.where(lane == at, jnp.sum(w, axis=1, keepdims=True), d_cum)
                d_cum_rows = jnp.where(row == at, jnp.sum(w, axis=0, keepdims=True), d_cum_rows)
                back.append(dot(mixing.astype(bf16), dy_low, ((0,), (0,))))
            d_xs = jnp.where(low_half, back[0], back[1])
            prod = xp * d_xs
            first = jnp.sum(jnp.where(low_half, prod, 0.0), axis=1, keepdims=True)
            second = jnp.sum(jnp.where(low_half, 0.0, prod), axis=1, keepdims=True)
            at = HEAD_AT + 2 * p
            d_step = jnp.where(lane == at, first, jnp.where(lane == at + 1, second, d_step))
            dxs.append(d_xs * steps)
        dscores_ref[...] = d_scores
        dx = jnp.concatenate(dxs, axis=1) + cx[5:6] * dy
        skip_grad = jnp.sum(x * dy, axis=0, keepdims=True)
        d_x_pre = dx * (x_sig + x * (1.0 - x_sig))
        d_x_raw, conv_grad = taps_back(d_x_pre, x_raw, marks, cx)
        dproj_ref[j, :, 384:768] = d_x_raw.astype(bf16)
        rowid = lax.broadcasted_iota(jnp.int32, (8, 384), 0)
        gcx_ref[j] = jnp.where(rowid == 5, skip_grad, jnp.where(rowid == 6, norm_grad, conv_grad))
        d_cum = d_cum - d_cum_rows.T
        d_rate = sum(dot(causal.astype(bf16), part, ((0,), (0,))) for part in split3(d_cum))
        d_raw = (d_step - d_rate * hp_ref[j, 0:1]) * jax.nn.sigmoid(raw)
        dproj_ref[j, :, 768:896] = d_raw.astype(bf16)
        rowid = lax.broadcasted_iota(jnp.int32, (8, 128), 0)
        gheads_ref[j] = jnp.where(
            rowid == 0,
            jnp.sum(d_rate * rate, axis=0, keepdims=True),
            jnp.where(rowid == 1, jnp.sum(d_raw, axis=0, keepdims=True), 0.0),
        )

    @pl.when(i == 4)
    def _():
        marks = marks_ref[...]
        d_scores = dscores_ref[...].astype(bf16)
        d_bc = (dot(d_scores, bc_ref[1], ((0,), (0,))), dot(d_scores, bc_ref[0]))
        low_half = lanes((256, 128)) < 64
        for k in (0, 1):
            raw = bc_raw(proj_ref, k)
            pre = taps_pre(raw, marks, cbc_ref[k])
            sig = jax.nn.sigmoid(pre)
            d_pre = d_bc[k] * (sig + pre * sig * (1.0 - sig))
            d_raw, conv_grad = taps_back(d_pre, raw, marks, cbc_ref[k])
            gcbc_ref[k] = conv_grad
            for h, moved in enumerate((d_raw, roll(d_raw, 64, 1))):
                steps = dproj_ref[2 * k + h, :, 768:896].astype(f32)
                dproj_ref[2 * k + h, :, 768:896] = jnp.where(low_half, moved, steps).astype(bf16)
        dn_ref[...] = jnp.zeros_like(dn_ref)

    @pl.when(i >= 4)
    def _():
        j = i - 4
        d_proj = dproj_ref[j]
        dn_ref[...] += dot(d_proj, w_in_ref[0], ((1,), (1,)))
        gin_ref[0, :, :768] = dot(normed_ref[...], d_proj[:, :768], ((0,), (0,))).astype(bf16)
        last = dot(normed_ref[...], d_proj[:, 768:], ((0,), (0,)))
        last = last + dot(ffn_ref[...], drout_ref[j], ((0,), (0,)))
        gin_ref[0, :, 768:] = last.astype(bf16)


def mixer_backward(dm, kappa, w_out, w_in, normed, ffn_in, drout, proj, y, scaled, cx, cbc, hp, marks, seg):
    def late(i):
        return jnp.maximum(i - 4, 0)

    def early(i):
        return jnp.minimum(i, 3)

    small = [
        jax.ShapeDtypeStruct((256, 1536), f32),
        jax.ShapeDtypeStruct((4, 8, 384), f32),
        jax.ShapeDtypeStruct((2, 8, 128), f32),
        jax.ShapeDtypeStruct((4, 8, 128), f32),
    ]
    w_out_spec = pl.BlockSpec((4, 384, 384), lambda i: (0, early(i), 0))
    w_in_spec = pl.BlockSpec((1, 1536, 896), lambda i: (late(i), 0, 0))
    return pl.pallas_call(
        backward_kernel,
        grid=(8,),
        out_shape=[
            jax.ShapeDtypeStruct((4, 1536, 384), bf16),
            jax.ShapeDtypeStruct((4, 1536, 896), bf16),
            *small,
        ],
        in_specs=[
            fixed(dm),
            fixed(kappa),
            w_out_spec,
            w_in_spec,
            *[fixed(v) for v in (normed, ffn_in, drout, proj, y, scaled, cx, cbc, hp, marks, seg)],
        ],
        out_specs=[w_out_spec, w_in_spec, *[fixed(o) for o in small]],
        scratch_shapes=[
            pltpu.VMEM((4, 256, 896), bf16),
            pltpu.VMEM((256, 256), f32),
            pltpu.VMEM((256, 256), f32),
            pltpu.VMEM((2, 256, 128), bf16),
        ],
        compiler_params=pltpu.CompilerParams(vmem_limit_bytes=56 * 2**20),
        cost_estimate=pl.CostEstimate(
            flops=4 * 256 * 1536 * (3584 + 1536), bytes_accessed=40 * 2**20, transcendentals=2**21
        ),
        name="mixer_backward",
    )(dm, kappa, w_out, w_in, normed, ffn_in, drout, proj, y, scaled, cx, cbc, hp, marks, seg)


def swap(v):
    return lax.ppermute(v, "seq", [(0, 1), (1, 0)])


def both_halves(own, other, s):
    first = jnp.where(s == 0, own, other)
    second = jnp.where(s == 0, other, own)
    return jnp.concatenate([first, second], axis=0)


def halves(v, s):
    rows = v.shape[0] // 2
    return (
        lax.dynamic_slice_in_dim(v, s * rows, rows, 0),
        lax.dynamic_slice_in_dim(v, (1 - s) * rows, rows, 0),
    )


def hi_lo(v):
    hi = v.astype(bf16)
    return hi, (v - hi.astype(f32)).astype(bf16)


def rms(v):
    return lax.rsqrt(jnp.mean(v * v, axis=-1, keepdims=True) + EPS)


def silu_grad(v):
    sig = jax.nn.sigmoid(v)
    return sig * (1.0 + v * (1.0 - sig))


def local(
    tokens,
    out_grad,
    lengths,
    routes,
    in_norm,
    in_proj,
    conv_weight,
    conv_bias,
    head_params,
    mixer_norm,
    out_proj,
    ffn_norm,
    router,
    shared_gate_up,
    shared_down,
    expert_gate_up,
    expert_down,
):
    s = lax.axis_index("seq")
    dp = lax.axis_index(DP)
    experts, slots = 64, 24
    n_slots = experts * slots

    vec = [in_norm[None], ffn_norm[None], mixer_norm[None], conv_weight.T, conv_bias[None]]
    vec = jnp.concatenate([jnp.pad(v, ((0, 0), (0, 128 - v.shape[1]))) for v in vec], axis=0)
    other_tokens = swap(tokens)
    other_grad = swap(out_grad)
    other_gate_up = swap(expert_gate_up[0])
    other_down = swap(expert_down[0])
    w_in, w_sgu, w_out, w_sdown, vecs = gather(
        jnp.pad(in_proj, ((0, 4), (0, 80))),
        jnp.pad(shared_gate_up, ((0, 4), (0, 0))),
        jnp.pad(router, ((0, 4), (0, 64))),
        jnp.concatenate([out_proj, shared_down], axis=0),
        jnp.pad(vec, ((0, 8), (0, 0))),
    )
    w_in = w_in.reshape(4, 1536, 896)
    w_sgu = w_sgu.reshape(4, 1536, 256)
    w_out = w_out.reshape(4, 1536, 384)
    w_sdown = w_sdown.reshape(4, 512, 384)

    vecs = vecs.reshape(128, 16, 128).astype(f32)
    g_in = vecs[:, 0, :12].reshape(1, 1536)
    g_ffn = vecs[:, 1, :12].reshape(1536)
    g_mix = lax.dynamic_slice_in_dim(vecs[:, 2, :24].reshape(1, 3072), s * 1536, 1536, 1)
    conv = vecs[:, 3:8, :26].transpose(1, 0, 2).reshape(5, 3328)
    heads = lax.dynamic_slice_in_dim(head_params.astype(f32), s * 24, 24, 1)
    cx = jnp.concatenate(
        [
            lax.dynamic_slice_in_dim(conv[:, :3072], s * 1536, 1536, 1),
            jnp.broadcast_to(heads[2][:, None], (24, 64)).reshape(1, 1536),
            g_mix,
            jnp.zeros((1, 1536), f32),
        ],
        axis=0,
    )
    cx = cx.reshape(8, 4, 384).transpose(1, 0, 2)
    cbc = jnp.pad(conv[:, 3072:], ((0, 3), (0, 0))).reshape(8, 2, 128).transpose(1, 0, 2)
    hp = jnp.stack([jnp.exp(heads[0]), heads[1]]).reshape(2, 4, 6).transpose(1, 0, 2)
    hp = jnp.pad(hp, ((0, 0), (0, 6), (HEAD_AT, 122 - HEAD_AT)))
    w_eg = both_halves(expert_gate_up[0], other_gate_up, s)
    w_ed = both_halves(expert_down[0], other_down, s)

    ids = jnp.arange(experts, dtype=jnp.int32)
    named = jnp.sum((routes[:, :, None] == ids).astype(f32), axis=1)
    t128 = jnp.arange(128)
    before = (t128[:, None] > t128[None, :]).astype(bf16)
    rank = dot(before, named.astype(bf16))
    slot = jnp.arange(n_slots, dtype=jnp.int32)
    spread = (slot[None, :] // slots == ids[:, None]).astype(bf16)
    is_named = dot(named.astype(bf16), spread) > 0.5
    in_slot = dot(rank.astype(bf16), spread) == (slot % slots).astype(f32)[None, :]
    place = (is_named & in_slot).astype(bf16)

    def to_slots(v):
        return dot(place, v, ((0,), (0,))).astype(bf16).reshape(experts, slots, v.shape[1])

    grad_slots, w_in = lax.optimization_barrier((to_slots(out_grad), w_in))
    grad_rows = lax.all_to_all(grad_slots, DP, 0, 0, tiled=True).reshape(n_slots, 1536)

    ends = jnp.cumsum(lengths[0])
    t256 = jnp.arange(256, dtype=jnp.int32)
    segment = jnp.sum((t256[:, None] >= ends[None, :]).astype(jnp.int32), axis=1)
    seg = segment.astype(f32)
    same = [
        (jnp.pad(segment, (d, 0), constant_values=-1)[:256] == segment).astype(f32)
        for d in range(4)
    ]
    marks = jnp.pad(jnp.stack(same + [seg], axis=1), ((0, 0), (0, 123)))
    seg = jnp.broadcast_to(seg, (8, 256))
    x_full = both_halves(tokens, other_tokens, s)
    normed, proj, y, scaled, part, squares = mixer_forward(
        x_full, jnp.broadcast_to(g_in, (8, 1536)), w_in, w_out, cx, cbc, hp, marks, seg
    )
    squares = squares[:, :1]
    part_own, part_other = halves(part, s)
    sq_own, sq_other = halves(squares, s)
    part = part_own + swap(part_other)
    q = lax.rsqrt((sq_own + swap(sq_other)) / 3072.0 + EPS)
    residual = tokens.astype(f32) + q * part

    r = rms(residual)
    ffn_in = (residual * r * g_ffn).astype(bf16)
    w_router = w_in[:, :, 832:848].transpose(1, 0, 2).reshape(1536, 64)
    logits = dot(ffn_in, w_router)
    logits = jnp.where(named > 0.5, logits, -1e30)
    top = jnp.max(logits, axis=1, keepdims=True)
    weights = jnp.where(named > 0.5, jnp.exp(logits - top), 0.0)
    gating = weights / jnp.sum(weights, axis=1, keepdims=True)
    gate_hi, gate_lo = hi_lo(gating)
    sent = to_slots(jnp.concatenate([ffn_in, gate_hi, gate_lo], axis=1))
    sent, grad_rows = lax.optimization_barrier((sent, grad_rows))
    arrived = lax.all_to_all(sent, DP, 0, 0, tiled=True).reshape(n_slots, 1664)

    ffn_full = both_halves(ffn_in, swap(ffn_in), s)
    og_full = both_halves(out_grad, other_grad, s)
    sgu = jnp.stack([dot(ffn_full, w_sgu[j]) for j in range(4)])
    sg, su = sgu[..., :128], sgu[..., 128:]
    s_act = (jax.nn.silu(sg) * su).astype(bf16)
    s_flat = s_act.transpose(1, 0, 2).reshape(256, 512)
    s_out = jnp.concatenate([dot(s_flat, w_sdown[j]) for j in range(4)], axis=1)
    s_own, s_other = halves(s_out, s)
    s_out = s_own + swap(s_other.astype(bf16)).astype(f32)
    og_cols = og_full.reshape(256, 4, 384).transpose(1, 0, 2)
    d_s_act = sum(dot(og_cols[j], w_sdown[j], ((1,), (1,))) for j in range(4))
    d_s_act = d_s_act.reshape(256, 4, 128).transpose(1, 0, 2)
    d_sgu = jnp.concatenate([d_s_act * su * silu_grad(sg), d_s_act * jax.nn.silu(sg)], axis=-1)
    d_sgu = d_sgu.astype(bf16)
    grad_sdown = jnp.stack([dot(s_flat, og_cols[j], ((0,), (0,))) for j in range(4)]).astype(bf16)
    grad_sgu = jnp.stack([dot(ffn_full, d_sgu[j], ((0,), (0,))) for j in range(4)]).astype(bf16)
    d_ffn = sum(dot(d_sgu[j], w_sgu[j], ((1,), (1,))) for j in range(4))
    df_own, df_other = halves(d_ffn, s)
    d_ffn = df_own + swap(df_other.astype(bf16)).astype(f32)

    lane = jnp.arange(128, dtype=jnp.int32) % 64
    pick = (lane == dp).astype(f32)[None, :]
    d_rows, e_act, w_act, w_gu = expert_grads(arrived, grad_rows, w_eg, w_ed, pick)
    d_back = lax.all_to_all(d_rows.reshape(experts, slots, 1664), DP, 0, 0, tiled=True)
    e_out = dot(e_act, w_ed).astype(bf16)
    grad_ed = dot(w_act, grad_rows, ((0,), (0,)))
    grad_eg = dot(arrived[:, :1536], w_gu, ((0,), (0,)))
    ge_own, ge_other = halves(grad_eg, s)
    grad_eg = ge_own + swap(ge_other.astype(bf16)).astype(f32)
    gd_own, gd_other = halves(grad_ed, s)
    grad_ed = gd_own + swap(gd_other.astype(bf16)).astype(f32)
    e_out, d_back, grad_eg, grad_ed, d_ffn = lax.optimization_barrier(
        (e_out, d_back, grad_eg, grad_ed, d_ffn)
    )
    d_back = d_back.reshape(n_slots, 1664)
    out_back = lax.all_to_all(e_out.reshape(experts, slots, 1536), DP, 0, 0, tiled=True)
    out_back = out_back.reshape(n_slots, 1536)

    wide_gate = dot(gate_hi, spread) + dot(gate_lo, spread)
    weighted = (place.astype(f32) * wide_gate).astype(bf16)
    d_route = dot(weighted, d_back[:, :1536])
    dg = d_back[:, 1536:1538].T
    d_gating = dot(place * dg[0:1], spread, ((1,), (1,))) + dot(
        place * dg[1:2], spread, ((1,), (1,))
    )
    d_logits = gating * (d_gating - jnp.sum(gating * d_gating, axis=1, keepdims=True))
    d_logits_low = d_logits.astype(bf16)
    d_ffn = d_ffn + dot(d_logits_low, w_router, ((1,), (1,))) + d_route
    ffn_norm_grad = jnp.sum(d_ffn * residual * r, axis=0)
    u = d_ffn * g_ffn
    d_residual = (
        out_grad.astype(f32)
        + r * u
        - r * r * r * residual * jnp.mean(u * residual, axis=1, keepdims=True)
    )

    d_mixed = (q * d_residual).astype(bf16)
    kappa = q * q / 3072.0 * jnp.sum(d_mixed.astype(f32) * part, axis=1, keepdims=True)
    d_mixed_full = both_halves(d_mixed, swap(d_mixed), s)
    kappa = both_halves(kappa, swap(kappa), s)
    drout = jnp.pad(d_logits_low.reshape(128, 4, 16).transpose(1, 0, 2), ((0, 0), (0, 0), (64, 48)))
    grad_out, grad_in, d_normed, g_cx, g_cbc, g_heads = mixer_backward(
        d_mixed_full, kappa, w_out, w_in, normed, ffn_in, drout, proj, y, scaled, cx, cbc, hp, marks, seg
    )
    conv_x_grad = g_cx[:, :5].transpose(1, 0, 2).reshape(5, 1536)
    conv_bc_grad = g_cbc[:, :5].transpose(1, 0, 2).reshape(5, 256)
    mixer_norm_grad = g_cx[:, 6].reshape(1536)
    head_grad = g_heads[:, :2, HEAD_AT : HEAD_AT + 6].transpose(1, 0, 2).reshape(2, 24)
    d_skip = jnp.sum(g_cx[:, 5].reshape(24, 64), axis=1)
    head_grad = jnp.concatenate([head_grad, d_skip[None]], axis=0)
    dn_own, dn_other = halves(d_normed, s)
    d_normed = dn_own + swap(dn_other.astype(bf16)).astype(f32)
    x_own = tokens.astype(f32)
    p = rms(x_own)
    in_norm_grad = jnp.sum(d_normed * x_own * p, axis=0)
    v = d_normed * g_in
    token_grad = (
        d_residual + p * v - p * p * p * x_own * jnp.mean(v * x_own, axis=1, keepdims=True)
    ).astype(bf16)

    conv_grad = lax.dynamic_update_slice(
        jnp.zeros((5, 3328), f32), conv_x_grad, (0, s * 1536)
    )
    conv_grad = lax.dynamic_update_slice(conv_grad, conv_bc_grad, (0, 3072))
    mixer_norm_grad = lax.dynamic_update_slice(
        jnp.zeros((128, 24), f32), mixer_norm_grad.reshape(64, 24), (s * 64, 0)
    )
    head_grad = lax.dynamic_update_slice(jnp.zeros((3, 48), f32), head_grad, (0, s * 24))
    def rows_of(v, width):
        return jnp.pad(v.reshape(128, 1, width), ((0, 0), (0, 0), (0, 64 - width)))

    conv_grad = conv_grad.reshape(5, 128, 26).transpose(1, 0, 2)
    small = jnp.concatenate(
        [
            rows_of(in_norm_grad, 12),
            rows_of(ffn_norm_grad, 12),
            rows_of(mixer_norm_grad, 24),
            jnp.pad(conv_grad, ((0, 0), (0, 0), (0, 38))),
        ],
        axis=1,
    )
    head_rows = jnp.broadcast_to(jnp.pad(head_grad, ((0, 5), (0, 16)))[None], (128, 8, 64))
    small = jnp.concatenate([small, head_rows], axis=2).reshape(2, 4, 4, 4, 8, 128)
    weighted_late, grad_in = lax.optimization_barrier((weighted, grad_in))
    routed = dot(weighted_late, out_back)
    block_out = (residual + s_out + routed).astype(bf16)
    block_out, small = lax.optimization_barrier((block_out, small))
    in_proj_grad, router_grad, sgu_grad, out_proj_grad, sdown_grad, small = scatter(
        (
            grad_in.reshape(4, 2, 4, 4, 48, 896),
            grad_sgu.reshape(4, 2, 4, 4, 48, 256),
            grad_out.reshape(4, 4, 4, 2, 48, 384),
            grad_sdown.reshape(4, 4, 4, 2, 16, 384),
            small,
        )
    )
    return (
        block_out,
        token_grad,
        small[0, :12],
        in_proj_grad,
        small[3:7, :26].T,
        small[7, :26],
        small[:3, 64:112],
        small[2, :24],
        out_proj_grad,
        small[1, :12],
        router_grad,
        sgu_grad,
        sdown_grad,
        grad_eg[None],
        grad_ed[None],
    )


def solution(mesh):
    finer = Mesh(mesh.devices.reshape(2, 4, 4, 4), ALL)
    placed = (
        P(DP_SEQ, None),
        P(DP_SEQ, None),
        P(DP, None),
        P(DP_SEQ, None),
        P(ALL),
        P(ALL, None),
        P(ALL, None),
        P(ALL),
        P(),
        P(ALL),
        P(ALL, None),
        P(ALL),
        P(ALL, None),
        P(ALL, None),
        P(ALL, None),
        P(DP, "seq", None),
        P(DP, "seq", None),
    )
    return jax.shard_map(
        local,
        mesh=finer,
        in_specs=placed,
        out_specs=(
            P(DP_SEQ, None),
            P(DP_SEQ, None),
            P(ALL),
            P(ALL, None),
            P(ALL, None),
            P(ALL),
            P(),
            P(ALL),
            P(ALL, None),
            P(ALL),
            P(ALL, None),
            P(ALL, None),
            P(ALL, None),
            P(DP, "seq", None),
            P(DP, "seq", None),
        ),
        check_vma=False,
    )
```

```python
import functools

import jax
import jax.numpy as jnp
import numpy as np
from jax import lax
from jax.experimental import pallas as pl
from jax.experimental.pallas import tpu as pltpu
from jax.sharding import Mesh
from jax.sharding import PartitionSpec as P

DP = ("z", "x", "y")
ALL = ("seq", "z", "x", "y")
DP_SEQ = ("z", "x", "y", "seq")
ORDER = (("z", "x", "y"), ("x", "y", "z"), ("y", "z", "x"))
REM = (("z", "x"), ("y", "x"), ("y", "z"))
MESH_ID = pl.DeviceIdType.MESH
EPS = 1e-05
f32 = jnp.float32
bf16 = jnp.bfloat16

ROWS_FIRST = (("y", "s", "z", "x"), "rows")
CHANNELS = (("y", "z", "x", "s"), "cols")
VECTORS = (("s", "z", "x", "y"), "one")
SPECS = (ROWS_FIRST, ROWS_FIRST, CHANNELS, CHANNELS, VECTORS)
HEAD_AT = 80
SIZES = {"y": 4, "z": 4, "x": 4, "s": 2}


def dot(a, b, dims=((1,), (0,))):
    return lax.dot_general(a, b, (dims, ((), ())), preferred_element_type=f32)


def neighbours():
    pos = {a: lax.axis_index(a) for a in DP}
    right = {a: lax.rem(pos[a] + 1, 4) for a in DP}
    left = {a: lax.rem(pos[a] + 3, 4) for a in DP}
    opp = {a: lax.rem(pos[a] + 2, 4) for a in DP}
    return pos, right, left, opp


def chip_row():
    core, y = lax.axis_index("seq"), lax.axis_index("y")
    return [(lax.rem(core + c, 2), lax.rem(y + d, 4)) for c in range(2) for d in range(4)]


def greet(right, left):
    barrier = pltpu.get_barrier_semaphore()

    def signal(device_id):
        pl.semaphore_signal(barrier, inc=1, device_id=device_id, device_id_type=MESH_ID)

    for a in ("z", "x"):
        signal({a: right[a]})
        signal({a: left[a]})
    for core, y in chip_row()[1:]:
        signal({"seq": core, "y": y})


def met(count):
    pl.semaphore_wait(pltpu.get_barrier_semaphore(), count)


def cuts(spec):
    return range(1 if spec[1] == "one" else 3)


def third(shape, split, a):
    rows, cols = shape[-2:]
    if split == "one":
        return (slice(None), slice(None))
    if split == "rows":
        return (pl.ds(rows // 3 * a, rows // 3), slice(None))
    return (slice(None), pl.ds(cols // 3 * a, cols // 3))


def third_shape(shape, split):
    rows, cols = shape[-2:]
    return {"one": (rows, cols), "rows": (rows // 3, cols), "cols": (rows, cols // 3)}[split]


def region(ref, spec, free, fixed, a, s=None):
    order, split = spec
    ix = []
    for d in order:
        if d == "s":
            ix.append(slice(None) if s is None else s)
        else:
            ix.append(slice(None) if d in free else fixed[d])
    return ref.at[tuple(ix) + third(ref.shape, split, a)]


def roll(v, by, axis):
    by = by % v.shape[axis]
    return pltpu.roll(v, by, axis) if by else v


def lanes(shape):
    return lax.broadcasted_iota(jnp.int32, shape, len(shape) - 1)


def moved(v, at, to, width):
    lane = lanes(v.shape)
    return jnp.where((lane >= to) & (lane < to + width), roll(v, to - at, 1), 0.0)


def gather_kernel(in_ref, gu_ref, router_ref, rows_ref, *refs):
    specs, n = SPECS, len(SPECS)
    vec_refs, outs, blocks = refs[:5], refs[5 : 5 + n], refs[5 + n : 5 + 2 * n]
    pin, pout, bin_, bout, wide, vec, send0, recv0, send, recv, loc = refs[5 + 2 * n :]
    pos, right, left, opp = neighbours()
    row = chip_row()
    (core, y) = row[0]
    greet(right, left)
    wide[...] = jnp.zeros_like(wide)
    wide[0, :12, :48] = in_ref[:, 6400:].astype(f32)
    wide[1, :12, :64] = router_ref[...].astype(f32)
    at = 0
    for v in vec_refs:
        wide[2, at : at + v.shape[0], : v.shape[1]] = v[...].astype(f32)
        at += v.shape[0]
    vec[...] = wide[2].astype(bf16)
    bc = [in_ref[:, 6144 + 128 * k : 6272 + 128 * k].astype(f32) for k in range(2)]
    steps, router = wide[0, :12], wide[1, :12]
    for c in range(2):
        for j in range(4):
            k, at = 4 * c + j, c * 1536 + j * 384
            misc = (
                moved(bc[j // 2], 64 * (j % 2), 0, 64)
                + moved(router, 16 * j, 64, 16)
                + moved(steps, 24 * c + 6 * j, HEAD_AT, 6)
            )
            pin[k, :12, :384] = in_ref[:, at : at + 384]
            pin[k, :12, 384:768] = in_ref[:, 3072 + at : 3456 + at]
            pin[k, :12, 768:896] = misc.astype(bf16)
            pin[k, :12, 896:1024] = gu_ref[:, 128 * k : 128 * k + 128]
            pin[k, :12, 1024:] = gu_ref[:, 1024 + 128 * k : 1152 + 128 * k]
    for j in range(4):
        pout[j] = rows_ref[:, 384 * j : 384 * j + 384]
    met(11)
    sends, first = [], []

    def push(src, dst, k, device_id):
        c = pltpu.make_async_remote_copy(
            src_ref=src,
            dst_ref=dst,
            send_sem=send0.at[k],
            recv_sem=recv0.at[k],
            device_id=device_id,
            device_id_type=MESH_ID,
        )
        c.start()
        sends.append(c)
        first.append(c)

    for k, (c, d) in enumerate(row):
        if k:
            push(pin.at[4 * c + d], bin_.at[4 * core + y], k, {"seq": c, "y": d})
    for k, (_, d) in enumerate(row[:4]):
        if k:
            push(pout.at[d], bout.at[y], 8 + k, {"y": d})
    push(vec, blocks[4].at[core], 0, {"seq": 1 - core})
    blocks[4][core] = vec[...]
    bin_[4 * core + y] = pin[4 * core + y]
    bout[y] = pout[y]
    for c in first:
        c.wait_recv()
    for c in range(2):
        v = jnp.concatenate([bin_[4 * c + d].astype(f32)[:12] for d in range(4)], axis=0)
        blocks[0][c] = v[:, :896].astype(bf16)
        blocks[1][c] = v[:, 896:].astype(bf16)
    v = [bout[d].astype(f32) for d in range(4)]
    for h in range(2):
        blocks[2][h] = jnp.concatenate([v[2 * h][:24], v[2 * h + 1][:24]], axis=0).astype(bf16)
        blocks[3][h] = jnp.concatenate([v[2 * h][24:], v[2 * h + 1][24:]], axis=0).astype(bf16)

    own = []
    for i in range(n):
        ix = tuple(slice(None) if d == "s" else pos[d] for d in specs[i][0])
        c = pltpu.make_async_copy(blocks[i], outs[i].at[ix], loc.at[i])
        c.start()
        own.append(c)

    def remote(i, st, a, k, src, dst, ax, to):
        c = pltpu.make_async_remote_copy(
            src_ref=src,
            dst_ref=dst,
            send_sem=send.at[i, st, a, k],
            recv_sem=recv.at[i, st, a, k],
            device_id={ax: to},
            device_id_type=MESH_ID,
        )
        c.start()
        sends.append(c)
        return c

    every = [(i, a) for i in range(n) for a in cuts(specs[i])]
    first, later = {}, {}

    def begin(i, a, st):
        ax, free = ORDER[a][st], ORDER[a][:st]
        dst = region(outs[i], specs[i], free, pos, a)
        src = dst
        if st == 0:
            src = blocks[i].at[(slice(None),) + third(blocks[i].shape, specs[i][1], a)]
        for d, to in enumerate((right[ax], left[ax])):
            first[i, a, d] = remote(i, st, a, d, src, dst, ax, to)

    for i, a in every:
        begin(i, a, 0)
    for c in own:
        c.wait()
    for st in range(3):
        for i, a in every:
            ax, free = ORDER[a][st], ORDER[a][:st]
            for d, (to, frm) in enumerate(((right[ax], left[ax]), (left[ax], right[ax]))):
                first[i, a, d].wait_recv()
                r = region(outs[i], specs[i], free, {**pos, ax: frm}, a, s=d)
                later[i, a, d] = remote(i, st, a, 2 + d, r, r, ax, to)
        for i, a in every:
            for d in range(2):
                later[i, a, d].wait_recv()
            if st < 2:
                begin(i, a, st + 1)
    for c in sends:
        c.wait_send()


def gather(in_proj, gate_up, router, rows, vectors):
    n = len(SPECS)
    blocks = [(2, 48, 896), (2, 48, 256), (2, 48, 384), (2, 16, 384), (2, 16, 128)]
    outs = [
        jax.ShapeDtypeStruct(tuple(SIZES[d] for d in spec[0]) + v[1:], bf16)
        for v, spec in zip(blocks, SPECS)
    ]
    total = sum(int(np.prod(o.shape)) for o in outs) * 2
    return pl.pallas_call(
        gather_kernel,
        out_shape=outs,
        in_specs=[pl.BlockSpec(memory_space=pltpu.VMEM)] * 9,
        out_specs=[pl.BlockSpec(memory_space=pl.ANY)] * n,
        scratch_shapes=[pltpu.VMEM(v, bf16) for v in blocks]
        + [
            pltpu.VMEM((8, 16, 1152), bf16),
            pltpu.VMEM((4, 32, 384), bf16),
            pltpu.VMEM((8, 16, 1152), bf16),
            pltpu.VMEM((4, 32, 384), bf16),
            pltpu.VMEM((3, 16, 128), f32),
            pltpu.VMEM((16, 128), bf16),
            pltpu.SemaphoreType.DMA((12,)),
            pltpu.SemaphoreType.DMA((12,)),
            pltpu.SemaphoreType.DMA((n, 3, 3, 4)),
            pltpu.SemaphoreType.DMA((n, 3, 3, 4)),
            pltpu.SemaphoreType.DMA((n,)),
        ],
        compiler_params=pltpu.CompilerParams(
            collective_id=1, has_side_effects=True, vmem_limit_bytes=60 * 2**20
        ),
        cost_estimate=pl.CostEstimate(flops=0, bytes_accessed=2 * total, transcendentals=0),
        name="gather_weights",
    )(in_proj, gate_up, router, rows, *vectors)


def each(lead, fn):
    if not lead:
        fn((Ellipsis,))
        return

    @pl.loop(0, int(np.prod(lead)))
    def _(i):
        ix = []
        for d in reversed(lead):
            ix.append(lax.rem(i, d))
            i = lax.div(i, d)
        fn(tuple(reversed(ix)))


def scatter_kernel(*refs):
    specs, n = SPECS, len(SPECS)
    gs, (bin_, bout, small_out) = refs[:n], refs[n : n + 3]
    outs, refs = refs[n + 3 : 2 * n + 3], refs[2 * n + 3 :]
    held, got = refs[:n], [refs[n + 3 * i : n + 3 * i + 3] for i in range(n)]
    pin, pout, other, send0, recv0, send, recv, loc = refs[4 * n :]
    pos, right, left, opp = neighbours()
    row = chip_row()
    (core, y) = row[0]

    def source(i, st, a, idx, s):
        ax = ORDER[a][2 - st]
        if st == 0:
            return region(gs[i], specs[i], [d for d in DP if d != ax], {ax: idx}, a, s)
        part = held[i].at[a, 2 + s]
        if st == 1:
            return part.at[:, idx] if REM[a][1] == ax else part.at[idx]
        me = pos[ORDER[a][1]]
        return part.at[me, idx] if REM[a][1] == ax else part.at[idx, me]

    local = {}
    for i in range(n):
        for a in cuts(specs[i]):
            ax = ORDER[a][2]
            for k, (idx, s) in enumerate(((right[ax], 0), (left[ax], 1), (pos[ax], 0), (pos[ax], 1))):
                c = pltpu.make_async_copy(source(i, 0, a, idx, s), held[i].at[a, k], loc.at[i, a, k])
                c.start()
                local[i, a, k] = c
    greet(right, left)
    met(11)
    sends = []

    def remote(i, st, a, k, src, ax, to):
        c = pltpu.make_async_remote_copy(
            src_ref=src,
            dst_ref=got[i][st].at[a, k],
            send_sem=send.at[i, st, a, k],
            recv_sem=recv.at[i, st, a, k],
            device_id={ax: to},
            device_id_type=MESH_ID,
        )
        c.start()
        sends.append(c)
        return c

    every = [(i, a) for i in range(n) for a in cuts(specs[i])]
    cp = {}

    def begin(i, a, st):
        ax = ORDER[a][2 - st]
        cp[i, a, 0] = remote(i, st, a, 0, source(i, st, a, opp[ax], 0), ax, right[ax])
        cp[i, a, 1] = remote(i, st, a, 1, source(i, st, a, opp[ax], 1), ax, left[ax])
        cp[i, a, 2] = remote(i, st, a, 2, source(i, st, a, right[ax], 1), ax, right[ax])
        cp[i, a, 3] = remote(i, st, a, 3, source(i, st, a, left[ax], 0), ax, left[ax])

    for i, a in every:
        begin(i, a, 0)
    for st in range(3):
        lead = ((4, 4), (4,), ())[st]
        for i, a in every:
            ax = ORDER[a][2 - st]
            for d, to in enumerate((right[ax], left[ax])):
                cp[i, a, d].wait_recv()
                if st == 0:
                    local[i, a, d].wait()
                    acc = held[i].at[a, d]
                else:
                    acc = source(i, st, a, to, d)
                more = got[i][st].at[a, d]

                def add(ix, acc=acc, more=more):
                    acc[ix] = (acc[ix].astype(f32) + more[ix].astype(f32)).astype(acc.dtype)

                each(lead, add)
                cp[i, a, 4 + d] = remote(i, st, a, 4 + d, acc, ax, to)
        for i, a in every:
            ax = ORDER[a][2 - st]
            if st == 0:
                local[i, a, 2].wait()
                local[i, a, 3].wait()
            for s, (p, q) in enumerate(((4, 3), (2, 5))):
                cp[i, a, p].wait_recv()
                cp[i, a, q].wait_recv()
                acc = held[i].at[a, 2 + s] if st == 0 else source(i, st, a, pos[ax], s)
                one, two = got[i][st].at[a, p], got[i][st].at[a, q]
                if st == 2:
                    ix = (s,) + third(outs[i].shape, specs[i][1], a)
                    outs[i][ix] = acc[...].astype(f32) + one[...].astype(f32) + two[...].astype(f32)
                else:

                    def close(ix, acc=acc, one=one, two=two):
                        total = acc[ix].astype(f32) + one[ix].astype(f32) + two[ix].astype(f32)
                        acc[ix] = total.astype(acc.dtype)

                    each(lead, close)
            if st < 2:
                begin(i, a, st + 1)

    for k in range(8):
        c, d = divmod(k, 4)
        pin[k, :12, :896] = outs[0][c, 12 * d : 12 * d + 12, :]
        pin[k, :12, 896:] = outs[1][c, 12 * d : 12 * d + 12, :]
    for d in range(4):
        h, at = divmod(d, 2)
        pout[d, :24] = outs[2][h, 24 * at : 24 * at + 24, :]
        pout[d, 24:] = outs[3][h, 8 * at : 8 * at + 8, :]
    last = []

    def push(src, dst, k, device_id):
        c = pltpu.make_async_remote_copy(
            src_ref=src,
            dst_ref=dst,
            send_sem=send0.at[k],
            recv_sem=recv0.at[k],
            device_id=device_id,
            device_id_type=MESH_ID,
        )
        c.start()
        sends.append(c)
        last.append(c)

    for k, (c, d) in enumerate(row):
        if k:
            push(pin.at[4 * c + d], bin_.at[4 * core + y], k, {"seq": c, "y": d})
    for k, (_, d) in enumerate(row[:4]):
        if k:
            push(pout.at[d], bout.at[y], 8 + k, {"y": d})
    push(outs[4].at[1 - core], other, 0, {"seq": 1 - core})
    bin_[4 * core + y] = pin[4 * core + y]
    bout[y] = pout[y]
    for c in last:
        c.wait_recv()
    small_out[...] = outs[4][core] + other[...]
    for c in sends:
        c.wait_send()


def finish_kernel(bin_, bout, small, in_out, router_out, gu_out, out_out, down_out, heads_out, taps_out, *vecs):
    misc = []
    for k in range(8):
        got_k = bin_[k]
        in_out[:, 384 * k : 384 * k + 384] = got_k[:12, :384]
        in_out[:, 3072 + 384 * k : 3456 + 384 * k] = got_k[:12, 384:768]
        gu_out[:, 128 * k : 128 * k + 128] = got_k[:12, 896:1024]
        gu_out[:, 1024 + 128 * k : 1152 + 128 * k] = got_k[:12, 1024:]
        misc.append(got_k[:, 768:896])
    both = [misc[j] + misc[4 + j] for j in range(4)]
    for h in range(2):
        pair = moved(both[2 * h], 0, 0, 64) + moved(both[2 * h + 1], 0, 64, 64)
        in_out[:, 6144 + 128 * h : 6272 + 128 * h] = pair[:12]
    steps = sum(moved(misc[k], HEAD_AT, 6 * k, 6) for k in range(8))
    in_out[:, 6400:] = steps[:12, :48]
    router = sum(moved(both[j], 64, 16 * j, 16) for j in range(4))
    router_out[...] = router[:12, :64]
    for j in range(4):
        out_out[:, 384 * j : 384 * j + 384] = bout[j, :24]
        down_out[:, 384 * j : 384 * j + 384] = bout[j, 24:]
    heads_out[...] = moved(small[...], 64, 0, 48)[:3, :48]
    taps_out[...] = jnp.concatenate([small[...]] * 16, axis=0).T[:26, 3:7]
    for v, at in zip(vecs, (0, 1, 2, 7)):
        v[...] = small[at : at + 1, : v.shape[1]]


def finish(bin_, bout, small):
    results = [(12, 6448), (12, 64), (12, 2048), (24, 1536), (8, 1536), (3, 48), (26, 4)]
    results += [(1, 12), (1, 12), (1, 24), (1, 26)]
    return pl.pallas_call(
        finish_kernel,
        out_shape=[jax.ShapeDtypeStruct(v, f32) for v in results],
        in_specs=[pl.BlockSpec(memory_space=pltpu.VMEM)] * 3,
        out_specs=[pl.BlockSpec(memory_space=pltpu.VMEM)] * len(results),
        name="finish_grads",
    )(bin_, bout, small)


def scatter(arrays):
    n = len(arrays)
    results = [(8, 16, 1152), (4, 32, 384), (8, 128)]
    pieces = [(third_shape(v.shape, spec[1]), v.dtype) for v, spec in zip(arrays, SPECS)]
    cut = [len(cuts(spec)) for spec in SPECS]
    total = sum(int(np.prod(v.shape)) for v in arrays) * 2
    return pl.pallas_call(
        scatter_kernel,
        out_shape=[jax.ShapeDtypeStruct(v, f32) for v in results],
        in_specs=[pl.BlockSpec(memory_space=pl.ANY)] * n,
        out_specs=[pl.BlockSpec(memory_space=pltpu.VMEM)] * len(results),
        scratch_shapes=[pltpu.VMEM((2,) + v.shape[4:], f32) for v in arrays]
        + [pltpu.VMEM((k, 4, 4, 4) + p, t) for k, (p, t) in zip(cut, pieces)]
        + [
            pltpu.VMEM((k, 6) + lead + p, t)
            for k, (p, t) in zip(cut, pieces)
            for lead in ((4, 4), (4,), ())
        ]
        + [
            pltpu.VMEM((8, 16, 1152), f32),
            pltpu.VMEM((4, 32, 384), f32),
            pltpu.VMEM((8, 128), f32),
            pltpu.SemaphoreType.DMA((12,)),
            pltpu.SemaphoreType.DMA((12,)),
            pltpu.SemaphoreType.DMA((n, 3, 3, 6)),
            pltpu.SemaphoreType.DMA((n, 3, 3, 6)),
            pltpu.SemaphoreType.DMA((n, 3, 4)),
        ],
        compiler_params=pltpu.CompilerParams(
            collective_id=2, has_side_effects=True, vmem_limit_bytes=56 * 2**20
        ),
        cost_estimate=pl.CostEstimate(flops=0, bytes_accessed=2 * total, transcendentals=0),
        name="scatter_grads",
    )(*arrays)


def expert_kernel(rows_ref, grad_ref, gu_ref, down_ref, pick_ref, back_ref, act_ref, wact_ref, wgu_ref):
    e_gu = dot(rows_ref[:, :1536], gu_ref[...])
    eg, eu = e_gu[:, :512], e_gu[:, 512:]
    sig = jax.nn.sigmoid(eg)
    silu = eg * sig
    act32 = silu * eu
    act = act32.astype(bf16)
    slot_gate = jnp.sum(rows_ref[:, 1536:].astype(f32) * pick_ref[...], axis=1, keepdims=True)
    d_act = dot(grad_ref[...], down_ref[...], ((1,), (1,)))
    d_gate = jnp.sum(act.astype(f32) * d_act, axis=1, keepdims=True)
    d_eg = d_act * eu * (sig + silu * (1.0 - sig))
    d_eu = d_act * silu
    d_gu = jnp.concatenate([d_eg.astype(bf16), d_eu.astype(bf16)], axis=1)
    back_ref[:, :1536] = dot(d_gu, gu_ref[...], ((1,), (1,))).astype(bf16)
    hi = d_gate.astype(bf16).astype(f32)
    lane = lax.broadcasted_iota(jnp.int32, (rows_ref.shape[0], 128), 1)
    tail = jnp.where(lane == 0, hi, jnp.where(lane == 1, d_gate - hi, 0.0))
    back_ref[:, 1536:] = tail.astype(bf16)
    act_ref[...] = act
    wact_ref[...] = (act32 * slot_gate).astype(bf16)
    wgu_ref[:, :512] = (d_eg * slot_gate).astype(bf16)
    wgu_ref[:, 512:] = (d_eu * slot_gate).astype(bf16)


def expert_grads(rows, grad_rows, gate_up, down, pick):
    n, block = rows.shape[0], 512
    widths = (1664, 512, 512, 1024)

    def blocked(w):
        return pl.BlockSpec((block, w), lambda i: (i, 0))

    def whole(v):
        return pl.BlockSpec(v.shape, lambda i: (0, 0))

    return pl.pallas_call(
        expert_kernel,
        grid=(n // block,),
        out_shape=[jax.ShapeDtypeStruct((n, w), bf16) for w in widths],
        in_specs=[blocked(1664), blocked(1536), whole(gate_up), whole(down), whole(pick)],
        out_specs=[blocked(w) for w in widths],
        compiler_params=pltpu.CompilerParams(vmem_limit_bytes=48 * 2**20),
        cost_estimate=pl.CostEstimate(
            flops=2 * n * 1536 * (1024 + 512 + 1024), bytes_accessed=26 * 2**20, transcendentals=0
        ),
        name="expert_grads",
    )(rows, grad_rows, gate_up, down, pick)


def split3(v):
    hi = v.astype(bf16)
    rest = v - hi.astype(f32)
    mid = rest.astype(bf16)
    return hi, mid, (rest - mid.astype(f32)).astype(bf16)


def taps_pre(v, marks, w):
    total = w[4:5] + w[3:4] * v
    for d in (1, 2, 3):
        total = total + w[3 - d : 4 - d] * (roll(v, d, 0) * marks[:, d : d + 1])
    return total


def taps_back(d_pre, v, marks, w):
    d_v = w[3:4] * d_pre
    d_w = [jnp.sum(d_pre * v, axis=0, keepdims=True)]
    for d in (1, 2, 3):
        masked = d_pre * marks[:, d : d + 1]
        d_w.insert(0, jnp.sum(masked * roll(v, d, 0), axis=0, keepdims=True))
        d_v = d_v + w[3 - d : 4 - d] * roll(masked, 256 - d, 0)
    zero = jnp.zeros((3, v.shape[1]), f32)
    return d_v, jnp.concatenate(d_w + [jnp.sum(d_pre, axis=0, keepdims=True), zero], axis=0)


def joined(first, second):
    return jnp.where(lanes(first.shape) < 64, first, roll(second, 64, 1))


def bc_raw(proj_ref, k):
    return joined(
        proj_ref[2 * k, :, 768:896].astype(f32), proj_ref[2 * k + 1, :, 768:896].astype(f32)
    )


def head_steps(proj_ref, hp_ref, j, tri):
    raw = proj_ref[j, :, 768:896].astype(f32) + hp_ref[j, 1:2]
    step = jnp.maximum(raw, 0.0) + jnp.log1p(jnp.exp(-jnp.abs(raw)))
    rate = -step * hp_ref[j, 0:1]
    cum = sum(dot(tri, part) for part in split3(rate))
    return raw, step, rate, cum


def triangle():
    t = lax.broadcasted_iota(jnp.int32, (256, 256), 0)
    return t >= lanes((256, 256))


def pair_of(cols, p):
    at = HEAD_AT + 2 * p
    first = jnp.broadcast_to(cols[:, at : at + 1], (256, 128))
    return jnp.where(lanes((256, 128)) < 64, first, cols[:, at + 1 : at + 2])


def fade_of(cum, cum_rows, h, inside):
    at = HEAD_AT + h
    return jnp.exp(jnp.where(inside, cum[:, at : at + 1] - cum_rows[at : at + 1], -1e30))


def forward_kernel(
    x_ref, g_ref, w_in_ref, w_out_ref, cx_ref, cbc_ref, hp_ref, marks_ref, seg_ref,
    normed_ref, proj_ref, y_ref, scaled_ref, part_ref, squares_ref, scores_ref,
):
    i = pl.program_id(0)

    @pl.when(i == 0)
    def _():
        x = x_ref[...].astype(f32)
        normed_ref[...] = (x * rms(x) * g_ref[0:1]).astype(bf16)

    @pl.when(i < 4)
    def _():
        proj_ref[i] = dot(normed_ref[...], w_in_ref[0]).astype(bf16)

    @pl.when(i == 4)
    def _():
        marks = marks_ref[...]
        b_mat, c_mat = [jax.nn.silu(taps_pre(bc_raw(proj_ref, k), marks, cbc_ref[k])) for k in (0, 1)]
        scores_ref[...] = dot(c_mat.astype(bf16), b_mat.astype(bf16), ((1,), (1,)))
        part_ref[...] = jnp.zeros_like(part_ref)
        squares_ref[...] = jnp.zeros_like(squares_ref)

    @pl.when(i >= 4)
    def _():
        j = i - 4
        marks, cx = marks_ref[...], cx_ref[j]
        causal = triangle()
        inside = causal & (marks[:, 4:5] == seg_ref[0:1])
        _, step, _, cum = head_steps(proj_ref, hp_ref, j, causal.astype(bf16))
        cum_rows = cum.T
        x = jax.nn.silu(taps_pre(proj_ref[j, :, 384:768].astype(f32), marks, cx))
        scores = scores_ref[...]
        ys = []
        for p in range(3):
            xp = x[:, 128 * p : 128 * p + 128]
            xs = (xp * pair_of(step, p)).astype(bf16)
            y0, y1 = [
                dot((fade_of(cum, cum_rows, 2 * p + k, inside) * scores).astype(bf16), xs)
                for k in (0, 1)
            ]
            ys.append(jnp.where(lanes((256, 128)) < 64, y0, y1))
        y = jnp.concatenate(ys, axis=1) + cx[5:6] * x
        z = proj_ref[j, :, :384].astype(f32)
        gated = y * jax.nn.silu(z)
        scaled = (gated * cx[6:7]).astype(bf16)
        y_ref[j] = y
        scaled_ref[j] = scaled
        squares_ref[...] += jnp.broadcast_to(
            jnp.sum(gated * gated, axis=1, keepdims=True), squares_ref.shape
        )
        for c in range(4):
            part_ref[:, c * 384 : c * 384 + 384] += dot(scaled, w_out_ref[c])


def fixed(v):
    return pl.BlockSpec(v.shape, lambda i: (0,) * len(v.shape))


def mixer_forward(x, g, w_in, w_out, cx, cbc, hp, marks, seg):
    outs = [
        jax.ShapeDtypeStruct((256, 1536), bf16),
        jax.ShapeDtypeStruct((4, 256, 896), bf16),
        jax.ShapeDtypeStruct((4, 256, 384), f32),
        jax.ShapeDtypeStruct((4, 256, 384), bf16),
        jax.ShapeDtypeStruct((256, 1536), f32),
        jax.ShapeDtypeStruct((256, 128), f32),
    ]
    return pl.pallas_call(
        forward_kernel,
        grid=(8,),
        out_shape=outs,
        in_specs=[
            fixed(x),
            fixed(g),
            pl.BlockSpec((1, 1536, 896), lambda i: (jnp.minimum(i, 3), 0, 0)),
            pl.BlockSpec((4, 384, 384), lambda i: (0, jnp.maximum(i - 4, 0), 0)),
            *[fixed(v) for v in (cx, cbc, hp, marks, seg)],
        ],
        out_specs=[fixed(o) for o in outs],
        scratch_shapes=[pltpu.VMEM((256, 256), f32)],
        compiler_params=pltpu.CompilerParams(vmem_limit_bytes=48 * 2**20),
        cost_estimate=pl.CostEstimate(
            flops=2 * 256 * 1536 * (3584 + 1536), bytes_accessed=22 * 2**20, transcendentals=2**21
        ),
        name="mixer_forward",
    )(x, g, w_in, w_out, cx, cbc, hp, marks, seg)


def backward_kernel(
    dm_ref, kappa_ref, w_out_ref, w_in_ref, normed_ref, ffn_ref, drout_ref, proj_ref, y_ref,
    scaled_ref, cx_ref, cbc_ref, hp_ref, marks_ref, seg_ref,
    gout_ref, gin_ref, dn_ref, gcx_ref, gcbc_ref, gheads_ref,
    dproj_ref, scores_ref, dscores_ref, bc_ref,
):
    i = pl.program_id(0)

    @pl.when(i == 0)
    def _():
        marks = marks_ref[...]
        for k in (0, 1):
            bc_ref[k] = jax.nn.silu(taps_pre(bc_raw(proj_ref, k), marks, cbc_ref[k])).astype(bf16)
        scores_ref[...] = dot(bc_ref[1], bc_ref[0], ((1,), (1,)))
        dscores_ref[...] = jnp.zeros_like(dscores_ref)

    @pl.when(i < 4)
    def _():
        j = i
        marks, cx = marks_ref[...], cx_ref[j]
        scaled = scaled_ref[j]
        d_scaled = jnp.zeros((256, 384), f32)
        for c in range(4):
            dm = dm_ref[:, c * 384 : c * 384 + 384]
            d_scaled = d_scaled + dot(dm, w_out_ref[c], ((1,), (1,)))
            gout_ref[c] = dot(scaled, dm, ((0,), (0,))).astype(bf16)
        y = y_ref[j]
        z = proj_ref[j, :, :384].astype(f32)
        sig = jax.nn.sigmoid(z)
        gate = z * sig
        gated = y * gate
        d_gated = d_scaled * cx[6:7] - kappa_ref[:, 0:1] * gated
        dy = d_gated * gate
        dproj_ref[j, :, :384] = (d_gated * y * (sig + gate * (1.0 - sig))).astype(bf16)
        norm_grad = jnp.sum(d_scaled * gated, axis=0, keepdims=True)

        causal = triangle()
        inside = causal & (marks[:, 4:5] == seg_ref[0:1])
        raw, step, rate, cum = head_steps(proj_ref, hp_ref, j, causal.astype(bf16))
        cum_rows = cum.T
        x_raw = proj_ref[j, :, 384:768].astype(f32)
        x_pre = taps_pre(x_raw, marks, cx)
        x_sig = jax.nn.sigmoid(x_pre)
        x = x_pre * x_sig
        scores = scores_ref[...]
        d_scores = dscores_ref[...]
        lane = lanes((256, 128))
        low_half = lane < 64
        row = lax.broadcasted_iota(jnp.int32, (128, 256), 0)
        d_cum = jnp.zeros((256, 128), f32)
        d_cum_rows = jnp.zeros((128, 256), f32)
        d_step = jnp.zeros((256, 128), f32)
        dxs = []
        for p in range(3):
            xp = x[:, 128 * p : 128 * p + 128]
            dyp = dy[:, 128 * p : 128 * p + 128]
            steps = pair_of(step, p)
            xs = (xp * steps).astype(bf16)
            dy_low = dyp.astype(bf16)
            back = []
            for k in (0, 1):
                at = HEAD_AT + 2 * p + k
                fade = fade_of(cum, cum_rows, 2 * p + k, inside)
                mine = jnp.where(low_half if k == 0 else ~low_half, dyp, 0.0).astype(bf16)
                pair = dot(mine, xs, ((1,), (1,)))
                mixing = fade * scores
                w = mixing * pair
                d_scores = d_scores + fade * pair
                d_cum = jnp.where(lane == at, jnp.sum(w, axis=1, keepdims=True), d_cum)
                d_cum_rows = jnp.where(row == at, jnp.sum(w, axis=0, keepdims=True), d_cum_rows)
                back.append(dot(mixing.astype(bf16), dy_low, ((0,), (0,))))
            d_xs = jnp.where(low_half, back[0], back[1])
            prod = xp * d_xs
            first = jnp.sum(jnp.where(low_half, prod, 0.0), axis=1, keepdims=True)
            second = jnp.sum(jnp.where(low_half, 0.0, prod), axis=1, keepdims=True)
            at = HEAD_AT + 2 * p
            d_step = jnp.where(lane == at, first, jnp.where(lane == at + 1, second, d_step))
            dxs.append(d_xs * steps)
        dscores_ref[...] = d_scores
        dx = jnp.concatenate(dxs, axis=1) + cx[5:6] * dy
        skip_grad = jnp.sum(x * dy, axis=0, keepdims=True)
        d_x_pre = dx * (x_sig + x * (1.0 - x_sig))
        d_x_raw, conv_grad = taps_back(d_x_pre, x_raw, marks, cx)
        dproj_ref[j, :, 384:768] = d_x_raw.astype(bf16)
        rowid = lax.broadcasted_iota(jnp.int32, (8, 384), 0)
        gcx_ref[j] = jnp.where(rowid == 5, skip_grad, jnp.where(rowid == 6, norm_grad, conv_grad))
        d_cum = d_cum - d_cum_rows.T
        d_rate = sum(dot(causal.astype(bf16), part, ((0,), (0,))) for part in split3(d_cum))
        d_raw = (d_step - d_rate * hp_ref[j, 0:1]) * jax.nn.sigmoid(raw)
        dproj_ref[j, :, 768:896] = d_raw.astype(bf16)
        rowid = lax.broadcasted_iota(jnp.int32, (8, 128), 0)
        gheads_ref[j] = jnp.where(
            rowid == 0,
            jnp.sum(d_rate * rate, axis=0, keepdims=True),
            jnp.where(rowid == 1, jnp.sum(d_raw, axis=0, keepdims=True), 0.0),
        )

    @pl.when(i == 4)
    def _():
        marks = marks_ref[...]
        d_scores = dscores_ref[...].astype(bf16)
        d_bc = (dot(d_scores, bc_ref[1], ((0,), (0,))), dot(d_scores, bc_ref[0]))
        low_half = lanes((256, 128)) < 64
        for k in (0, 1):
            raw = bc_raw(proj_ref, k)
            pre = taps_pre(raw, marks, cbc_ref[k])
            sig = jax.nn.sigmoid(pre)
            d_pre = d_bc[k] * (sig + pre * sig * (1.0 - sig))
            d_raw, conv_grad = taps_back(d_pre, raw, marks, cbc_ref[k])
            gcbc_ref[k] = conv_grad
            for h, moved in enumerate((d_raw, roll(d_raw, 64, 1))):
                steps = dproj_ref[2 * k + h, :, 768:896].astype(f32)
                dproj_ref[2 * k + h, :, 768:896] = jnp.where(low_half, moved, steps).astype(bf16)
        dn_ref[...] = jnp.zeros_like(dn_ref)

    @pl.when(i >= 4)
    def _():
        j = i - 4
        d_proj = dproj_ref[j]
        dn_ref[...] += dot(d_proj, w_in_ref[0], ((1,), (1,)))
        gin_ref[0, :, :768] = dot(normed_ref[...], d_proj[:, :768], ((0,), (0,))).astype(bf16)
        last = dot(normed_ref[...], d_proj[:, 768:], ((0,), (0,)))
        last = last + dot(ffn_ref[...], drout_ref[j], ((0,), (0,)))
        gin_ref[0, :, 768:] = last.astype(bf16)


def mixer_backward(dm, kappa, w_out, w_in, normed, ffn_in, drout, proj, y, scaled, cx, cbc, hp, marks, seg):
    def late(i):
        return jnp.maximum(i - 4, 0)

    def early(i):
        return jnp.minimum(i, 3)

    small = [
        jax.ShapeDtypeStruct((256, 1536), f32),
        jax.ShapeDtypeStruct((4, 8, 384), f32),
        jax.ShapeDtypeStruct((2, 8, 128), f32),
        jax.ShapeDtypeStruct((4, 8, 128), f32),
    ]
    w_out_spec = pl.BlockSpec((4, 384, 384), lambda i: (0, early(i), 0))
    w_in_spec = pl.BlockSpec((1, 1536, 896), lambda i: (late(i), 0, 0))
    return pl.pallas_call(
        backward_kernel,
        grid=(8,),
        out_shape=[
            jax.ShapeDtypeStruct((4, 1536, 384), bf16),
            jax.ShapeDtypeStruct((4, 1536, 896), bf16),
            *small,
        ],
        in_specs=[
            fixed(dm),
            fixed(kappa),
            w_out_spec,
            w_in_spec,
            *[fixed(v) for v in (normed, ffn_in, drout, proj, y, scaled, cx, cbc, hp, marks, seg)],
        ],
        out_specs=[w_out_spec, w_in_spec, *[fixed(o) for o in small]],
        scratch_shapes=[
            pltpu.VMEM((4, 256, 896), bf16),
            pltpu.VMEM((256, 256), f32),
            pltpu.VMEM((256, 256), f32),
            pltpu.VMEM((2, 256, 128), bf16),
        ],
        compiler_params=pltpu.CompilerParams(vmem_limit_bytes=56 * 2**20),
        cost_estimate=pl.CostEstimate(
            flops=4 * 256 * 1536 * (3584 + 1536), bytes_accessed=40 * 2**20, transcendentals=2**21
        ),
        name="mixer_backward",
    )(dm, kappa, w_out, w_in, normed, ffn_in, drout, proj, y, scaled, cx, cbc, hp, marks, seg)


def swap(v):
    return lax.ppermute(v, "seq", [(0, 1), (1, 0)])


def both_halves(own, other, s):
    first = jnp.where(s == 0, own, other)
    second = jnp.where(s == 0, other, own)
    return jnp.concatenate([first, second], axis=0)


def halves(v, s):
    rows = v.shape[0] // 2
    return (
        lax.dynamic_slice_in_dim(v, s * rows, rows, 0),
        lax.dynamic_slice_in_dim(v, (1 - s) * rows, rows, 0),
    )


def hi_lo(v):
    hi = v.astype(bf16)
    return hi, (v - hi.astype(f32)).astype(bf16)


def rms(v):
    return lax.rsqrt(jnp.mean(v * v, axis=-1, keepdims=True) + EPS)


def silu_grad(v):
    sig = jax.nn.sigmoid(v)
    return sig * (1.0 + v * (1.0 - sig))


def local(
    tokens,
    out_grad,
    lengths,
    routes,
    in_norm,
    in_proj,
    conv_weight,
    conv_bias,
    head_params,
    mixer_norm,
    out_proj,
    ffn_norm,
    router,
    shared_gate_up,
    shared_down,
    expert_gate_up,
    expert_down,
):
    s = lax.axis_index("seq")
    dp = lax.axis_index(DP)
    experts, slots = 64, 24
    n_slots = experts * slots

    other_tokens = swap(tokens)
    other_grad = swap(out_grad)
    other_gate_up = swap(expert_gate_up[0])
    other_down = swap(expert_down[0])
    w_in, w_sgu, w_out, w_sdown, vecs = gather(
        in_proj,
        shared_gate_up,
        router,
        jnp.concatenate([out_proj, shared_down], axis=0),
        (in_norm[None], ffn_norm[None], mixer_norm[None], conv_weight.T, conv_bias[None]),
    )
    w_in = w_in.reshape(4, 1536, 896)
    w_sgu = w_sgu.reshape(4, 1536, 256)
    w_out = w_out.reshape(4, 1536, 384)
    w_sdown = w_sdown.reshape(4, 512, 384)

    vecs = vecs.reshape(128, 16, 128).astype(f32)
    g_in = vecs[:, 0, :12].reshape(1, 1536)
    g_ffn = vecs[:, 1, :12].reshape(1536)
    g_mix = lax.dynamic_slice_in_dim(vecs[:, 2, :24].reshape(1, 3072), s * 1536, 1536, 1)
    conv = vecs[:, 3:8, :26].transpose(1, 0, 2).reshape(5, 3328)
    heads = lax.dynamic_slice_in_dim(head_params.astype(f32), s * 24, 24, 1)
    cx = jnp.concatenate(
        [
            lax.dynamic_slice_in_dim(conv[:, :3072], s * 1536, 1536, 1),
            jnp.broadcast_to(heads[2][:, None], (24, 64)).reshape(1, 1536),
            g_mix,
            jnp.zeros((1, 1536), f32),
        ],
        axis=0,
    )
    cx = cx.reshape(8, 4, 384).transpose(1, 0, 2)
    cbc = jnp.pad(conv[:, 3072:], ((0, 3), (0, 0))).reshape(8, 2, 128).transpose(1, 0, 2)
    hp = jnp.stack([jnp.exp(heads[0]), heads[1]]).reshape(2, 4, 6).transpose(1, 0, 2)
    hp = jnp.pad(hp, ((0, 0), (0, 6), (HEAD_AT, 122 - HEAD_AT)))
    w_eg = both_halves(expert_gate_up[0], other_gate_up, s)
    w_ed = both_halves(expert_down[0], other_down, s)

    ids = jnp.arange(experts, dtype=jnp.int32)
    named = jnp.sum((routes[:, :, None] == ids).astype(f32), axis=1)
    t128 = jnp.arange(128)
    before = (t128[:, None] > t128[None, :]).astype(bf16)
    rank = dot(before, named.astype(bf16))
    slot = jnp.arange(n_slots, dtype=jnp.int32)
    spread = (slot[None, :] // slots == ids[:, None]).astype(bf16)
    is_named = dot(named.astype(bf16), spread) > 0.5
    in_slot = dot(rank.astype(bf16), spread) == (slot % slots).astype(f32)[None, :]
    place = (is_named & in_slot).astype(bf16)

    def to_slots(v):
        return dot(place, v, ((0,), (0,))).astype(bf16).reshape(experts, slots, v.shape[1])

    grad_slots, w_in = lax.optimization_barrier((to_slots(out_grad), w_in))
    grad_rows = lax.all_to_all(grad_slots, DP, 0, 0, tiled=True).reshape(n_slots, 1536)

    ends = jnp.cumsum(lengths[0])
    t256 = jnp.arange(256, dtype=jnp.int32)
    segment = jnp.sum((t256[:, None] >= ends[None, :]).astype(jnp.int32), axis=1)
    seg = segment.astype(f32)
    same = [
        (jnp.pad(segment, (d, 0), constant_values=-1)[:256] == segment).astype(f32)
        for d in range(4)
    ]
    marks = jnp.pad(jnp.stack(same + [seg], axis=1), ((0, 0), (0, 123)))
    seg = jnp.broadcast_to(seg, (8, 256))
    x_full = both_halves(tokens, other_tokens, s)
    normed, proj, y, scaled, part, squares = mixer_forward(
        x_full, jnp.broadcast_to(g_in, (8, 1536)), w_in, w_out, cx, cbc, hp, marks, seg
    )
    squares = squares[:, :1]
    part_own, part_other = halves(part, s)
    sq_own, sq_other = halves(squares, s)
    part = part_own + swap(part_other)
    q = lax.rsqrt((sq_own + swap(sq_other)) / 3072.0 + EPS)
    residual = tokens.astype(f32) + q * part

    r = rms(residual)
    ffn_in = (residual * r * g_ffn).astype(bf16)
    w_router = w_in[:, :, 832:848].transpose(1, 0, 2).reshape(1536, 64)
    logits = dot(ffn_in, w_router)
    logits = jnp.where(named > 0.5, logits, -1e30)
    top = jnp.max(logits, axis=1, keepdims=True)
    weights = jnp.where(named > 0.5, jnp.exp(logits - top), 0.0)
    gating = weights / jnp.sum(weights, axis=1, keepdims=True)
    gate_hi, gate_lo = hi_lo(gating)
    sent = to_slots(jnp.concatenate([ffn_in, gate_hi, gate_lo], axis=1))
    sent, grad_rows = lax.optimization_barrier((sent, grad_rows))
    arrived = lax.all_to_all(sent, DP, 0, 0, tiled=True).reshape(n_slots, 1664)

    ffn_full = both_halves(ffn_in, swap(ffn_in), s)
    og_full = both_halves(out_grad, other_grad, s)
    sgu = jnp.stack([dot(ffn_full, w_sgu[j]) for j in range(4)])
    sg, su = sgu[..., :128], sgu[..., 128:]
    s_act = (jax.nn.silu(sg) * su).astype(bf16)
    s_flat = s_act.transpose(1, 0, 2).reshape(256, 512)
    s_out = jnp.concatenate([dot(s_flat, w_sdown[j]) for j in range(4)], axis=1)
    s_own, s_other = halves(s_out, s)
    s_out = s_own + swap(s_other.astype(bf16)).astype(f32)
    og_cols = og_full.reshape(256, 4, 384).transpose(1, 0, 2)
    d_s_act = sum(dot(og_cols[j], w_sdown[j], ((1,), (1,))) for j in range(4))
    d_s_act = d_s_act.reshape(256, 4, 128).transpose(1, 0, 2)
    d_sgu = jnp.concatenate([d_s_act * su * silu_grad(sg), d_s_act * jax.nn.silu(sg)], axis=-1)
    d_sgu = d_sgu.astype(bf16)
    grad_sdown = jnp.stack([dot(s_flat, og_cols[j], ((0,), (0,))) for j in range(4)]).astype(bf16)
    grad_sgu = jnp.stack([dot(ffn_full, d_sgu[j], ((0,), (0,))) for j in range(4)]).astype(bf16)
    d_ffn = sum(dot(d_sgu[j], w_sgu[j], ((1,), (1,))) for j in range(4))
    df_own, df_other = halves(d_ffn, s)
    d_ffn = df_own + swap(df_other.astype(bf16)).astype(f32)

    lane = jnp.arange(128, dtype=jnp.int32) % 64
    pick = (lane == dp).astype(f32)[None, :]
    d_rows, e_act, w_act, w_gu = expert_grads(arrived, grad_rows, w_eg, w_ed, pick)
    d_back = lax.all_to_all(d_rows.reshape(experts, slots, 1664), DP, 0, 0, tiled=True)
    e_out = dot(e_act, w_ed).astype(bf16)
    grad_ed = dot(w_act, grad_rows, ((0,), (0,)))
    grad_eg = dot(arrived[:, :1536], w_gu, ((0,), (0,)))
    ge_own, ge_other = halves(grad_eg, s)
    grad_eg = ge_own + swap(ge_other.astype(bf16)).astype(f32)
    gd_own, gd_other = halves(grad_ed, s)
    grad_ed = gd_own + swap(gd_other.astype(bf16)).astype(f32)
    e_out, d_back, grad_eg, grad_ed, d_ffn = lax.optimization_barrier(
        (e_out, d_back, grad_eg, grad_ed, d_ffn)
    )
    d_back = d_back.reshape(n_slots, 1664)
    out_back = lax.all_to_all(e_out.reshape(experts, slots, 1536), DP, 0, 0, tiled=True)
    out_back = out_back.reshape(n_slots, 1536)

    wide_gate = dot(gate_hi, spread) + dot(gate_lo, spread)
    weighted = (place.astype(f32) * wide_gate).astype(bf16)
    d_route = dot(weighted, d_back[:, :1536])
    dg = d_back[:, 1536:1538].T
    d_gating = dot(place * dg[0:1], spread, ((1,), (1,))) + dot(
        place * dg[1:2], spread, ((1,), (1,))
    )
    d_logits = gating * (d_gating - jnp.sum(gating * d_gating, axis=1, keepdims=True))
    d_logits_low = d_logits.astype(bf16)
    d_ffn = d_ffn + dot(d_logits_low, w_router, ((1,), (1,))) + d_route
    ffn_norm_grad = jnp.sum(d_ffn * residual * r, axis=0)
    u = d_ffn * g_ffn
    d_residual = (
        out_grad.astype(f32)
        + r * u
        - r * r * r * residual * jnp.mean(u * residual, axis=1, keepdims=True)
    )

    d_mixed = (q * d_residual).astype(bf16)
    kappa = q * q / 3072.0 * jnp.sum(d_mixed.astype(f32) * part, axis=1, keepdims=True)
    d_mixed_full = both_halves(d_mixed, swap(d_mixed), s)
    kappa = both_halves(kappa, swap(kappa), s)
    drout = jnp.pad(d_logits_low.reshape(128, 4, 16).transpose(1, 0, 2), ((0, 0), (0, 0), (64, 48)))
    grad_out, grad_in, d_normed, g_cx, g_cbc, g_heads = mixer_backward(
        d_mixed_full, kappa, w_out, w_in, normed, ffn_in, drout, proj, y, scaled, cx, cbc, hp, marks, seg
    )
    conv_x_grad = g_cx[:, :5].transpose(1, 0, 2).reshape(5, 1536)
    conv_bc_grad = g_cbc[:, :5].transpose(1, 0, 2).reshape(5, 256)
    mixer_norm_grad = g_cx[:, 6].reshape(1536)
    head_grad = g_heads[:, :2, HEAD_AT : HEAD_AT + 6].transpose(1, 0, 2).reshape(2, 24)
    d_skip = jnp.sum(g_cx[:, 5].reshape(24, 64), axis=1)
    head_grad = jnp.concatenate([head_grad, d_skip[None]], axis=0)
    dn_own, dn_other = halves(d_normed, s)
    d_normed = dn_own + swap(dn_other.astype(bf16)).astype(f32)
    x_own = tokens.astype(f32)
    p = rms(x_own)
    in_norm_grad = jnp.sum(d_normed * x_own * p, axis=0)
    v = d_normed * g_in
    token_grad = (
        d_residual + p * v - p * p * p * x_own * jnp.mean(v * x_own, axis=1, keepdims=True)
    ).astype(bf16)

    conv_grad = lax.dynamic_update_slice(
        jnp.zeros((5, 3328), f32), conv_x_grad, (0, s * 1536)
    )
    conv_grad = lax.dynamic_update_slice(conv_grad, conv_bc_grad, (0, 3072))
    mixer_norm_grad = lax.dynamic_update_slice(
        jnp.zeros((128, 24), f32), mixer_norm_grad.reshape(64, 24), (s * 64, 0)
    )
    head_grad = lax.dynamic_update_slice(jnp.zeros((3, 48), f32), head_grad, (0, s * 24))
    def rows_of(v, width):
        return jnp.pad(v.reshape(128, 1, width), ((0, 0), (0, 0), (0, 64 - width)))

    conv_grad = conv_grad.reshape(5, 128, 26).transpose(1, 0, 2)
    small = jnp.concatenate(
        [
            rows_of(in_norm_grad, 12),
            rows_of(ffn_norm_grad, 12),
            rows_of(mixer_norm_grad, 24),
            jnp.pad(conv_grad, ((0, 0), (0, 0), (0, 38))),
        ],
        axis=1,
    )
    head_rows = jnp.broadcast_to(jnp.pad(head_grad, ((0, 5), (0, 16)))[None], (128, 8, 64))
    small = jnp.concatenate([small, head_rows], axis=2).reshape(2, 4, 4, 4, 8, 128)
    weighted_late, grad_in = lax.optimization_barrier((weighted, grad_in))
    routed = dot(weighted_late, out_back)
    block_out = (residual + s_out + routed).astype(bf16)
    block_out, small = lax.optimization_barrier((block_out, small))
    sums = scatter(
        (
            grad_in.reshape(4, 2, 4, 4, 48, 896),
            grad_sgu.reshape(4, 2, 4, 4, 48, 256),
            grad_out.reshape(4, 4, 4, 2, 48, 384),
            grad_sdown.reshape(4, 4, 4, 2, 16, 384),
            small,
        )
    )
    (
        in_proj_grad, router_grad, sgu_grad, out_proj_grad, sdown_grad, head_grad, conv_grad,
        in_norm_grad, ffn_norm_grad, mixer_norm_grad, conv_bias_grad,
    ) = finish(*sums)
    return (
        block_out,
        token_grad,
        in_norm_grad[0],
        in_proj_grad,
        conv_grad,
        conv_bias_grad[0],
        head_grad,
        mixer_norm_grad[0],
        out_proj_grad,
        ffn_norm_grad[0],
        router_grad,
        sgu_grad,
        sdown_grad,
        grad_eg[None],
        grad_ed[None],
    )


def solution(mesh):
    finer = Mesh(mesh.devices.reshape(2, 4, 4, 4), ALL)
    placed = (
        P(DP_SEQ, None),
        P(DP_SEQ, None),
        P(DP, None),
        P(DP_SEQ, None),
        P(ALL),
        P(ALL, None),
        P(ALL, None),
        P(ALL),
        P(),
        P(ALL),
        P(ALL, None),
        P(ALL),
        P(ALL, None),
        P(ALL, None),
        P(ALL, None),
        P(DP, "seq", None),
        P(DP, "seq", None),
    )
    return jax.shard_map(
        local,
        mesh=finer,
        in_specs=placed,
        out_specs=(
            P(DP_SEQ, None),
            P(DP_SEQ, None),
            P(ALL),
            P(ALL, None),
            P(ALL, None),
            P(ALL),
            P(),
            P(ALL),
            P(ALL, None),
            P(ALL),
            P(ALL, None),
            P(ALL, None),
            P(ALL, None),
            P(DP, "seq", None),
            P(DP, "seq", None),
        ),
        check_vma=False,
    )
```

```python
import functools

import jax
import jax.numpy as jnp
import numpy as np
from jax import lax
from jax.experimental import pallas as pl
from jax.experimental.pallas import tpu as pltpu
from jax.sharding import Mesh
from jax.sharding import PartitionSpec as P

DP = ("z", "x", "y")
ALL = ("seq", "z", "x", "y")
DP_SEQ = ("z", "x", "y", "seq")
ORDER = (("z", "x", "y"), ("x", "y", "z"), ("y", "z", "x"))
REM = (("z", "x"), ("y", "x"), ("y", "z"))
MESH_ID = pl.DeviceIdType.MESH
EPS = 1e-05
f32 = jnp.float32
bf16 = jnp.bfloat16

ROWS_FIRST = (("y", "s", "z", "x"), "rows")
CHANNELS = (("y", "z", "x", "s"), "cols")
VECTORS = (("s", "z", "x", "y"), "one")
SPECS = (ROWS_FIRST, ROWS_FIRST, CHANNELS, CHANNELS, VECTORS)
HEAD_AT = 80
SIZES = {"y": 4, "z": 4, "x": 4, "s": 2}


def dot(a, b, dims=((1,), (0,))):
    return lax.dot_general(a, b, (dims, ((), ())), preferred_element_type=f32)


def neighbours():
    pos = {a: lax.axis_index(a) for a in DP}
    right = {a: lax.rem(pos[a] + 1, 4) for a in DP}
    left = {a: lax.rem(pos[a] + 3, 4) for a in DP}
    opp = {a: lax.rem(pos[a] + 2, 4) for a in DP}
    return pos, right, left, opp


def chip_row():
    core, y = lax.axis_index("seq"), lax.axis_index("y")
    return [(lax.rem(core + c, 2), lax.rem(y + d, 4)) for c in range(2) for d in range(4)]


def greet(right, left, opp):
    barrier = pltpu.get_barrier_semaphore()

    def signal(device_id):
        pl.semaphore_signal(barrier, inc=1, device_id=device_id, device_id_type=MESH_ID)

    for a in ("z", "x"):
        signal({a: right[a]})
        signal({a: left[a]})
        signal({a: opp[a]})
    for core, y in chip_row()[1:]:
        signal({"seq": core, "y": y})


def met(count):
    pl.semaphore_wait(pltpu.get_barrier_semaphore(), count)


def cuts(spec):
    return range(1 if spec[1] == "one" else 3)


def third(shape, split, a):
    rows, cols = shape[-2:]
    if split == "one":
        return (slice(None), slice(None))
    if split == "rows":
        return (pl.ds(rows // 3 * a, rows // 3), slice(None))
    return (slice(None), pl.ds(cols // 3 * a, cols // 3))


def third_shape(shape, split):
    rows, cols = shape[-2:]
    return {"one": (rows, cols), "rows": (rows // 3, cols), "cols": (rows, cols // 3)}[split]


def region(ref, spec, free, fixed, a, s=None):
    order, split = spec
    ix = []
    for d in order:
        if d == "s":
            ix.append(slice(None) if s is None else s)
        else:
            ix.append(slice(None) if d in free else fixed[d])
    return ref.at[tuple(ix) + third(ref.shape, split, a)]


def roll(v, by, axis):
    by = by % v.shape[axis]
    return pltpu.roll(v, by, axis) if by else v


def lanes(shape):
    return lax.broadcasted_iota(jnp.int32, shape, len(shape) - 1)


def moved(v, at, to, width):
    lane = lanes(v.shape)
    return jnp.where((lane >= to) & (lane < to + width), roll(v, to - at, 1), 0.0)


def gather_kernel(in_ref, gu_ref, router_ref, rows_ref, *refs):
    specs, n = SPECS, len(SPECS)
    vec_refs, outs, blocks = refs[:5], refs[5 : 5 + n], refs[5 + n : 5 + 2 * n]
    pin, pout, bin_, bout, wide, vec, send0, recv0, send, recv, loc = refs[5 + 2 * n :]
    pos, right, left, opp = neighbours()
    row = chip_row()
    (core, y) = row[0]
    greet(right, left, opp)
    wide[...] = jnp.zeros_like(wide)
    wide[0, :12, :48] = in_ref[:, 6400:].astype(f32)
    wide[1, :12, :64] = router_ref[...].astype(f32)
    at = 0
    for v in vec_refs:
        wide[2, at : at + v.shape[0], : v.shape[1]] = v[...].astype(f32)
        at += v.shape[0]
    vec[...] = wide[2].astype(bf16)
    bc = [in_ref[:, 6144 + 128 * k : 6272 + 128 * k].astype(f32) for k in range(2)]
    steps, router = wide[0, :12], wide[1, :12]
    for c in range(2):
        for j in range(4):
            k, at = 4 * c + j, c * 1536 + j * 384
            misc = (
                moved(bc[j // 2], 64 * (j % 2), 0, 64)
                + moved(router, 16 * j, 64, 16)
                + moved(steps, 24 * c + 6 * j, HEAD_AT, 6)
            )
            pin[k, :12, :384] = in_ref[:, at : at + 384]
            pin[k, :12, 384:768] = in_ref[:, 3072 + at : 3456 + at]
            pin[k, :12, 768:896] = misc.astype(bf16)
            pin[k, :12, 896:1024] = gu_ref[:, 128 * k : 128 * k + 128]
            pin[k, :12, 1024:] = gu_ref[:, 1024 + 128 * k : 1152 + 128 * k]
    for j in range(4):
        pout[j] = rows_ref[:, 384 * j : 384 * j + 384]
    met(13)
    sends, first = [], []

    def push(src, dst, k, device_id):
        c = pltpu.make_async_remote_copy(
            src_ref=src,
            dst_ref=dst,
            send_sem=send0.at[k],
            recv_sem=recv0.at[k],
            device_id=device_id,
            device_id_type=MESH_ID,
        )
        c.start()
        sends.append(c)
        first.append(c)

    for k, (c, d) in enumerate(row):
        if k:
            push(pin.at[4 * c + d], bin_.at[4 * core + y], k, {"seq": c, "y": d})
    for k, (_, d) in enumerate(row[:4]):
        if k:
            push(pout.at[d], bout.at[y], 8 + k, {"y": d})
    push(vec, blocks[4].at[core], 0, {"seq": 1 - core})
    blocks[4][core] = vec[...]
    bin_[4 * core + y] = pin[4 * core + y]
    bout[y] = pout[y]
    for c in first:
        c.wait_recv()
    for c in range(2):
        v = jnp.concatenate([bin_[4 * c + d].astype(f32)[:12] for d in range(4)], axis=0)
        blocks[0][c] = v[:, :896].astype(bf16)
        blocks[1][c] = v[:, 896:].astype(bf16)
    v = [bout[d].astype(f32) for d in range(4)]
    for h in range(2):
        blocks[2][h] = jnp.concatenate([v[2 * h][:24], v[2 * h + 1][:24]], axis=0).astype(bf16)
        blocks[3][h] = jnp.concatenate([v[2 * h][24:], v[2 * h + 1][24:]], axis=0).astype(bf16)

    own = []
    for i in range(n):
        ix = tuple(slice(None) if d == "s" else pos[d] for d in specs[i][0])
        c = pltpu.make_async_copy(blocks[i], outs[i].at[ix], loc.at[i])
        c.start()
        own.append(c)

    def remote(i, st, a, k, src, dst, ax, to):
        c = pltpu.make_async_remote_copy(
            src_ref=src,
            dst_ref=dst,
            send_sem=send.at[i, st, a, k],
            recv_sem=recv.at[i, st, a, k],
            device_id={ax: to},
            device_id_type=MESH_ID,
        )
        c.start()
        sends.append(c)
        return c

    every = [(i, a) for i in range(n) for a in cuts(specs[i])]
    first, later = {}, {}

    def begin(i, a, st):
        ax, free = ORDER[a][st], ORDER[a][:st]
        dst = region(outs[i], specs[i], free, pos, a)
        src = dst
        if st == 0:
            src = blocks[i].at[(slice(None),) + third(blocks[i].shape, specs[i][1], a)]
        for d, to in enumerate((right[ax], left[ax])):
            first[i, a, d] = remote(i, st, a, d, src, dst, ax, to)
        if st == 0:
            later[i, a, 0] = remote(i, st, a, 2, src, dst, ax, opp[ax])

    for i, a in every:
        begin(i, a, 0)
    for c in own:
        c.wait()
    for st in range(3):
        for i, a in every:
            ax, free = ORDER[a][st], ORDER[a][:st]
            for d, (to, frm) in enumerate(((right[ax], left[ax]), (left[ax], right[ax]))):
                first[i, a, d].wait_recv()
                if st:
                    r = region(outs[i], specs[i], free, {**pos, ax: frm}, a, s=d)
                    later[i, a, d] = remote(i, st, a, 2 + d, r, r, ax, to)
        for i, a in every:
            for d in range(2 if st else 1):
                later[i, a, d].wait_recv()
            if st < 2:
                begin(i, a, st + 1)
    for c in sends:
        c.wait_send()


def gather(in_proj, gate_up, router, rows, vectors):
    n = len(SPECS)
    blocks = [(2, 48, 896), (2, 48, 256), (2, 48, 384), (2, 16, 384), (2, 16, 128)]
    outs = [
        jax.ShapeDtypeStruct(tuple(SIZES[d] for d in spec[0]) + v[1:], bf16)
        for v, spec in zip(blocks, SPECS)
    ]
    total = sum(int(np.prod(o.shape)) for o in outs) * 2
    return pl.pallas_call(
        gather_kernel,
        out_shape=outs,
        in_specs=[pl.BlockSpec(memory_space=pltpu.VMEM)] * 9,
        out_specs=[pl.BlockSpec(memory_space=pl.ANY)] * n,
        scratch_shapes=[pltpu.VMEM(v, bf16) for v in blocks]
        + [
            pltpu.VMEM((8, 16, 1152), bf16),
            pltpu.VMEM((4, 32, 384), bf16),
            pltpu.VMEM((8, 16, 1152), bf16),
            pltpu.VMEM((4, 32, 384), bf16),
            pltpu.VMEM((3, 16, 128), f32),
            pltpu.VMEM((16, 128), bf16),
            pltpu.SemaphoreType.DMA((12,)),
            pltpu.SemaphoreType.DMA((12,)),
            pltpu.SemaphoreType.DMA((n, 3, 3, 4)),
            pltpu.SemaphoreType.DMA((n, 3, 3, 4)),
            pltpu.SemaphoreType.DMA((n,)),
        ],
        compiler_params=pltpu.CompilerParams(
            collective_id=1, has_side_effects=True, vmem_limit_bytes=60 * 2**20
        ),
        cost_estimate=pl.CostEstimate(flops=0, bytes_accessed=2 * total, transcendentals=0),
        name="gather_weights",
    )(in_proj, gate_up, router, rows, *vectors)


def each(lead, fn):
    @pl.loop(0, int(np.prod(lead)))
    def _(i):
        ix = []
        for d in reversed(lead):
            ix.append(lax.rem(i, d))
            i = lax.div(i, d)
        fn(tuple(reversed(ix)))


def scatter_kernel(*refs):
    specs, n = SPECS, len(SPECS)
    gs, (bin_, bout, small_out) = refs[:n], refs[n : n + 3]
    outs, refs = refs[n + 3 : 2 * n + 3], refs[2 * n + 3 :]
    held, got = refs[:n], [refs[n + 3 * i : n + 3 * i + 3] for i in range(n)]
    pin, pout, other, send0, recv0, send, recv, loc = refs[4 * n :]
    pos, right, left, opp = neighbours()
    row = chip_row()
    (core, y) = row[0]

    def source(i, st, a, idx, s):
        ax = ORDER[a][2 - st]
        if st == 0:
            return region(gs[i], specs[i], [d for d in DP if d != ax], {ax: idx}, a, s)
        part = held[i].at[a, 2 + s]
        if st == 1:
            return part.at[:, idx] if REM[a][1] == ax else part.at[idx]
        me = pos[ORDER[a][1]]
        return part.at[me, idx] if REM[a][1] == ax else part.at[idx, me]

    local = {}
    for i in range(n):
        for a in cuts(specs[i]):
            ax = ORDER[a][2]
            for k, (idx, s) in enumerate(((right[ax], 0), (left[ax], 1), (pos[ax], 0), (pos[ax], 1))):
                c = pltpu.make_async_copy(source(i, 0, a, idx, s), held[i].at[a, k], loc.at[i, a, k])
                c.start()
                local[i, a, k] = c
    greet(right, left, opp)
    met(13)
    sends = []

    def remote(i, st, a, k, src, ax, to):
        c = pltpu.make_async_remote_copy(
            src_ref=src,
            dst_ref=got[i][st].at[a, k],
            send_sem=send.at[i, st, a, k],
            recv_sem=recv.at[i, st, a, k],
            device_id={ax: to},
            device_id_type=MESH_ID,
        )
        c.start()
        sends.append(c)
        return c

    every = [(i, a) for i in range(n) for a in cuts(specs[i])]
    cp = {}

    def begin(i, a, st):
        ax = ORDER[a][2 - st]
        if st == 2:
            for k, to in enumerate((opp[ax], right[ax], left[ax])):
                for s in range(2):
                    cp[i, a, 2 * k + s] = remote(i, st, a, 2 * k + s, source(i, st, a, to, s), ax, to)
            return
        cp[i, a, 0] = remote(i, st, a, 0, source(i, st, a, opp[ax], 0), ax, right[ax])
        cp[i, a, 1] = remote(i, st, a, 1, source(i, st, a, opp[ax], 1), ax, left[ax])
        cp[i, a, 2] = remote(i, st, a, 2, source(i, st, a, right[ax], 1), ax, right[ax])
        cp[i, a, 3] = remote(i, st, a, 3, source(i, st, a, left[ax], 0), ax, left[ax])

    for i, a in every:
        begin(i, a, 0)
    for st in range(2):
        lead = ((4, 4), (4,))[st]
        for i, a in every:
            ax = ORDER[a][2 - st]
            for d, to in enumerate((right[ax], left[ax])):
                cp[i, a, d].wait_recv()
                if st == 0:
                    local[i, a, d].wait()
                    acc = held[i].at[a, d]
                else:
                    acc = source(i, st, a, to, d)
                more = got[i][st].at[a, d]

                def add(ix, acc=acc, more=more):
                    acc[ix] = (acc[ix].astype(f32) + more[ix].astype(f32)).astype(acc.dtype)

                each(lead, add)
                cp[i, a, 4 + d] = remote(i, st, a, 4 + d, acc, ax, to)
        for i, a in every:
            ax = ORDER[a][2 - st]
            if st == 0:
                local[i, a, 2].wait()
                local[i, a, 3].wait()
            for s, (p, q) in enumerate(((4, 3), (2, 5))):
                cp[i, a, p].wait_recv()
                cp[i, a, q].wait_recv()
                acc = held[i].at[a, 2 + s] if st == 0 else source(i, st, a, pos[ax], s)
                one, two = got[i][st].at[a, p], got[i][st].at[a, q]

                def close(ix, acc=acc, one=one, two=two):
                    total = acc[ix].astype(f32) + one[ix].astype(f32) + two[ix].astype(f32)
                    acc[ix] = total.astype(acc.dtype)

                each(lead, close)
            begin(i, a, st + 1)
    for i, a in every:
        ax = ORDER[a][0]
        for s in range(2):
            total = source(i, 2, a, pos[ax], s)[...].astype(f32)
            for k in range(3):
                cp[i, a, 2 * k + s].wait_recv()
                total = total + got[i][2][a, 2 * k + s].astype(f32)
            outs[i][(s,) + third(outs[i].shape, specs[i][1], a)] = total

    for k in range(8):
        c, d = divmod(k, 4)
        pin[k, :12, :896] = outs[0][c, 12 * d : 12 * d + 12, :]
        pin[k, :12, 896:] = outs[1][c, 12 * d : 12 * d + 12, :]
    for d in range(4):
        h, at = divmod(d, 2)
        pout[d, :24] = outs[2][h, 24 * at : 24 * at + 24, :]
        pout[d, 24:] = outs[3][h, 8 * at : 8 * at + 8, :]
    last = []

    def push(src, dst, k, device_id):
        c = pltpu.make_async_remote_copy(
            src_ref=src,
            dst_ref=dst,
            send_sem=send0.at[k],
            recv_sem=recv0.at[k],
            device_id=device_id,
            device_id_type=MESH_ID,
        )
        c.start()
        sends.append(c)
        last.append(c)

    for k, (c, d) in enumerate(row):
        if k:
            push(pin.at[4 * c + d], bin_.at[4 * core + y], k, {"seq": c, "y": d})
    for k, (_, d) in enumerate(row[:4]):
        if k:
            push(pout.at[d], bout.at[y], 8 + k, {"y": d})
    push(outs[4].at[1 - core], other, 0, {"seq": 1 - core})
    bin_[4 * core + y] = pin[4 * core + y]
    bout[y] = pout[y]
    for c in last:
        c.wait_recv()
    small_out[...] = outs[4][core] + other[...]
    for c in sends:
        c.wait_send()


def finish_kernel(bin_, bout, small, in_out, router_out, gu_out, out_out, down_out, heads_out, taps_out, *vecs):
    misc = []
    for k in range(8):
        got_k = bin_[k]
        in_out[:, 384 * k : 384 * k + 384] = got_k[:12, :384]
        in_out[:, 3072 + 384 * k : 3456 + 384 * k] = got_k[:12, 384:768]
        gu_out[:, 128 * k : 128 * k + 128] = got_k[:12, 896:1024]
        gu_out[:, 1024 + 128 * k : 1152 + 128 * k] = got_k[:12, 1024:]
        misc.append(got_k[:, 768:896])
    both = [misc[j] + misc[4 + j] for j in range(4)]
    for h in range(2):
        pair = moved(both[2 * h], 0, 0, 64) + moved(both[2 * h + 1], 0, 64, 64)
        in_out[:, 6144 + 128 * h : 6272 + 128 * h] = pair[:12]
    steps = sum(moved(misc[k], HEAD_AT, 6 * k, 6) for k in range(8))
    in_out[:, 6400:] = steps[:12, :48]
    router = sum(moved(both[j], 64, 16 * j, 16) for j in range(4))
    router_out[...] = router[:12, :64]
    for j in range(4):
        out_out[:, 384 * j : 384 * j + 384] = bout[j, :24]
        down_out[:, 384 * j : 384 * j + 384] = bout[j, 24:]
    heads_out[...] = moved(small[...], 64, 0, 48)[:3, :48]
    taps_out[...] = jnp.concatenate([small[...]] * 16, axis=0).T[:26, 3:7]
    for v, at in zip(vecs, (0, 1, 2, 7)):
        v[...] = small[at : at + 1, : v.shape[1]]


def finish(bin_, bout, small):
    results = [(12, 6448), (12, 64), (12, 2048), (24, 1536), (8, 1536), (3, 48), (26, 4)]
    results += [(1, 12), (1, 12), (1, 24), (1, 26)]
    return pl.pallas_call(
        finish_kernel,
        out_shape=[jax.ShapeDtypeStruct(v, f32) for v in results],
        in_specs=[pl.BlockSpec(memory_space=pltpu.VMEM)] * 3,
        out_specs=[pl.BlockSpec(memory_space=pltpu.VMEM)] * len(results),
        name="finish_grads",
    )(bin_, bout, small)


def scatter(arrays):
    n = len(arrays)
    results = [(8, 16, 1152), (4, 32, 384), (8, 128)]
    pieces = [(third_shape(v.shape, spec[1]), v.dtype) for v, spec in zip(arrays, SPECS)]
    cut = [len(cuts(spec)) for spec in SPECS]
    return pl.pallas_call(
        scatter_kernel,
        out_shape=[jax.ShapeDtypeStruct(v, f32) for v in results],
        in_specs=[pl.BlockSpec(memory_space=pl.ANY)] * n,
        out_specs=[pl.BlockSpec(memory_space=pltpu.VMEM)] * len(results),
        scratch_shapes=[pltpu.VMEM((2,) + v.shape[4:], f32) for v in arrays]
        + [pltpu.VMEM((k, 4, 4, 4) + p, t) for k, (p, t) in zip(cut, pieces)]
        + [
            pltpu.VMEM((k, 6) + lead + p, t)
            for k, (p, t) in zip(cut, pieces)
            for lead in ((4, 4), (4,), ())
        ]
        + [
            pltpu.VMEM((8, 16, 1152), f32),
            pltpu.VMEM((4, 32, 384), f32),
            pltpu.VMEM((8, 128), f32),
            pltpu.SemaphoreType.DMA((12,)),
            pltpu.SemaphoreType.DMA((12,)),
            pltpu.SemaphoreType.DMA((n, 3, 3, 6)),
            pltpu.SemaphoreType.DMA((n, 3, 3, 6)),
            pltpu.SemaphoreType.DMA((n, 3, 4)),
        ],
        compiler_params=pltpu.CompilerParams(
            collective_id=2, has_side_effects=True, vmem_limit_bytes=56 * 2**20
        ),
        cost_estimate=pl.CostEstimate(flops=0, bytes_accessed=0, transcendentals=0),
        name="scatter_grads",
    )(*arrays)


def expert_kernel(rows_ref, grad_ref, gu_ref, down_ref, pick_ref, back_ref, act_ref, wact_ref, wgu_ref):
    for at in range(0, rows_ref.shape[0], 256):
        part = pl.ds(at, 256)
        e_gu = dot(rows_ref[part, :1536], gu_ref[...])
        d_act = dot(grad_ref[part, :], down_ref[...], ((1,), (1,)))
        eg, eu = e_gu[:, :512], e_gu[:, 512:]
        sig = jax.nn.sigmoid(eg)
        silu = eg * sig
        act32 = silu * eu
        act = act32.astype(bf16)
        slot_gate = jnp.sum(rows_ref[part, 1536:].astype(f32) * pick_ref[...], axis=1, keepdims=True)
        d_gate = jnp.sum(act.astype(f32) * d_act, axis=1, keepdims=True)
        d_eg = d_act * eu * (sig + silu * (1.0 - sig))
        d_eu = d_act * silu
        d_gu = jnp.concatenate([d_eg.astype(bf16), d_eu.astype(bf16)], axis=1)
        back_ref[part, :1536] = dot(d_gu, gu_ref[...], ((1,), (1,))).astype(bf16)
        hi = d_gate.astype(bf16).astype(f32)
        lane = lanes((256, 128))
        tail = jnp.where(lane == 0, hi, jnp.where(lane == 1, d_gate - hi, 0.0))
        back_ref[part, 1536:] = tail.astype(bf16)
        act_ref[part, :] = act
        wact_ref[part, :] = (act32 * slot_gate).astype(bf16)
        wgu_ref[part, :512] = (d_eg * slot_gate).astype(bf16)
        wgu_ref[part, 512:] = (d_eu * slot_gate).astype(bf16)


def expert_grads(rows, grad_rows, gate_up, down, pick):
    n, block = rows.shape[0], 512
    widths = (1664, 512, 512, 1024)

    def blocked(w):
        return pl.BlockSpec((block, w), lambda i: (i, 0))

    def whole(v):
        return pl.BlockSpec(v.shape, lambda i: (0, 0))

    return pl.pallas_call(
        expert_kernel,
        grid=(n // block,),
        out_shape=[jax.ShapeDtypeStruct((n, w), bf16) for w in widths],
        in_specs=[blocked(1664), blocked(1536), whole(gate_up), whole(down), whole(pick)],
        out_specs=[blocked(w) for w in widths],
        compiler_params=pltpu.CompilerParams(vmem_limit_bytes=48 * 2**20),
        cost_estimate=pl.CostEstimate(
            flops=2 * n * 1536 * (1024 + 512 + 1024), bytes_accessed=26 * 2**20, transcendentals=0
        ),
        name="expert_grads",
    )(rows, grad_rows, gate_up, down, pick)


def split3(v):
    hi = v.astype(bf16)
    rest = v - hi.astype(f32)
    mid = rest.astype(bf16)
    return hi, mid, (rest - mid.astype(f32)).astype(bf16)


def taps_pre(v, marks, w):
    total = w[4:5] + w[3:4] * v
    for d in (1, 2, 3):
        total = total + w[3 - d : 4 - d] * (roll(v, d, 0) * marks[:, d : d + 1])
    return total


def taps_back(d_pre, v, marks, w):
    d_v = w[3:4] * d_pre
    d_w = [jnp.sum(d_pre * v, axis=0, keepdims=True)]
    for d in (1, 2, 3):
        masked = d_pre * marks[:, d : d + 1]
        d_w.insert(0, jnp.sum(masked * roll(v, d, 0), axis=0, keepdims=True))
        d_v = d_v + w[3 - d : 4 - d] * roll(masked, 256 - d, 0)
    zero = jnp.zeros((3, v.shape[1]), f32)
    return d_v, jnp.concatenate(d_w + [jnp.sum(d_pre, axis=0, keepdims=True), zero], axis=0)


def joined(first, second):
    return jnp.where(lanes(first.shape) < 64, first, roll(second, 64, 1))


def bc_raw(proj_ref, k):
    return joined(
        proj_ref[2 * k, :, 768:896].astype(f32), proj_ref[2 * k + 1, :, 768:896].astype(f32)
    )


def head_steps(proj_ref, hp_ref, j, tri):
    raw = proj_ref[j, :, 768:896].astype(f32) + hp_ref[j, 1:2]
    step = jnp.maximum(raw, 0.0) + jnp.log1p(jnp.exp(-jnp.abs(raw)))
    rate = -step * hp_ref[j, 0:1]
    cum = sum(dot(tri, part) for part in split3(rate))
    return raw, step, rate, cum


def triangle():
    t = lax.broadcasted_iota(jnp.int32, (256, 256), 0)
    return t >= lanes((256, 256))


def pair_of(cols, p):
    at = HEAD_AT + 2 * p
    first = jnp.broadcast_to(cols[:, at : at + 1], (256, 128))
    return jnp.where(lanes((256, 128)) < 64, first, cols[:, at + 1 : at + 2])


def fade_of(cum, cum_rows, h, inside):
    at = HEAD_AT + h
    return jnp.exp(jnp.where(inside, cum[:, at : at + 1] - cum_rows[at : at + 1], -1e30))


def forward_kernel(
    x_ref, g_ref, w_in_ref, w_out_ref, cx_ref, cbc_ref, hp_ref, marks_ref, seg_ref,
    normed_ref, proj_ref, y_ref, scaled_ref, part_ref, squares_ref, scores_ref,
):
    i = pl.program_id(0)

    @pl.when(i == 0)
    def _():
        x = x_ref[...].astype(f32)
        normed_ref[...] = (x * rms(x) * g_ref[0:1]).astype(bf16)

    @pl.when(i < 4)
    def _():
        proj_ref[i] = dot(normed_ref[...], w_in_ref[0]).astype(bf16)

    @pl.when(i == 4)
    def _():
        marks = marks_ref[...]
        b_mat, c_mat = [jax.nn.silu(taps_pre(bc_raw(proj_ref, k), marks, cbc_ref[k])) for k in (0, 1)]
        scores_ref[...] = dot(c_mat.astype(bf16), b_mat.astype(bf16), ((1,), (1,)))
        part_ref[...] = jnp.zeros_like(part_ref)
        squares_ref[...] = jnp.zeros_like(squares_ref)

    @pl.when(i >= 4)
    def _():
        j = i - 4
        marks, cx = marks_ref[...], cx_ref[j]
        causal = triangle()
        inside = causal & (marks[:, 4:5] == seg_ref[0:1])
        _, step, _, cum = head_steps(proj_ref, hp_ref, j, causal.astype(bf16))
        cum_rows = cum.T
        x = jax.nn.silu(taps_pre(proj_ref[j, :, 384:768].astype(f32), marks, cx))
        scores = scores_ref[...]
        ys = []
        for p in range(3):
            xp = x[:, 128 * p : 128 * p + 128]
            xs = (xp * pair_of(step, p)).astype(bf16)
            y0, y1 = [
                dot((fade_of(cum, cum_rows, 2 * p + k, inside) * scores).astype(bf16), xs)
                for k in (0, 1)
            ]
            ys.append(jnp.where(lanes((256, 128)) < 64, y0, y1))
        y = jnp.concatenate(ys, axis=1) + cx[5:6] * x
        z = proj_ref[j, :, :384].astype(f32)
        gated = y * jax.nn.silu(z)
        scaled = (gated * cx[6:7]).astype(bf16)
        y_ref[j] = y
        scaled_ref[j] = scaled
        squares_ref[...] += jnp.broadcast_to(
            jnp.sum(gated * gated, axis=1, keepdims=True), squares_ref.shape
        )
        for c in range(4):
            part_ref[:, c * 384 : c * 384 + 384] += dot(scaled, w_out_ref[c])


def fixed(v):
    return pl.BlockSpec(v.shape, lambda i: (0,) * len(v.shape))


def mixer_forward(x, g, w_in, w_out, cx, cbc, hp, marks, seg):
    outs = [
        jax.ShapeDtypeStruct((256, 1536), bf16),
        jax.ShapeDtypeStruct((4, 256, 896), bf16),
        jax.ShapeDtypeStruct((4, 256, 384), f32),
        jax.ShapeDtypeStruct((4, 256, 384), bf16),
        jax.ShapeDtypeStruct((256, 1536), f32),
        jax.ShapeDtypeStruct((256, 128), f32),
    ]
    return pl.pallas_call(
        forward_kernel,
        grid=(8,),
        out_shape=outs,
        in_specs=[
            fixed(x),
            fixed(g),
            pl.BlockSpec((1, 1536, 896), lambda i: (jnp.minimum(i, 3), 0, 0)),
            pl.BlockSpec((4, 384, 384), lambda i: (0, jnp.maximum(i - 4, 0), 0)),
            *[fixed(v) for v in (cx, cbc, hp, marks, seg)],
        ],
        out_specs=[fixed(o) for o in outs],
        scratch_shapes=[pltpu.VMEM((256, 256), f32)],
        compiler_params=pltpu.CompilerParams(vmem_limit_bytes=48 * 2**20),
        cost_estimate=pl.CostEstimate(
            flops=2 * 256 * 1536 * (3584 + 1536), bytes_accessed=22 * 2**20, transcendentals=2**21
        ),
        name="mixer_forward",
    )(x, g, w_in, w_out, cx, cbc, hp, marks, seg)


def backward_kernel(
    dm_ref, kappa_ref, w_out_ref, w_in_ref, normed_ref, ffn_ref, drout_ref, proj_ref, y_ref,
    scaled_ref, cx_ref, cbc_ref, hp_ref, marks_ref, seg_ref, x_ref,
    gout_ref, gin_ref, dn_ref, gcx_ref, gcbc_ref, gheads_ref, gnorm_ref,
    dproj_ref, scores_ref, dscores_ref, bc_ref,
):
    i = pl.program_id(0)

    @pl.when(i == 0)
    def _():
        marks = marks_ref[...]
        for k in (0, 1):
            bc_ref[k] = jax.nn.silu(taps_pre(bc_raw(proj_ref, k), marks, cbc_ref[k])).astype(bf16)
        scores_ref[...] = dot(bc_ref[1], bc_ref[0], ((1,), (1,)))
        dscores_ref[...] = jnp.zeros_like(dscores_ref)

    @pl.when(i < 4)
    def _():
        j = i
        marks, cx = marks_ref[...], cx_ref[j]
        scaled = scaled_ref[j]
        d_scaled = jnp.zeros((256, 384), f32)
        for c in range(4):
            dm = dm_ref[:, c * 384 : c * 384 + 384]
            d_scaled = d_scaled + dot(dm, w_out_ref[c], ((1,), (1,)))
            gout_ref[c] = dot(scaled, dm, ((0,), (0,))).astype(bf16)
        y = y_ref[j]
        z = proj_ref[j, :, :384].astype(f32)
        sig = jax.nn.sigmoid(z)
        gate = z * sig
        gated = y * gate
        d_gated = d_scaled * cx[6:7] - kappa_ref[:, 0:1] * gated
        dy = d_gated * gate
        dproj_ref[j, :, :384] = (d_gated * y * (sig + gate * (1.0 - sig))).astype(bf16)
        norm_grad = jnp.sum(d_scaled * gated, axis=0, keepdims=True)

        causal = triangle()
        inside = causal & (marks[:, 4:5] == seg_ref[0:1])
        raw, step, rate, cum = head_steps(proj_ref, hp_ref, j, causal.astype(bf16))
        cum_rows = cum.T
        x_raw = proj_ref[j, :, 384:768].astype(f32)
        x_pre = taps_pre(x_raw, marks, cx)
        x_sig = jax.nn.sigmoid(x_pre)
        x = x_pre * x_sig
        scores = scores_ref[...]
        d_scores = dscores_ref[...]
        lane = lanes((256, 128))
        low_half = lane < 64
        row = lax.broadcasted_iota(jnp.int32, (128, 256), 0)
        d_cum = jnp.zeros((256, 128), f32)
        d_cum_rows = jnp.zeros((128, 256), f32)
        d_step = jnp.zeros((256, 128), f32)
        dxs = []
        for p in range(3):
            xp = x[:, 128 * p : 128 * p + 128]
            dyp = dy[:, 128 * p : 128 * p + 128]
            steps = pair_of(step, p)
            xs = (xp * steps).astype(bf16)
            dy_low = dyp.astype(bf16)
            back = []
            for k in (0, 1):
                at = HEAD_AT + 2 * p + k
                fade = fade_of(cum, cum_rows, 2 * p + k, inside)
                mine = jnp.where(low_half if k == 0 else ~low_half, dyp, 0.0).astype(bf16)
                pair = dot(mine, xs, ((1,), (1,)))
                mixing = fade * scores
                w = mixing * pair
                d_scores = d_scores + fade * pair
                d_cum = jnp.where(lane == at, jnp.sum(w, axis=1, keepdims=True), d_cum)
                d_cum_rows = jnp.where(row == at, jnp.sum(w, axis=0, keepdims=True), d_cum_rows)
                back.append(dot(mixing.astype(bf16), dy_low, ((0,), (0,))))
            d_xs = jnp.where(low_half, back[0], back[1])
            prod = xp * d_xs
            first = jnp.sum(jnp.where(low_half, prod, 0.0), axis=1, keepdims=True)
            second = jnp.sum(jnp.where(low_half, 0.0, prod), axis=1, keepdims=True)
            at = HEAD_AT + 2 * p
            d_step = jnp.where(lane == at, first, jnp.where(lane == at + 1, second, d_step))
            dxs.append(d_xs * steps)
        dscores_ref[...] = d_scores
        dx = jnp.concatenate(dxs, axis=1) + cx[5:6] * dy
        skip_grad = jnp.sum(x * dy, axis=0, keepdims=True)
        d_x_pre = dx * (x_sig + x * (1.0 - x_sig))
        d_x_raw, conv_grad = taps_back(d_x_pre, x_raw, marks, cx)
        dproj_ref[j, :, 384:768] = d_x_raw.astype(bf16)
        rowid = lax.broadcasted_iota(jnp.int32, (8, 384), 0)
        gcx_ref[j] = jnp.where(rowid == 5, skip_grad, jnp.where(rowid == 6, norm_grad, conv_grad))
        d_cum = d_cum - d_cum_rows.T
        d_rate = sum(dot(causal.astype(bf16), part, ((0,), (0,))) for part in split3(d_cum))
        d_raw = (d_step - d_rate * hp_ref[j, 0:1]) * jax.nn.sigmoid(raw)
        dproj_ref[j, :, 768:896] = d_raw.astype(bf16)
        rowid = lax.broadcasted_iota(jnp.int32, (8, 128), 0)
        gheads_ref[j] = jnp.where(
            rowid == 0,
            jnp.sum(d_rate * rate, axis=0, keepdims=True),
            jnp.where(rowid == 1, jnp.sum(d_raw, axis=0, keepdims=True), 0.0),
        )

    @pl.when(i == 4)
    def _():
        marks = marks_ref[...]
        d_scores = dscores_ref[...].astype(bf16)
        d_bc = (dot(d_scores, bc_ref[1], ((0,), (0,))), dot(d_scores, bc_ref[0]))
        low_half = lanes((256, 128)) < 64
        for k in (0, 1):
            raw = bc_raw(proj_ref, k)
            pre = taps_pre(raw, marks, cbc_ref[k])
            sig = jax.nn.sigmoid(pre)
            d_pre = d_bc[k] * (sig + pre * sig * (1.0 - sig))
            d_raw, conv_grad = taps_back(d_pre, raw, marks, cbc_ref[k])
            gcbc_ref[k] = conv_grad
            for h, moved in enumerate((d_raw, roll(d_raw, 64, 1))):
                steps = dproj_ref[2 * k + h, :, 768:896].astype(f32)
                dproj_ref[2 * k + h, :, 768:896] = jnp.where(low_half, moved, steps).astype(bf16)
        dn_ref[...] = jnp.zeros_like(dn_ref)

    @pl.when(i >= 4)
    def _():
        j = i - 4
        d_proj = dproj_ref[j]
        dn_ref[...] += dot(d_proj, w_in_ref[0], ((1,), (1,)))
        gin_ref[0, :, :768] = dot(normed_ref[...], d_proj[:, :768], ((0,), (0,))).astype(bf16)
        last = dot(normed_ref[...], d_proj[:, 768:], ((0,), (0,)))
        last = last + dot(ffn_ref[...], drout_ref[j], ((0,), (0,)))
        gin_ref[0, :, 768:] = last.astype(bf16)

    @pl.when(i == 7)
    def _():
        x = x_ref[...].astype(f32)
        total = jnp.sum(dn_ref[...] * x * rms(x), axis=0, keepdims=True)
        gnorm_ref[...] = jnp.broadcast_to(total, gnorm_ref.shape)


def mixer_backward(dm, kappa, w_out, w_in, *rest):
    def late(i):
        return jnp.maximum(i - 4, 0)

    def early(i):
        return jnp.minimum(i, 3)

    small = [
        jax.ShapeDtypeStruct((256, 1536), f32),
        jax.ShapeDtypeStruct((4, 8, 384), f32),
        jax.ShapeDtypeStruct((2, 8, 128), f32),
        jax.ShapeDtypeStruct((4, 8, 128), f32),
        jax.ShapeDtypeStruct((8, 1536), f32),
    ]
    w_out_spec = pl.BlockSpec((4, 384, 384), lambda i: (0, early(i), 0))
    w_in_spec = pl.BlockSpec((1, 1536, 896), lambda i: (late(i), 0, 0))
    return pl.pallas_call(
        backward_kernel,
        grid=(8,),
        out_shape=[
            jax.ShapeDtypeStruct((4, 1536, 384), bf16),
            jax.ShapeDtypeStruct((4, 1536, 896), bf16),
            *small,
        ],
        in_specs=[
            fixed(dm),
            fixed(kappa),
            w_out_spec,
            w_in_spec,
            *[fixed(v) for v in rest],
        ],
        out_specs=[w_out_spec, w_in_spec, *[fixed(o) for o in small]],
        scratch_shapes=[
            pltpu.VMEM((4, 256, 896), bf16),
            pltpu.VMEM((256, 256), f32),
            pltpu.VMEM((256, 256), f32),
            pltpu.VMEM((2, 256, 128), bf16),
        ],
        compiler_params=pltpu.CompilerParams(vmem_limit_bytes=56 * 2**20),
        cost_estimate=pl.CostEstimate(
            flops=0, bytes_accessed=0, transcendentals=0
        ),
        name="mixer_backward",
    )(dm, kappa, w_out, w_in, *rest)


def swap(v):
    return lax.ppermute(v, "seq", [(0, 1), (1, 0)])


def both_halves(own, other, s):
    first = jnp.where(s == 0, own, other)
    second = jnp.where(s == 0, other, own)
    return jnp.concatenate([first, second], axis=0)


def halves(v, s):
    rows = v.shape[0] // 2
    return (
        lax.dynamic_slice_in_dim(v, s * rows, rows, 0),
        lax.dynamic_slice_in_dim(v, (1 - s) * rows, rows, 0),
    )


def hi_lo(v):
    hi = v.astype(bf16)
    return hi, (v - hi.astype(f32)).astype(bf16)


def rms(v):
    return lax.rsqrt(jnp.mean(v * v, axis=-1, keepdims=True) + EPS)


def silu_grad(v):
    sig = jax.nn.sigmoid(v)
    return sig * (1.0 + v * (1.0 - sig))


def local(
    tokens,
    out_grad,
    lengths,
    routes,
    in_norm,
    in_proj,
    conv_weight,
    conv_bias,
    head_params,
    mixer_norm,
    out_proj,
    ffn_norm,
    router,
    shared_gate_up,
    shared_down,
    expert_gate_up,
    expert_down,
):
    s = lax.axis_index("seq")
    dp = lax.axis_index(DP)
    experts, slots = 64, 24
    n_slots = experts * slots

    other_tokens = swap(tokens)
    other_grad = swap(out_grad)
    other_gate_up = swap(expert_gate_up[0])
    other_down = swap(expert_down[0])
    w_in, w_sgu, w_out, w_sdown, vecs = gather(
        in_proj,
        shared_gate_up,
        router,
        jnp.concatenate([out_proj, shared_down], axis=0),
        (in_norm[None], ffn_norm[None], mixer_norm[None], conv_weight.T, conv_bias[None]),
    )
    w_in = w_in.reshape(4, 1536, 896)
    w_sgu = w_sgu.reshape(4, 1536, 256)
    w_out = w_out.reshape(4, 1536, 384)
    w_sdown = w_sdown.reshape(4, 512, 384)

    vecs = vecs.reshape(128, 16, 128).astype(f32)
    g_in = vecs[:, 0, :12].reshape(1, 1536)
    g_ffn = vecs[:, 1, :12].reshape(1536)
    g_mix = lax.dynamic_slice_in_dim(vecs[:, 2, :24].reshape(1, 3072), s * 1536, 1536, 1)
    conv = vecs[:, 3:8, :26].transpose(1, 0, 2).reshape(5, 3328)
    heads = lax.dynamic_slice_in_dim(head_params.astype(f32), s * 24, 24, 1)
    cx = jnp.concatenate(
        [
            lax.dynamic_slice_in_dim(conv[:, :3072], s * 1536, 1536, 1),
            jnp.broadcast_to(heads[2][:, None], (24, 64)).reshape(1, 1536),
            g_mix,
            jnp.zeros((1, 1536), f32),
        ],
        axis=0,
    )
    cx = cx.reshape(8, 4, 384).transpose(1, 0, 2)
    cbc = jnp.pad(conv[:, 3072:], ((0, 3), (0, 0))).reshape(8, 2, 128).transpose(1, 0, 2)
    hp = jnp.stack([jnp.exp(heads[0]), heads[1]]).reshape(2, 4, 6).transpose(1, 0, 2)
    hp = jnp.pad(hp, ((0, 0), (0, 6), (HEAD_AT, 122 - HEAD_AT)))
    w_eg = both_halves(expert_gate_up[0], other_gate_up, s)
    w_ed = both_halves(expert_down[0], other_down, s)

    ids = jnp.arange(experts, dtype=jnp.int32)
    named = jnp.sum((routes[:, :, None] == ids).astype(f32), axis=1)
    t128 = jnp.arange(128)
    before = (t128[:, None] > t128[None, :]).astype(bf16)
    rank = dot(before, named.astype(bf16))
    slot = jnp.arange(n_slots, dtype=jnp.int32)
    spread = (slot[None, :] // slots == ids[:, None]).astype(bf16)
    is_named = dot(named.astype(bf16), spread) > 0.5
    in_slot = dot(rank.astype(bf16), spread) == (slot % slots).astype(f32)[None, :]
    place = (is_named & in_slot).astype(bf16)

    def to_slots(v):
        return dot(place, v, ((0,), (0,))).astype(bf16).reshape(experts, slots, v.shape[1])

    grad_slots, w_in = lax.optimization_barrier((to_slots(out_grad), w_in))
    grad_rows = lax.all_to_all(grad_slots, DP, 0, 0, tiled=True).reshape(n_slots, 1536)

    ends = jnp.cumsum(lengths[0])
    t256 = jnp.arange(256, dtype=jnp.int32)
    segment = jnp.sum((t256[:, None] >= ends[None, :]).astype(jnp.int32), axis=1)
    seg = segment.astype(f32)
    same = [
        (jnp.pad(segment, (d, 0), constant_values=-1)[:256] == segment).astype(f32)
        for d in range(4)
    ]
    marks = jnp.pad(jnp.stack(same + [seg], axis=1), ((0, 0), (0, 123)))
    seg = jnp.broadcast_to(seg, (8, 256))
    x_full = both_halves(tokens, other_tokens, s)
    normed, proj, y, scaled, part, squares = mixer_forward(
        x_full, jnp.broadcast_to(g_in, (8, 1536)), w_in, w_out, cx, cbc, hp, marks, seg
    )
    squares = squares[:, :1]
    part_own, part_other = halves(part, s)
    sq_own, sq_other = halves(squares, s)
    part = part_own + swap(part_other)
    q = lax.rsqrt((sq_own + swap(sq_other)) / 3072.0 + EPS)
    residual = tokens.astype(f32) + q * part

    r = rms(residual)
    ffn_in = (residual * r * g_ffn).astype(bf16)
    w_router = w_in[:, :, 832:848].transpose(1, 0, 2).reshape(1536, 64)
    logits = dot(ffn_in, w_router)
    logits = jnp.where(named > 0.5, logits, -1e30)
    top = jnp.max(logits, axis=1, keepdims=True)
    weights = jnp.where(named > 0.5, jnp.exp(logits - top), 0.0)
    gating = weights / jnp.sum(weights, axis=1, keepdims=True)
    gate_hi, gate_lo = hi_lo(gating)
    sent = to_slots(jnp.concatenate([ffn_in, gate_hi, gate_lo], axis=1))
    sent, grad_rows = lax.optimization_barrier((sent, grad_rows))
    arrived = lax.all_to_all(sent, DP, 0, 0, tiled=True).reshape(n_slots, 1664)

    ffn_full = both_halves(ffn_in, swap(ffn_in), s)
    og_full = both_halves(out_grad, other_grad, s)
    sgu = jnp.stack([dot(ffn_full, w_sgu[j]) for j in range(4)])
    sg, su = sgu[..., :128], sgu[..., 128:]
    s_act = (jax.nn.silu(sg) * su).astype(bf16)
    s_flat = s_act.transpose(1, 0, 2).reshape(256, 512)
    s_out = jnp.concatenate([dot(s_flat, w_sdown[j]) for j in range(4)], axis=1)
    s_own, s_other = halves(s_out, s)
    s_out = s_own + swap(s_other.astype(bf16)).astype(f32)
    og_cols = og_full.reshape(256, 4, 384).transpose(1, 0, 2)
    d_s_act = sum(dot(og_cols[j], w_sdown[j], ((1,), (1,))) for j in range(4))
    d_s_act = d_s_act.reshape(256, 4, 128).transpose(1, 0, 2)
    d_sgu = jnp.concatenate([d_s_act * su * silu_grad(sg), d_s_act * jax.nn.silu(sg)], axis=-1)
    d_sgu = d_sgu.astype(bf16)
    grad_sdown = jnp.stack([dot(s_flat, og_cols[j], ((0,), (0,))) for j in range(4)]).astype(bf16)
    grad_sgu = jnp.stack([dot(ffn_full, d_sgu[j], ((0,), (0,))) for j in range(4)]).astype(bf16)
    d_ffn = sum(dot(d_sgu[j], w_sgu[j], ((1,), (1,))) for j in range(4))
    df_own, df_other = halves(d_ffn, s)
    d_ffn = df_own + swap(df_other.astype(bf16)).astype(f32)

    lane = jnp.arange(128, dtype=jnp.int32) % 64
    pick = (lane == dp).astype(f32)[None, :]
    d_rows, e_act, w_act, w_gu = expert_grads(arrived, grad_rows, w_eg, w_ed, pick)
    d_back = lax.all_to_all(d_rows.reshape(experts, slots, 1664), DP, 0, 0, tiled=True)
    e_out = dot(e_act, w_ed).astype(bf16)
    grad_ed = dot(w_act, grad_rows, ((0,), (0,)))
    grad_eg = dot(arrived[:, :1536], w_gu, ((0,), (0,)))
    ge_own, ge_other = halves(grad_eg, s)
    grad_eg = ge_own + swap(ge_other.astype(bf16)).astype(f32)
    gd_own, gd_other = halves(grad_ed, s)
    grad_ed = gd_own + swap(gd_other.astype(bf16)).astype(f32)
    e_out, d_back, grad_eg, grad_ed, d_ffn, grad_sgu, grad_sdown = lax.optimization_barrier(
        (e_out, d_back, grad_eg, grad_ed, d_ffn, grad_sgu, grad_sdown)
    )
    d_back = d_back.reshape(n_slots, 1664)
    out_back = lax.all_to_all(e_out.reshape(experts, slots, 1536), DP, 0, 0, tiled=True)
    out_back = out_back.reshape(n_slots, 1536)

    wide_gate = dot(gate_hi, spread) + dot(gate_lo, spread)
    weighted = (place.astype(f32) * wide_gate).astype(bf16)
    d_route = dot(weighted, d_back[:, :1536])
    dg = d_back[:, 1536:1538].T
    d_gating = dot(place * dg[0:1], spread, ((1,), (1,))) + dot(
        place * dg[1:2], spread, ((1,), (1,))
    )
    d_logits = gating * (d_gating - jnp.sum(gating * d_gating, axis=1, keepdims=True))
    d_logits_low = d_logits.astype(bf16)
    d_ffn = d_ffn + dot(d_logits_low, w_router, ((1,), (1,))) + d_route
    ffn_norm_grad = jnp.sum(d_ffn * residual * r, axis=0)
    u = d_ffn * g_ffn
    d_residual = (
        out_grad.astype(f32)
        + r * u
        - r * r * r * residual * jnp.mean(u * residual, axis=1, keepdims=True)
    )

    d_mixed = (q * d_residual).astype(bf16)
    kappa = q * q / 3072.0 * jnp.sum(d_mixed.astype(f32) * part, axis=1, keepdims=True)
    d_mixed_full = both_halves(d_mixed, swap(d_mixed), s)
    kappa = both_halves(kappa, swap(kappa), s)
    drout = jnp.pad(d_logits_low.reshape(128, 4, 16).transpose(1, 0, 2), ((0, 0), (0, 0), (64, 48)))
    grad_out, grad_in, d_normed, g_cx, g_cbc, g_heads, in_norm_grad = mixer_backward(
        d_mixed_full, kappa, w_out, w_in, normed, ffn_in, drout, proj, y, scaled, cx, cbc, hp, marks, seg, x_full
    )
    conv_x_grad = g_cx[:, :5].transpose(1, 0, 2).reshape(5, 1536)
    conv_bc_grad = g_cbc[:, :5].transpose(1, 0, 2).reshape(5, 256)
    mixer_norm_grad = g_cx[:, 6].reshape(1536)
    head_grad = g_heads[:, :2, HEAD_AT : HEAD_AT + 6].transpose(1, 0, 2).reshape(2, 24)
    d_skip = jnp.sum(g_cx[:, 5].reshape(24, 64), axis=1)
    head_grad = jnp.concatenate([head_grad, d_skip[None]], axis=0)
    dn_own, dn_other = halves(d_normed, s)
    dn_other = swap(dn_other.astype(bf16))

    conv_grad = lax.dynamic_update_slice(
        jnp.zeros((5, 3328), f32), conv_x_grad, (0, s * 1536)
    )
    conv_grad = lax.dynamic_update_slice(conv_grad, conv_bc_grad, (0, 3072))
    mixer_norm_grad = lax.dynamic_update_slice(
        jnp.zeros((128, 24), f32), mixer_norm_grad.reshape(64, 24), (s * 64, 0)
    )
    head_grad = lax.dynamic_update_slice(jnp.zeros((3, 48), f32), head_grad, (0, s * 24))
    def rows_of(v, width):
        return jnp.pad(v.reshape(128, 1, width), ((0, 0), (0, 0), (0, 64 - width)))

    conv_grad = conv_grad.reshape(5, 128, 26).transpose(1, 0, 2)
    small = jnp.concatenate(
        [
            rows_of(in_norm_grad[0], 12),
            rows_of(ffn_norm_grad, 12),
            rows_of(mixer_norm_grad, 24),
            jnp.pad(conv_grad, ((0, 0), (0, 0), (0, 38))),
        ],
        axis=1,
    )
    head_rows = jnp.broadcast_to(jnp.pad(head_grad, ((0, 5), (0, 16)))[None], (128, 8, 64))
    small = jnp.concatenate([small, head_rows], axis=2).reshape(2, 4, 4, 4, 8, 128)
    sums = scatter(
        (
            grad_in.reshape(4, 2, 4, 4, 48, 896),
            grad_sgu.reshape(4, 2, 4, 4, 48, 256),
            grad_out.reshape(4, 4, 4, 2, 48, 384),
            grad_sdown.reshape(4, 4, 4, 2, 16, 384),
            small,
        )
    )
    weighted_late, dn_own, sums = lax.optimization_barrier((weighted, dn_own, tuple(sums)))
    routed = dot(weighted_late, out_back)
    block_out = (residual + s_out + routed).astype(bf16)
    d_normed = dn_own + dn_other.astype(f32)
    x_own = tokens.astype(f32)
    p = rms(x_own)
    v = d_normed * g_in
    token_grad = (
        d_residual + p * v - p * p * p * x_own * jnp.mean(v * x_own, axis=1, keepdims=True)
    ).astype(bf16)
    (
        in_proj_grad, router_grad, sgu_grad, out_proj_grad, sdown_grad, head_grad, conv_grad,
        in_norm_grad, ffn_norm_grad, mixer_norm_grad, conv_bias_grad,
    ) = finish(*sums)
    return (
        block_out,
        token_grad,
        in_norm_grad[0],
        in_proj_grad,
        conv_grad,
        conv_bias_grad[0],
        head_grad,
        mixer_norm_grad[0],
        out_proj_grad,
        ffn_norm_grad[0],
        router_grad,
        sgu_grad,
        sdown_grad,
        grad_eg[None],
        grad_ed[None],
    )


def solution(mesh):
    finer = Mesh(mesh.devices.reshape(2, 4, 4, 4), ALL)
    placed = (
        P(DP_SEQ, None),
        P(DP_SEQ, None),
        P(DP, None),
        P(DP_SEQ, None),
        P(ALL),
        P(ALL, None),
        P(ALL, None),
        P(ALL),
        P(),
        P(ALL),
        P(ALL, None),
        P(ALL),
        P(ALL, None),
        P(ALL, None),
        P(ALL, None),
        P(DP, "seq", None),
        P(DP, "seq", None),
    )
    return jax.shard_map(
        local,
        mesh=finer,
        in_specs=placed,
        out_specs=(
            P(DP_SEQ, None),
            P(DP_SEQ, None),
            P(ALL),
            P(ALL, None),
            P(ALL, None),
            P(ALL),
            P(),
            P(ALL),
            P(ALL, None),
            P(ALL),
            P(ALL, None),
            P(ALL, None),
            P(ALL, None),
            P(DP, "seq", None),
            P(DP, "seq", None),
        ),
        check_vma=False,
    )
```

```python
import functools

import jax
import jax.numpy as jnp
import numpy as np
from jax import lax
from jax.experimental import pallas as pl
from jax.experimental.pallas import tpu as pltpu
from jax.sharding import Mesh
from jax.sharding import PartitionSpec as P

DP = ("z", "x", "y")
ALL = ("seq", "z", "x", "y")
DP_SEQ = ("z", "x", "y", "seq")
ORDER = (("z", "x", "y"), ("x", "y", "z"), ("y", "z", "x"))
REM = (("z", "x"), ("y", "x"), ("y", "z"))
MESH_ID = pl.DeviceIdType.MESH
EPS = 1e-05
f32 = jnp.float32
bf16 = jnp.bfloat16

ROWS_FIRST = (("y", "s", "z", "x"), "rows")
CHANNELS = (("y", "z", "x", "s"), "cols")
VECTORS = (("s", "z", "x", "y"), "one")
SPECS = (ROWS_FIRST, ROWS_FIRST, CHANNELS, CHANNELS, VECTORS)
HEAD_AT = 80
SIZES = {"y": 4, "z": 4, "x": 4, "s": 2}


def dot(a, b, dims=((1,), (0,))):
    return lax.dot_general(a, b, (dims, ((), ())), preferred_element_type=f32)


def neighbours():
    pos = {a: lax.axis_index(a) for a in DP}
    right = {a: lax.rem(pos[a] + 1, 4) for a in DP}
    left = {a: lax.rem(pos[a] + 3, 4) for a in DP}
    opp = {a: lax.rem(pos[a] + 2, 4) for a in DP}
    return pos, right, left, opp


def chip_row():
    core, y = lax.axis_index("seq"), lax.axis_index("y")
    return [(lax.rem(core + c, 2), lax.rem(y + d, 4)) for c in range(2) for d in range(4)]


def greet(right, left, opp):
    barrier = pltpu.get_barrier_semaphore()

    def signal(device_id):
        pl.semaphore_signal(barrier, inc=1, device_id=device_id, device_id_type=MESH_ID)

    for a in ("z", "x"):
        signal({a: right[a]})
        signal({a: left[a]})
        signal({a: opp[a]})
    for core, y in chip_row()[1:]:
        signal({"seq": core, "y": y})


def met(count):
    pl.semaphore_wait(pltpu.get_barrier_semaphore(), count)


def cuts(spec):
    return range(1 if spec[1] == "one" else 3)


def third(shape, split, a):
    rows, cols = shape[-2:]
    if split == "one":
        return (slice(None), slice(None))
    if split == "rows":
        return (pl.ds(rows // 3 * a, rows // 3), slice(None))
    return (slice(None), pl.ds(cols // 3 * a, cols // 3))


def third_shape(shape, split):
    rows, cols = shape[-2:]
    return {"one": (rows, cols), "rows": (rows // 3, cols), "cols": (rows, cols // 3)}[split]


def region(ref, spec, free, fixed, a, s=None):
    order, split = spec
    ix = []
    for d in order:
        if d == "s":
            ix.append(slice(None) if s is None else s)
        else:
            ix.append(slice(None) if d in free else fixed[d])
    return ref.at[tuple(ix) + third(ref.shape, split, a)]


def roll(v, by, axis):
    by = by % v.shape[axis]
    return pltpu.roll(v, by, axis) if by else v


def lanes(shape):
    return lax.broadcasted_iota(jnp.int32, shape, len(shape) - 1)


def moved(v, at, to, width):
    lane = lanes(v.shape)
    return jnp.where((lane >= to) & (lane < to + width), roll(v, to - at, 1), 0.0)


def gather_kernel(in_ref, gu_ref, router_ref, rows_ref, *refs):
    specs, n = SPECS, len(SPECS)
    vec_refs, outs, blocks = refs[:5], refs[5 : 5 + n], refs[5 + n : 5 + 2 * n]
    pin, pout, bin_, bout, wide, vec, send0, recv0, send, recv, loc = refs[5 + 2 * n :]
    pos, right, left, opp = neighbours()
    row = chip_row()
    (core, y) = row[0]
    greet(right, left, opp)
    wide[...] = jnp.zeros_like(wide)
    wide[0, :12, :48] = in_ref[:, 6400:].astype(f32)
    wide[1, :12, :64] = router_ref[...].astype(f32)
    at = 0
    for v in vec_refs:
        wide[2, at : at + v.shape[0], : v.shape[1]] = v[...].astype(f32)
        at += v.shape[0]
    vec[...] = wide[2].astype(bf16)
    bc = [in_ref[:, 6144 + 128 * k : 6272 + 128 * k].astype(f32) for k in range(2)]
    steps, router = wide[0, :12], wide[1, :12]
    for c in range(2):
        for j in range(4):
            k, at = 4 * c + j, c * 1536 + j * 384
            misc = (
                moved(bc[j // 2], 64 * (j % 2), 0, 64)
                + moved(router, 16 * j, 64, 16)
                + moved(steps, 24 * c + 6 * j, HEAD_AT, 6)
            )
            pin[k, :12, :384] = in_ref[:, at : at + 384]
            pin[k, :12, 384:768] = in_ref[:, 3072 + at : 3456 + at]
            pin[k, :12, 768:896] = misc.astype(bf16)
            pin[k, :12, 896:1024] = gu_ref[:, 128 * k : 128 * k + 128]
            pin[k, :12, 1024:] = gu_ref[:, 1024 + 128 * k : 1152 + 128 * k]
    for j in range(4):
        pout[j] = rows_ref[:, 384 * j : 384 * j + 384]
    met(13)
    sends, first = [], []

    def push(src, dst, k, device_id):
        c = pltpu.make_async_remote_copy(
            src_ref=src,
            dst_ref=dst,
            send_sem=send0.at[k],
            recv_sem=recv0.at[k],
            device_id=device_id,
            device_id_type=MESH_ID,
        )
        c.start()
        sends.append(c)
        first.append(c)

    for k, (c, d) in enumerate(row):
        if k:
            push(pin.at[4 * c + d], bin_.at[4 * core + y], k, {"seq": c, "y": d})
    for k, (_, d) in enumerate(row[:4]):
        if k:
            push(pout.at[d], bout.at[y], 8 + k, {"y": d})
    push(vec, blocks[4].at[core], 0, {"seq": 1 - core})
    blocks[4][core] = vec[...]
    bin_[4 * core + y] = pin[4 * core + y]
    bout[y] = pout[y]
    for c in first:
        c.wait_recv()
    for c in range(2):
        v = jnp.concatenate([bin_[4 * c + d].astype(f32)[:12] for d in range(4)], axis=0)
        blocks[0][c] = v[:, :896].astype(bf16)
        blocks[1][c] = v[:, 896:].astype(bf16)
    v = [bout[d].astype(f32) for d in range(4)]
    for h in range(2):
        blocks[2][h] = jnp.concatenate([v[2 * h][:24], v[2 * h + 1][:24]], axis=0).astype(bf16)
        blocks[3][h] = jnp.concatenate([v[2 * h][24:], v[2 * h + 1][24:]], axis=0).astype(bf16)

    own = []
    for i in range(n):
        ix = tuple(slice(None) if d == "s" else pos[d] for d in specs[i][0])
        c = pltpu.make_async_copy(blocks[i], outs[i].at[ix], loc.at[i])
        c.start()
        own.append(c)

    def remote(i, st, a, k, src, dst, ax, to):
        c = pltpu.make_async_remote_copy(
            src_ref=src,
            dst_ref=dst,
            send_sem=send.at[i, st, a, k],
            recv_sem=recv.at[i, st, a, k],
            device_id={ax: to},
            device_id_type=MESH_ID,
        )
        c.start()
        sends.append(c)
        return c

    every = [(i, a) for i in range(n) for a in cuts(specs[i])]
    first, later = {}, {}

    def begin(i, a, st):
        ax, free = ORDER[a][st], ORDER[a][:st]
        dst = region(outs[i], specs[i], free, pos, a)
        src = dst
        if st == 0:
            src = blocks[i].at[(slice(None),) + third(blocks[i].shape, specs[i][1], a)]
        for d, to in enumerate((right[ax], left[ax])):
            first[i, a, d] = remote(i, st, a, d, src, dst, ax, to)
        if st == 0:
            later[i, a, 0] = remote(i, st, a, 2, src, dst, ax, opp[ax])

    for i, a in every:
        begin(i, a, 0)
    for c in own:
        c.wait()
    for st in range(3):
        for i, a in every:
            ax, free = ORDER[a][st], ORDER[a][:st]
            for d, (to, frm) in enumerate(((right[ax], left[ax]), (left[ax], right[ax]))):
                first[i, a, d].wait_recv()
                if st:
                    r = region(outs[i], specs[i], free, {**pos, ax: frm}, a, s=d)
                    later[i, a, d] = remote(i, st, a, 2 + d, r, r, ax, to)
        for i, a in every:
            for d in range(2 if st else 1):
                later[i, a, d].wait_recv()
            if st < 2:
                begin(i, a, st + 1)
    for c in sends:
        c.wait_send()


def gather(in_proj, gate_up, router, rows, vectors):
    n = len(SPECS)
    blocks = [(2, 48, 896), (2, 48, 256), (2, 48, 384), (2, 16, 384), (2, 16, 128)]
    outs = [
        jax.ShapeDtypeStruct(tuple(SIZES[d] for d in spec[0]) + v[1:], bf16)
        for v, spec in zip(blocks, SPECS)
    ]
    total = sum(int(np.prod(o.shape)) for o in outs) * 2
    return pl.pallas_call(
        gather_kernel,
        out_shape=outs,
        in_specs=[pl.BlockSpec(memory_space=pltpu.VMEM)] * 9,
        out_specs=[pl.BlockSpec(memory_space=pl.ANY)] * n,
        scratch_shapes=[pltpu.VMEM(v, bf16) for v in blocks]
        + [
            pltpu.VMEM((8, 16, 1152), bf16),
            pltpu.VMEM((4, 32, 384), bf16),
            pltpu.VMEM((8, 16, 1152), bf16),
            pltpu.VMEM((4, 32, 384), bf16),
            pltpu.VMEM((3, 16, 128), f32),
            pltpu.VMEM((16, 128), bf16),
            pltpu.SemaphoreType.DMA((12,)),
            pltpu.SemaphoreType.DMA((12,)),
            pltpu.SemaphoreType.DMA((n, 3, 3, 4)),
            pltpu.SemaphoreType.DMA((n, 3, 3, 4)),
            pltpu.SemaphoreType.DMA((n,)),
        ],
        compiler_params=pltpu.CompilerParams(
            collective_id=1, has_side_effects=True, vmem_limit_bytes=60 * 2**20
        ),
        cost_estimate=pl.CostEstimate(flops=0, bytes_accessed=2 * total, transcendentals=0),
        name="gather_weights",
    )(in_proj, gate_up, router, rows, *vectors)


def each(lead, fn):
    @pl.loop(0, int(np.prod(lead)))
    def _(i):
        ix = []
        for d in reversed(lead):
            ix.append(lax.rem(i, d))
            i = lax.div(i, d)
        fn(tuple(reversed(ix)))


def scatter_kernel(*refs):
    specs, n = SPECS, len(SPECS)
    gs, (bin_, bout, small_out) = refs[:n], refs[n : n + 3]
    outs, refs = refs[n + 3 : 2 * n + 3], refs[2 * n + 3 :]
    held, got = refs[:n], [refs[n + 3 * i : n + 3 * i + 3] for i in range(n)]
    pin, pout, other, send0, recv0, send, recv, loc = refs[4 * n :]
    pos, right, left, opp = neighbours()
    row = chip_row()
    (core, y) = row[0]

    def source(i, st, a, idx, s):
        ax = ORDER[a][2 - st]
        if st == 0:
            return region(gs[i], specs[i], [d for d in DP if d != ax], {ax: idx}, a, s)
        part = held[i].at[a, 2 + s]
        if st == 1:
            return part.at[:, idx] if REM[a][1] == ax else part.at[idx]
        me = pos[ORDER[a][1]]
        return part.at[me, idx] if REM[a][1] == ax else part.at[idx, me]

    local = {}
    for i in range(n):
        for a in cuts(specs[i]):
            ax = ORDER[a][2]
            for k, (idx, s) in enumerate(((right[ax], 0), (left[ax], 1), (pos[ax], 0), (pos[ax], 1))):
                c = pltpu.make_async_copy(source(i, 0, a, idx, s), held[i].at[a, k], loc.at[i, a, k])
                c.start()
                local[i, a, k] = c
    greet(right, left, opp)
    met(13)
    sends = []

    def remote(i, st, a, k, src, ax, to):
        c = pltpu.make_async_remote_copy(
            src_ref=src,
            dst_ref=got[i][st].at[a, k],
            send_sem=send.at[i, st, a, k],
            recv_sem=recv.at[i, st, a, k],
            device_id={ax: to},
            device_id_type=MESH_ID,
        )
        c.start()
        sends.append(c)
        return c

    every = [(i, a) for i in range(n) for a in cuts(specs[i])]
    cp = {}

    def begin(i, a, st):
        ax = ORDER[a][2 - st]
        if st == 2:
            for k, to in enumerate((opp[ax], right[ax], left[ax])):
                for s in range(2):
                    cp[i, a, 2 * k + s] = remote(i, st, a, 2 * k + s, source(i, st, a, to, s), ax, to)
            return
        cp[i, a, 0] = remote(i, st, a, 0, source(i, st, a, opp[ax], 0), ax, right[ax])
        cp[i, a, 1] = remote(i, st, a, 1, source(i, st, a, opp[ax], 1), ax, left[ax])
        cp[i, a, 2] = remote(i, st, a, 2, source(i, st, a, right[ax], 1), ax, right[ax])
        cp[i, a, 3] = remote(i, st, a, 3, source(i, st, a, left[ax], 0), ax, left[ax])

    for i, a in every:
        begin(i, a, 0)
    for st in range(2):
        lead = ((4, 4), (4,))[st]
        for i, a in every:
            ax = ORDER[a][2 - st]
            for d, to in enumerate((right[ax], left[ax])):
                cp[i, a, d].wait_recv()
                if st == 0:
                    local[i, a, d].wait()
                    acc = held[i].at[a, d]
                else:
                    acc = source(i, st, a, to, d)
                more = got[i][st].at[a, d]

                def add(ix, acc=acc, more=more):
                    acc[ix] = (acc[ix].astype(f32) + more[ix].astype(f32)).astype(acc.dtype)

                each(lead, add)
                cp[i, a, 4 + d] = remote(i, st, a, 4 + d, acc, ax, to)
        for i, a in every:
            ax = ORDER[a][2 - st]
            if st == 0:
                local[i, a, 2].wait()
                local[i, a, 3].wait()
            for s, (p, q) in enumerate(((4, 3), (2, 5))):
                cp[i, a, p].wait_recv()
                cp[i, a, q].wait_recv()
                acc = held[i].at[a, 2 + s] if st == 0 else source(i, st, a, pos[ax], s)
                one, two = got[i][st].at[a, p], got[i][st].at[a, q]

                def close(ix, acc=acc, one=one, two=two):
                    total = acc[ix].astype(f32) + one[ix].astype(f32) + two[ix].astype(f32)
                    acc[ix] = total.astype(acc.dtype)

                each(lead, close)
            begin(i, a, st + 1)
    for i, a in every:
        ax = ORDER[a][0]
        for s in range(2):
            total = source(i, 2, a, pos[ax], s)[...].astype(f32)
            for k in range(3):
                cp[i, a, 2 * k + s].wait_recv()
                total = total + got[i][2][a, 2 * k + s].astype(f32)
            outs[i][(s,) + third(outs[i].shape, specs[i][1], a)] = total

    for k in range(8):
        c, d = divmod(k, 4)
        pin[k, :12, :896] = outs[0][c, 12 * d : 12 * d + 12, :]
        pin[k, :12, 896:] = outs[1][c, 12 * d : 12 * d + 12, :]
    for d in range(4):
        h, at = divmod(d, 2)
        pout[d, :24] = outs[2][h, 24 * at : 24 * at + 24, :]
        pout[d, 24:] = outs[3][h, 8 * at : 8 * at + 8, :]
    last = []

    def push(src, dst, k, device_id):
        c = pltpu.make_async_remote_copy(
            src_ref=src,
            dst_ref=dst,
            send_sem=send0.at[k],
            recv_sem=recv0.at[k],
            device_id=device_id,
            device_id_type=MESH_ID,
        )
        c.start()
        sends.append(c)
        last.append(c)

    for k, (c, d) in enumerate(row):
        if k:
            push(pin.at[4 * c + d], bin_.at[4 * core + y], k, {"seq": c, "y": d})
    for k, (_, d) in enumerate(row[:4]):
        if k:
            push(pout.at[d], bout.at[y], 8 + k, {"y": d})
    push(outs[4].at[1 - core], other, 0, {"seq": 1 - core})
    bin_[4 * core + y] = pin[4 * core + y]
    bout[y] = pout[y]
    for c in last:
        c.wait_recv()
    small_out[...] = outs[4][core] + other[...]
    for c in sends:
        c.wait_send()


def finish_kernel(bin_, bout, small, in_out, router_out, gu_out, out_out, down_out, heads_out, taps_out, *vecs):
    misc = []
    for k in range(8):
        got_k = bin_[k]
        in_out[:, 384 * k : 384 * k + 384] = got_k[:12, :384]
        in_out[:, 3072 + 384 * k : 3456 + 384 * k] = got_k[:12, 384:768]
        gu_out[:, 128 * k : 128 * k + 128] = got_k[:12, 896:1024]
        gu_out[:, 1024 + 128 * k : 1152 + 128 * k] = got_k[:12, 1024:]
        misc.append(got_k[:, 768:896])
    both = [misc[j] + misc[4 + j] for j in range(4)]
    for h in range(2):
        pair = moved(both[2 * h], 0, 0, 64) + moved(both[2 * h + 1], 0, 64, 64)
        in_out[:, 6144 + 128 * h : 6272 + 128 * h] = pair[:12]
    steps = sum(moved(misc[k], HEAD_AT, 6 * k, 6) for k in range(8))
    in_out[:, 6400:] = steps[:12, :48]
    router = sum(moved(both[j], 64, 16 * j, 16) for j in range(4))
    router_out[...] = router[:12, :64]
    for j in range(4):
        out_out[:, 384 * j : 384 * j + 384] = bout[j, :24]
        down_out[:, 384 * j : 384 * j + 384] = bout[j, 24:]
    heads_out[...] = moved(small[...], 64, 0, 48)[:3, :48]
    taps_out[...] = jnp.concatenate([small[...]] * 16, axis=0).T[:26, 3:7]
    for v, at in zip(vecs, (0, 1, 2, 7)):
        v[...] = small[at : at + 1, : v.shape[1]]


def finish(bin_, bout, small):
    results = [(12, 6448), (12, 64), (12, 2048), (24, 1536), (8, 1536), (3, 48), (26, 4)]
    results += [(1, 12), (1, 12), (1, 24), (1, 26)]
    return pl.pallas_call(
        finish_kernel,
        out_shape=[jax.ShapeDtypeStruct(v, f32) for v in results],
        in_specs=[pl.BlockSpec(memory_space=pltpu.VMEM)] * 3,
        out_specs=[pl.BlockSpec(memory_space=pltpu.VMEM)] * len(results),
        name="finish_grads",
    )(bin_, bout, small)


def scatter(arrays):
    n = len(arrays)
    results = [(8, 16, 1152), (4, 32, 384), (8, 128)]
    pieces = [(third_shape(v.shape, spec[1]), v.dtype) for v, spec in zip(arrays, SPECS)]
    cut = [len(cuts(spec)) for spec in SPECS]
    return pl.pallas_call(
        scatter_kernel,
        out_shape=[jax.ShapeDtypeStruct(v, f32) for v in results],
        in_specs=[pl.BlockSpec(memory_space=pl.ANY)] * n,
        out_specs=[pl.BlockSpec(memory_space=pltpu.VMEM)] * len(results),
        scratch_shapes=[pltpu.VMEM((2,) + v.shape[4:], f32) for v in arrays]
        + [pltpu.VMEM((k, 4, 4, 4) + p, t) for k, (p, t) in zip(cut, pieces)]
        + [
            pltpu.VMEM((k, 6) + lead + p, t)
            for k, (p, t) in zip(cut, pieces)
            for lead in ((4, 4), (4,), ())
        ]
        + [
            pltpu.VMEM((8, 16, 1152), f32),
            pltpu.VMEM((4, 32, 384), f32),
            pltpu.VMEM((8, 128), f32),
            pltpu.SemaphoreType.DMA((12,)),
            pltpu.SemaphoreType.DMA((12,)),
            pltpu.SemaphoreType.DMA((n, 3, 3, 6)),
            pltpu.SemaphoreType.DMA((n, 3, 3, 6)),
            pltpu.SemaphoreType.DMA((n, 3, 4)),
        ],
        compiler_params=pltpu.CompilerParams(
            collective_id=2, has_side_effects=True, vmem_limit_bytes=56 * 2**20
        ),
        cost_estimate=pl.CostEstimate(flops=0, bytes_accessed=0, transcendentals=0),
        name="scatter_grads",
    )(*arrays)


def expert_kernel(rows_ref, grad_ref, gu_ref, down_ref, pick_ref, back_ref, act_ref, wact_ref, wgu_ref):
    for at in range(0, rows_ref.shape[0], 256):
        part = pl.ds(at, 256)
        e_gu = dot(rows_ref[part, :1536], gu_ref[...])
        d_act = dot(grad_ref[part, :], down_ref[...], ((1,), (1,)))
        eg, eu = e_gu[:, :512], e_gu[:, 512:]
        sig = jax.nn.sigmoid(eg)
        silu = eg * sig
        act32 = silu * eu
        act = act32.astype(bf16)
        slot_gate = jnp.sum(rows_ref[part, 1536:].astype(f32) * pick_ref[...], axis=1, keepdims=True)
        d_gate = jnp.sum(act.astype(f32) * d_act, axis=1, keepdims=True)
        d_eg = d_act * eu * (sig + silu * (1.0 - sig))
        d_eu = d_act * silu
        d_gu = jnp.concatenate([d_eg.astype(bf16), d_eu.astype(bf16)], axis=1)
        back_ref[part, :1536] = dot(d_gu, gu_ref[...], ((1,), (1,))).astype(bf16)
        hi = d_gate.astype(bf16).astype(f32)
        lane = lanes((256, 128))
        tail = jnp.where(lane == 0, hi, jnp.where(lane == 1, d_gate - hi, 0.0))
        back_ref[part, 1536:] = tail.astype(bf16)
        act_ref[part, :] = act
        wact_ref[part, :] = (act32 * slot_gate).astype(bf16)
        wgu_ref[part, :512] = (d_eg * slot_gate).astype(bf16)
        wgu_ref[part, 512:] = (d_eu * slot_gate).astype(bf16)


def expert_grads(rows, grad_rows, gate_up, down, pick):
    n, block = rows.shape[0], 512
    widths = (1664, 512, 512, 1024)

    def blocked(w):
        return pl.BlockSpec((block, w), lambda i: (i, 0))

    def whole(v):
        return pl.BlockSpec(v.shape, lambda i: (0, 0))

    return pl.pallas_call(
        expert_kernel,
        grid=(n // block,),
        out_shape=[jax.ShapeDtypeStruct((n, w), bf16) for w in widths],
        in_specs=[blocked(1664), blocked(1536), whole(gate_up), whole(down), whole(pick)],
        out_specs=[blocked(w) for w in widths],
        compiler_params=pltpu.CompilerParams(vmem_limit_bytes=48 * 2**20),
        cost_estimate=pl.CostEstimate(
            flops=2 * n * 1536 * (1024 + 512 + 1024), bytes_accessed=26 * 2**20, transcendentals=0
        ),
        name="expert_grads",
    )(rows, grad_rows, gate_up, down, pick)


def split3(v):
    hi = v.astype(bf16)
    rest = v - hi.astype(f32)
    mid = rest.astype(bf16)
    return hi, mid, (rest - mid.astype(f32)).astype(bf16)


def taps_pre(v, marks, w):
    total = w[4:5] + w[3:4] * v
    for d in (1, 2, 3):
        total = total + w[3 - d : 4 - d] * (roll(v, d, 0) * marks[:, d : d + 1])
    return total


def taps_back(d_pre, v, marks, w):
    d_v = w[3:4] * d_pre
    d_w = [jnp.sum(d_pre * v, axis=0, keepdims=True)]
    for d in (1, 2, 3):
        masked = d_pre * marks[:, d : d + 1]
        d_w.insert(0, jnp.sum(masked * roll(v, d, 0), axis=0, keepdims=True))
        d_v = d_v + w[3 - d : 4 - d] * roll(masked, 256 - d, 0)
    zero = jnp.zeros((3, v.shape[1]), f32)
    return d_v, jnp.concatenate(d_w + [jnp.sum(d_pre, axis=0, keepdims=True), zero], axis=0)


def joined(first, second):
    return jnp.where(lanes(first.shape) < 64, first, roll(second, 64, 1))


def bc_raw(proj_ref, k):
    return joined(
        proj_ref[2 * k, :, 768:896].astype(f32), proj_ref[2 * k + 1, :, 768:896].astype(f32)
    )


def head_steps(proj_ref, hp_ref, j, tri):
    raw = proj_ref[j, :, 768:896].astype(f32) + hp_ref[j, 1:2]
    step = jnp.maximum(raw, 0.0) + jnp.log1p(jnp.exp(-jnp.abs(raw)))
    rate = -step * hp_ref[j, 0:1]
    cum = sum(dot(tri, part) for part in split3(rate))
    return raw, step, rate, cum


def triangle():
    t = lax.broadcasted_iota(jnp.int32, (256, 256), 0)
    return t >= lanes((256, 256))


def pair_of(cols, p):
    at = HEAD_AT + 2 * p
    first = jnp.broadcast_to(cols[:, at : at + 1], (256, 128))
    return jnp.where(lanes((256, 128)) < 64, first, cols[:, at + 1 : at + 2])


def fade_of(cum, cum_rows, h, inside):
    at = HEAD_AT + h
    return jnp.exp(jnp.where(inside, cum[:, at : at + 1] - cum_rows[at : at + 1], -1e30))


def forward_kernel(
    x_ref, g_ref, w_in_ref, w_out_ref, cx_ref, cbc_ref, hp_ref, marks_ref, seg_ref,
    normed_ref, proj_ref, y_ref, scaled_ref, part_ref, squares_ref, scores_ref,
):
    i = pl.program_id(0)

    @pl.when(i == 0)
    def _():
        x = x_ref[...].astype(f32)
        normed_ref[...] = (x * rms(x) * g_ref[0:1]).astype(bf16)

    @pl.when(i < 4)
    def _():
        proj_ref[i] = dot(normed_ref[...], w_in_ref[0]).astype(bf16)

    @pl.when(i == 4)
    def _():
        marks = marks_ref[...]
        b_mat, c_mat = [jax.nn.silu(taps_pre(bc_raw(proj_ref, k), marks, cbc_ref[k])) for k in (0, 1)]
        scores_ref[...] = dot(c_mat.astype(bf16), b_mat.astype(bf16), ((1,), (1,)))
        part_ref[...] = jnp.zeros_like(part_ref)
        squares_ref[...] = jnp.zeros_like(squares_ref)

    @pl.when(i >= 4)
    def _():
        j = i - 4
        marks, cx = marks_ref[...], cx_ref[j]
        causal = triangle()
        inside = causal & (marks[:, 4:5] == seg_ref[0:1])
        _, step, _, cum = head_steps(proj_ref, hp_ref, j, causal.astype(bf16))
        cum_rows = cum.T
        x = jax.nn.silu(taps_pre(proj_ref[j, :, 384:768].astype(f32), marks, cx))
        scores = scores_ref[...]
        ys = []
        for p in range(3):
            xp = x[:, 128 * p : 128 * p + 128]
            xs = (xp * pair_of(step, p)).astype(bf16)
            y0, y1 = [
                dot((fade_of(cum, cum_rows, 2 * p + k, inside) * scores).astype(bf16), xs)
                for k in (0, 1)
            ]
            ys.append(jnp.where(lanes((256, 128)) < 64, y0, y1))
        y = jnp.concatenate(ys, axis=1) + cx[5:6] * x
        z = proj_ref[j, :, :384].astype(f32)
        gated = y * jax.nn.silu(z)
        scaled = (gated * cx[6:7]).astype(bf16)
        y_ref[j] = y
        scaled_ref[j] = scaled
        squares_ref[...] += jnp.broadcast_to(
            jnp.sum(gated * gated, axis=1, keepdims=True), squares_ref.shape
        )
        for c in range(4):
            part_ref[:, c * 384 : c * 384 + 384] += dot(scaled, w_out_ref[c])


def fixed(v):
    return pl.BlockSpec(v.shape, lambda i: (0,) * len(v.shape))


def mixer_forward(x, g, w_in, w_out, cx, cbc, hp, marks, seg):
    outs = [
        jax.ShapeDtypeStruct((256, 1536), bf16),
        jax.ShapeDtypeStruct((4, 256, 896), bf16),
        jax.ShapeDtypeStruct((4, 256, 384), f32),
        jax.ShapeDtypeStruct((4, 256, 384), bf16),
        jax.ShapeDtypeStruct((256, 1536), f32),
        jax.ShapeDtypeStruct((256, 128), f32),
    ]
    return pl.pallas_call(
        forward_kernel,
        grid=(8,),
        out_shape=outs,
        in_specs=[
            fixed(x),
            fixed(g),
            pl.BlockSpec((1, 1536, 896), lambda i: (jnp.minimum(i, 3), 0, 0)),
            pl.BlockSpec((4, 384, 384), lambda i: (0, jnp.maximum(i - 4, 0), 0)),
            *[fixed(v) for v in (cx, cbc, hp, marks, seg)],
        ],
        out_specs=[fixed(o) for o in outs],
        scratch_shapes=[pltpu.VMEM((256, 256), f32)],
        compiler_params=pltpu.CompilerParams(vmem_limit_bytes=48 * 2**20),
        cost_estimate=pl.CostEstimate(
            flops=2 * 256 * 1536 * (3584 + 1536), bytes_accessed=22 * 2**20, transcendentals=2**21
        ),
        name="mixer_forward",
    )(x, g, w_in, w_out, cx, cbc, hp, marks, seg)


def backward_kernel(
    dm_ref, kappa_ref, w_out_ref, w_in_ref, normed_ref, ffn_ref, drout_ref, proj_ref, y_ref,
    scaled_ref, cx_ref, cbc_ref, hp_ref, marks_ref, seg_ref, x_ref,
    gout_ref, gin_ref, dn_ref, gcx_ref, gcbc_ref, gheads_ref, gnorm_ref,
    dproj_ref, scores_ref, dscores_ref, bc_ref, w_ref, fetched,
):
    i = pl.program_id(0)

    def fetch(j):
        return pltpu.make_async_copy(w_in_ref.at[j], w_ref.at[j], fetched.at[j])

    @pl.when(i == 0)
    def _():
        for j in range(4):
            fetch(j).start()
        marks = marks_ref[...]
        for k in (0, 1):
            bc_ref[k] = jax.nn.silu(taps_pre(bc_raw(proj_ref, k), marks, cbc_ref[k])).astype(bf16)
        scores_ref[...] = dot(bc_ref[1], bc_ref[0], ((1,), (1,)))
        dscores_ref[...] = jnp.zeros_like(dscores_ref)

    @pl.when(i < 4)
    def _():
        j = i
        marks, cx = marks_ref[...], cx_ref[j]
        scaled = scaled_ref[0]
        d_scaled = jnp.zeros((256, 384), f32)
        for c in range(4):
            dm = dm_ref[:, c * 384 : c * 384 + 384]
            d_scaled = d_scaled + dot(dm, w_out_ref[c], ((1,), (1,)))
            gout_ref[c] = dot(scaled, dm, ((0,), (0,))).astype(bf16)
        y = y_ref[0]
        z = proj_ref[j, :, :384].astype(f32)
        sig = jax.nn.sigmoid(z)
        gate = z * sig
        gated = y * gate
        d_gated = d_scaled * cx[6:7] - kappa_ref[:, 0:1] * gated
        dy = d_gated * gate
        dproj_ref[j, :, :384] = (d_gated * y * (sig + gate * (1.0 - sig))).astype(bf16)
        norm_grad = jnp.sum(d_scaled * gated, axis=0, keepdims=True)

        causal = triangle()
        inside = causal & (marks[:, 4:5] == seg_ref[0:1])
        raw, step, rate, cum = head_steps(proj_ref, hp_ref, j, causal.astype(bf16))
        cum_rows = cum.T
        x_raw = proj_ref[j, :, 384:768].astype(f32)
        x_pre = taps_pre(x_raw, marks, cx)
        x_sig = jax.nn.sigmoid(x_pre)
        x = x_pre * x_sig
        scores = scores_ref[...]
        d_scores = dscores_ref[...]
        lane = lanes((256, 128))
        low_half = lane < 64
        row = lax.broadcasted_iota(jnp.int32, (128, 256), 0)
        d_cum = jnp.zeros((256, 128), f32)
        d_cum_rows = jnp.zeros((128, 256), f32)
        d_step = jnp.zeros((256, 128), f32)
        dxs = []
        for p in range(3):
            xp = x[:, 128 * p : 128 * p + 128]
            dyp = dy[:, 128 * p : 128 * p + 128]
            steps = pair_of(step, p)
            xs = (xp * steps).astype(bf16)
            dy_low = dyp.astype(bf16)
            back = []
            for k in (0, 1):
                at = HEAD_AT + 2 * p + k
                fade = fade_of(cum, cum_rows, 2 * p + k, inside)
                mine = jnp.where(low_half if k == 0 else ~low_half, dyp, 0.0).astype(bf16)
                pair = dot(mine, xs, ((1,), (1,)))
                mixing = fade * scores
                w = mixing * pair
                d_scores = d_scores + fade * pair
                d_cum = jnp.where(lane == at, jnp.sum(w, axis=1, keepdims=True), d_cum)
                d_cum_rows = jnp.where(row == at, jnp.sum(w, axis=0, keepdims=True), d_cum_rows)
                back.append(dot(mixing.astype(bf16), dy_low, ((0,), (0,))))
            d_xs = jnp.where(low_half, back[0], back[1])
            prod = xp * d_xs
            first = jnp.sum(jnp.where(low_half, prod, 0.0), axis=1, keepdims=True)
            second = jnp.sum(jnp.where(low_half, 0.0, prod), axis=1, keepdims=True)
            at = HEAD_AT + 2 * p
            d_step = jnp.where(lane == at, first, jnp.where(lane == at + 1, second, d_step))
            dxs.append(d_xs * steps)
        dscores_ref[...] = d_scores
        dx = jnp.concatenate(dxs, axis=1) + cx[5:6] * dy
        skip_grad = jnp.sum(x * dy, axis=0, keepdims=True)
        d_x_pre = dx * (x_sig + x * (1.0 - x_sig))
        d_x_raw, conv_grad = taps_back(d_x_pre, x_raw, marks, cx)
        dproj_ref[j, :, 384:768] = d_x_raw.astype(bf16)
        rowid = lax.broadcasted_iota(jnp.int32, (8, 384), 0)
        gcx_ref[j] = jnp.where(rowid == 5, skip_grad, jnp.where(rowid == 6, norm_grad, conv_grad))
        d_cum = d_cum - d_cum_rows.T
        d_rate = sum(dot(causal.astype(bf16), part, ((0,), (0,))) for part in split3(d_cum))
        d_raw = (d_step - d_rate * hp_ref[j, 0:1]) * jax.nn.sigmoid(raw)
        dproj_ref[j, :, 768:896] = d_raw.astype(bf16)
        rowid = lax.broadcasted_iota(jnp.int32, (8, 128), 0)
        gheads_ref[j] = jnp.where(
            rowid == 0,
            jnp.sum(d_rate * rate, axis=0, keepdims=True),
            jnp.where(rowid == 1, jnp.sum(d_raw, axis=0, keepdims=True), 0.0),
        )

    @pl.when(i == 4)
    def _():
        marks = marks_ref[...]
        d_scores = dscores_ref[...].astype(bf16)
        d_bc = (dot(d_scores, bc_ref[1], ((0,), (0,))), dot(d_scores, bc_ref[0]))
        low_half = lanes((256, 128)) < 64
        for k in (0, 1):
            raw = bc_raw(proj_ref, k)
            pre = taps_pre(raw, marks, cbc_ref[k])
            sig = jax.nn.sigmoid(pre)
            d_pre = d_bc[k] * (sig + pre * sig * (1.0 - sig))
            d_raw, conv_grad = taps_back(d_pre, raw, marks, cbc_ref[k])
            gcbc_ref[k] = conv_grad
            for h, moved in enumerate((d_raw, roll(d_raw, 64, 1))):
                steps = dproj_ref[2 * k + h, :, 768:896].astype(f32)
                dproj_ref[2 * k + h, :, 768:896] = jnp.where(low_half, moved, steps).astype(bf16)
        dn_ref[...] = jnp.zeros_like(dn_ref)

    @pl.when(i >= 4)
    def _():
        j = i - 4
        d_proj = dproj_ref[j]
        fetch(j).wait()
        dn_ref[...] += dot(d_proj, w_ref[j], ((1,), (1,)))
        gin_ref[0, :, :768] = dot(normed_ref[...], d_proj[:, :768], ((0,), (0,))).astype(bf16)
        last = dot(normed_ref[...], d_proj[:, 768:], ((0,), (0,)))
        last = last + dot(ffn_ref[...], drout_ref[j], ((0,), (0,)))
        gin_ref[0, :, 768:] = last.astype(bf16)

    @pl.when(i == 7)
    def _():
        x = x_ref[...].astype(f32)
        total = jnp.sum(dn_ref[...] * x * rms(x), axis=0, keepdims=True)
        gnorm_ref[...] = jnp.broadcast_to(total, gnorm_ref.shape)


def mixer_backward(dm, kappa, w_out, w_in, normed, ffn_in, drout, proj, y, scaled, *rest):
    def late(i):
        return jnp.maximum(i - 4, 0)

    def early(i):
        return jnp.minimum(i, 3)

    small = [
        jax.ShapeDtypeStruct((256, 1536), f32),
        jax.ShapeDtypeStruct((4, 8, 384), f32),
        jax.ShapeDtypeStruct((2, 8, 128), f32),
        jax.ShapeDtypeStruct((4, 8, 128), f32),
        jax.ShapeDtypeStruct((8, 1536), f32),
    ]
    w_out_spec = pl.BlockSpec((4, 384, 384), lambda i: (0, early(i), 0))
    w_in_spec = pl.BlockSpec((1, 1536, 896), lambda i: (late(i), 0, 0))
    return pl.pallas_call(
        backward_kernel,
        grid=(8,),
        out_shape=[
            jax.ShapeDtypeStruct((4, 1536, 384), bf16),
            jax.ShapeDtypeStruct((4, 1536, 896), bf16),
            *small,
        ],
        in_specs=[
            fixed(dm),
            fixed(kappa),
            w_out_spec,
            pl.BlockSpec(memory_space=pl.ANY),
            *[fixed(v) for v in (normed, ffn_in, drout, proj)],
            *[pl.BlockSpec((1, 256, 384), lambda i: (early(i), 0, 0))] * 2,
            *[fixed(v) for v in rest],
        ],
        out_specs=[w_out_spec, w_in_spec, *[fixed(o) for o in small]],
        scratch_shapes=[
            pltpu.VMEM((4, 256, 896), bf16),
            pltpu.VMEM((256, 256), f32),
            pltpu.VMEM((256, 256), f32),
            pltpu.VMEM((2, 256, 128), bf16),
            pltpu.VMEM((4, 1536, 896), bf16),
            pltpu.SemaphoreType.DMA((4,)),
        ],
        compiler_params=pltpu.CompilerParams(vmem_limit_bytes=56 * 2**20),
        cost_estimate=pl.CostEstimate(
            flops=0, bytes_accessed=0, transcendentals=0
        ),
        name="mixer_backward",
    )(dm, kappa, w_out, w_in, normed, ffn_in, drout, proj, y, scaled, *rest)


def swap(v):
    return lax.ppermute(v, "seq", [(0, 1), (1, 0)])


def both_halves(own, other, s):
    first = jnp.where(s == 0, own, other)
    second = jnp.where(s == 0, other, own)
    return jnp.concatenate([first, second], axis=0)


def halves(v, s):
    rows = v.shape[0] // 2
    return (
        lax.dynamic_slice_in_dim(v, s * rows, rows, 0),
        lax.dynamic_slice_in_dim(v, (1 - s) * rows, rows, 0),
    )


def hi_lo(v):
    hi = v.astype(bf16)
    return hi, (v - hi.astype(f32)).astype(bf16)


def rms(v):
    return lax.rsqrt(jnp.mean(v * v, axis=-1, keepdims=True) + EPS)


def silu_grad(v):
    sig = jax.nn.sigmoid(v)
    return sig * (1.0 + v * (1.0 - sig))


def local(
    tokens,
    out_grad,
    lengths,
    routes,
    in_norm,
    in_proj,
    conv_weight,
    conv_bias,
    head_params,
    mixer_norm,
    out_proj,
    ffn_norm,
    router,
    shared_gate_up,
    shared_down,
    expert_gate_up,
    expert_down,
):
    s = lax.axis_index("seq")
    dp = lax.axis_index(DP)
    experts, slots = 64, 24
    n_slots = experts * slots

    other_tokens = swap(tokens)
    other_grad = swap(out_grad)
    other_gate_up = swap(expert_gate_up[0])
    other_down = swap(expert_down[0])
    w_in, w_sgu, w_out, w_sdown, vecs = gather(
        in_proj,
        shared_gate_up,
        router,
        jnp.concatenate([out_proj, shared_down], axis=0),
        (in_norm[None], ffn_norm[None], mixer_norm[None], conv_weight.T, conv_bias[None]),
    )
    w_in = w_in.reshape(4, 1536, 896)
    w_sgu = w_sgu.reshape(4, 1536, 256)
    w_out = w_out.reshape(4, 1536, 384)
    w_sdown = w_sdown.reshape(4, 512, 384)

    vecs = vecs.reshape(128, 16, 128).astype(f32)
    g_in = vecs[:, 0, :12].reshape(1, 1536)
    g_ffn = vecs[:, 1, :12].reshape(1536)
    g_mix = lax.dynamic_slice_in_dim(vecs[:, 2, :24].reshape(1, 3072), s * 1536, 1536, 1)
    conv = vecs[:, 3:8, :26].transpose(1, 0, 2).reshape(5, 3328)
    heads = lax.dynamic_slice_in_dim(head_params.astype(f32), s * 24, 24, 1)
    cx = jnp.concatenate(
        [
            lax.dynamic_slice_in_dim(conv[:, :3072], s * 1536, 1536, 1),
            jnp.broadcast_to(heads[2][:, None], (24, 64)).reshape(1, 1536),
            g_mix,
            jnp.zeros((1, 1536), f32),
        ],
        axis=0,
    )
    cx = cx.reshape(8, 4, 384).transpose(1, 0, 2)
    cbc = jnp.pad(conv[:, 3072:], ((0, 3), (0, 0))).reshape(8, 2, 128).transpose(1, 0, 2)
    hp = jnp.stack([jnp.exp(heads[0]), heads[1]]).reshape(2, 4, 6).transpose(1, 0, 2)
    hp = jnp.pad(hp, ((0, 0), (0, 6), (HEAD_AT, 122 - HEAD_AT)))
    w_eg = both_halves(expert_gate_up[0], other_gate_up, s)
    w_ed = both_halves(expert_down[0], other_down, s)

    ids = jnp.arange(experts, dtype=jnp.int32)
    named = jnp.sum((routes[:, :, None] == ids).astype(f32), axis=1)
    t128 = jnp.arange(128)
    before = (t128[:, None] > t128[None, :]).astype(bf16)
    rank = dot(before, named.astype(bf16))
    slot = jnp.arange(n_slots, dtype=jnp.int32)
    spread = (slot[None, :] // slots == ids[:, None]).astype(bf16)
    is_named = dot(named.astype(bf16), spread) > 0.5
    in_slot = dot(rank.astype(bf16), spread) == (slot % slots).astype(f32)[None, :]
    place = (is_named & in_slot).astype(bf16)

    def to_slots(v):
        return dot(place, v, ((0,), (0,))).astype(bf16).reshape(experts, slots, v.shape[1])

    grad_slots, w_in = lax.optimization_barrier((to_slots(out_grad), w_in))
    grad_rows = lax.all_to_all(grad_slots, DP, 0, 0, tiled=True).reshape(n_slots, 1536)

    ends = jnp.cumsum(lengths[0])
    t256 = jnp.arange(256, dtype=jnp.int32)
    segment = jnp.sum((t256[:, None] >= ends[None, :]).astype(jnp.int32), axis=1)
    seg = segment.astype(f32)
    same = [
        (jnp.pad(segment, (d, 0), constant_values=-1)[:256] == segment).astype(f32)
        for d in range(4)
    ]
    marks = jnp.pad(jnp.stack(same + [seg], axis=1), ((0, 0), (0, 123)))
    seg = jnp.broadcast_to(seg, (8, 256))
    x_full = both_halves(tokens, other_tokens, s)
    normed, proj, y, scaled, part, squares = mixer_forward(
        x_full, jnp.broadcast_to(g_in, (8, 1536)), w_in, w_out, cx, cbc, hp, marks, seg
    )
    squares = squares[:, :1]
    part_own, part_other = halves(part, s)
    sq_own, sq_other = halves(squares, s)
    part = part_own + swap(part_other)
    q = lax.rsqrt((sq_own + swap(sq_other)) / 3072.0 + EPS)
    residual = tokens.astype(f32) + q * part

    r = rms(residual)
    ffn_in = (residual * r * g_ffn).astype(bf16)
    w_router = w_in[:, :, 832:848].transpose(1, 0, 2).reshape(1536, 64)
    logits = dot(ffn_in, w_router)
    logits = jnp.where(named > 0.5, logits, -1e30)
    top = jnp.max(logits, axis=1, keepdims=True)
    weights = jnp.where(named > 0.5, jnp.exp(logits - top), 0.0)
    gating = weights / jnp.sum(weights, axis=1, keepdims=True)
    gate_hi, gate_lo = hi_lo(gating)
    sent = to_slots(jnp.concatenate([ffn_in, gate_hi, gate_lo], axis=1))
    sent, grad_rows = lax.optimization_barrier((sent, grad_rows))
    arrived = lax.all_to_all(sent, DP, 0, 0, tiled=True).reshape(n_slots, 1664)

    ffn_full = both_halves(ffn_in, swap(ffn_in), s)
    og_full = both_halves(out_grad, other_grad, s)
    sgu = jnp.stack([dot(ffn_full, w_sgu[j]) for j in range(4)])
    sg, su = sgu[..., :128], sgu[..., 128:]
    s_act = (jax.nn.silu(sg) * su).astype(bf16)
    s_flat = s_act.transpose(1, 0, 2).reshape(256, 512)
    s_out = jnp.concatenate([dot(s_flat, w_sdown[j]) for j in range(4)], axis=1)
    s_own, s_other = halves(s_out, s)
    s_out = s_own + swap(s_other.astype(bf16)).astype(f32)
    og_cols = og_full.reshape(256, 4, 384).transpose(1, 0, 2)
    d_s_act = sum(dot(og_cols[j], w_sdown[j], ((1,), (1,))) for j in range(4))
    d_s_act = d_s_act.reshape(256, 4, 128).transpose(1, 0, 2)
    d_sgu = jnp.concatenate([d_s_act * su * silu_grad(sg), d_s_act * jax.nn.silu(sg)], axis=-1)
    d_sgu = d_sgu.astype(bf16)
    grad_sdown = jnp.stack([dot(s_flat, og_cols[j], ((0,), (0,))) for j in range(4)]).astype(bf16)
    grad_sgu = jnp.stack([dot(ffn_full, d_sgu[j], ((0,), (0,))) for j in range(4)]).astype(bf16)
    d_ffn = sum(dot(d_sgu[j], w_sgu[j], ((1,), (1,))) for j in range(4))
    df_own, df_other = halves(d_ffn, s)
    d_ffn = df_own + swap(df_other.astype(bf16)).astype(f32)

    lane = jnp.arange(128, dtype=jnp.int32) % 64
    pick = (lane == dp).astype(f32)[None, :]
    d_rows, e_act, w_act, w_gu = expert_grads(arrived, grad_rows, w_eg, w_ed, pick)
    d_back = lax.all_to_all(d_rows.reshape(experts, slots, 1664), DP, 0, 0, tiled=True)
    e_out = dot(e_act, w_ed).astype(bf16)
    grad_ed = dot(w_act, grad_rows, ((0,), (0,)))
    grad_eg = dot(arrived[:, :1536], w_gu, ((0,), (0,)))
    ge_own, ge_other = halves(grad_eg, s)
    grad_eg = ge_own + swap(ge_other.astype(bf16)).astype(f32)
    gd_own, gd_other = halves(grad_ed, s)
    grad_ed = gd_own + swap(gd_other.astype(bf16)).astype(f32)
    e_out, d_back, grad_eg, grad_ed, d_ffn, grad_sgu, grad_sdown = lax.optimization_barrier(
        (e_out, d_back, grad_eg, grad_ed, d_ffn, grad_sgu, grad_sdown)
    )
    d_back = d_back.reshape(n_slots, 1664)
    out_back = lax.all_to_all(e_out.reshape(experts, slots, 1536), DP, 0, 0, tiled=True)
    out_back = out_back.reshape(n_slots, 1536)

    wide_gate = dot(gate_hi, spread) + dot(gate_lo, spread)
    weighted = (place.astype(f32) * wide_gate).astype(bf16)
    d_route = dot(weighted, d_back[:, :1536])
    dg = d_back[:, 1536:1538].T
    d_gating = dot(place * dg[0:1], spread, ((1,), (1,))) + dot(
        place * dg[1:2], spread, ((1,), (1,))
    )
    d_logits = gating * (d_gating - jnp.sum(gating * d_gating, axis=1, keepdims=True))
    d_logits_low = d_logits.astype(bf16)
    d_ffn = d_ffn + dot(d_logits_low, w_router, ((1,), (1,))) + d_route
    ffn_norm_grad = jnp.sum(d_ffn * residual * r, axis=0)
    u = d_ffn * g_ffn
    d_residual = (
        out_grad.astype(f32)
        + r * u
        - r * r * r * residual * jnp.mean(u * residual, axis=1, keepdims=True)
    )

    d_mixed = (q * d_residual).astype(bf16)
    kappa = q * q / 3072.0 * jnp.sum(d_mixed.astype(f32) * part, axis=1, keepdims=True)
    d_mixed_full = both_halves(d_mixed, swap(d_mixed), s)
    kappa = both_halves(kappa, swap(kappa), s)
    drout = jnp.pad(d_logits_low.reshape(128, 4, 16).transpose(1, 0, 2), ((0, 0), (0, 0), (64, 48)))
    grad_out, grad_in, d_normed, g_cx, g_cbc, g_heads, in_norm_grad = mixer_backward(
        d_mixed_full, kappa, w_out, w_in, normed, ffn_in, drout, proj, y, scaled, cx, cbc, hp, marks, seg, x_full
    )
    conv_x_grad = g_cx[:, :5].transpose(1, 0, 2).reshape(5, 1536)
    conv_bc_grad = g_cbc[:, :5].transpose(1, 0, 2).reshape(5, 256)
    mixer_norm_grad = g_cx[:, 6].reshape(1536)
    head_grad = g_heads[:, :2, HEAD_AT : HEAD_AT + 6].transpose(1, 0, 2).reshape(2, 24)
    d_skip = jnp.sum(g_cx[:, 5].reshape(24, 64), axis=1)
    head_grad = jnp.concatenate([head_grad, d_skip[None]], axis=0)
    dn_own, dn_other = halves(d_normed, s)
    dn_other = swap(dn_other.astype(bf16))

    conv_grad = lax.dynamic_update_slice(
        jnp.zeros((5, 3328), f32), conv_x_grad, (0, s * 1536)
    )
    conv_grad = lax.dynamic_update_slice(conv_grad, conv_bc_grad, (0, 3072))
    mixer_norm_grad = lax.dynamic_update_slice(
        jnp.zeros((128, 24), f32), mixer_norm_grad.reshape(64, 24), (s * 64, 0)
    )
    head_grad = lax.dynamic_update_slice(jnp.zeros((3, 48), f32), head_grad, (0, s * 24))
    def rows_of(v, width):
        return jnp.pad(v.reshape(128, 1, width), ((0, 0), (0, 0), (0, 64 - width)))

    conv_grad = conv_grad.reshape(5, 128, 26).transpose(1, 0, 2)
    small = jnp.concatenate(
        [
            rows_of(in_norm_grad[0], 12),
            rows_of(ffn_norm_grad, 12),
            rows_of(mixer_norm_grad, 24),
            jnp.pad(conv_grad, ((0, 0), (0, 0), (0, 38))),
        ],
        axis=1,
    )
    head_rows = jnp.broadcast_to(jnp.pad(head_grad, ((0, 5), (0, 16)))[None], (128, 8, 64))
    small = jnp.concatenate([small, head_rows], axis=2).reshape(2, 4, 4, 4, 8, 128)
    sums = scatter(
        (
            grad_in.reshape(4, 2, 4, 4, 48, 896),
            grad_sgu.reshape(4, 2, 4, 4, 48, 256),
            grad_out.reshape(4, 4, 4, 2, 48, 384),
            grad_sdown.reshape(4, 4, 4, 2, 16, 384),
            small,
        )
    )
    weighted_late, dn_own, sums = lax.optimization_barrier((weighted, dn_own, tuple(sums)))
    routed = dot(weighted_late, out_back)
    block_out = (residual + s_out + routed).astype(bf16)
    d_normed = dn_own + dn_other.astype(f32)
    x_own = tokens.astype(f32)
    p = rms(x_own)
    v = d_normed * g_in
    token_grad = (
        d_residual + p * v - p * p * p * x_own * jnp.mean(v * x_own, axis=1, keepdims=True)
    ).astype(bf16)
    (
        in_proj_grad, router_grad, sgu_grad, out_proj_grad, sdown_grad, head_grad, conv_grad,
        in_norm_grad, ffn_norm_grad, mixer_norm_grad, conv_bias_grad,
    ) = finish(*sums)
    return (
        block_out,
        token_grad,
        in_norm_grad[0],
        in_proj_grad,
        conv_grad,
        conv_bias_grad[0],
        head_grad,
        mixer_norm_grad[0],
        out_proj_grad,
        ffn_norm_grad[0],
        router_grad,
        sgu_grad,
        sdown_grad,
        grad_eg[None],
        grad_ed[None],
    )


def solution(mesh):
    finer = Mesh(mesh.devices.reshape(2, 4, 4, 4), ALL)
    placed = (
        P(DP_SEQ, None),
        P(DP_SEQ, None),
        P(DP, None),
        P(DP_SEQ, None),
        P(ALL),
        P(ALL, None),
        P(ALL, None),
        P(ALL),
        P(),
        P(ALL),
        P(ALL, None),
        P(ALL),
        P(ALL, None),
        P(ALL, None),
        P(ALL, None),
        P(DP, "seq", None),
        P(DP, "seq", None),
    )
    return jax.shard_map(
        local,
        mesh=finer,
        in_specs=placed,
        out_specs=(
            P(DP_SEQ, None),
            P(DP_SEQ, None),
            P(ALL),
            P(ALL, None),
            P(ALL, None),
            P(ALL),
            P(),
            P(ALL),
            P(ALL, None),
            P(ALL),
            P(ALL, None),
            P(ALL, None),
            P(ALL, None),
            P(DP, "seq", None),
            P(DP, "seq", None),
        ),
        check_vma=False,
    )
```

```python
import functools

import jax
import jax.numpy as jnp
import numpy as np
from jax import lax
from jax.experimental import pallas as pl
from jax.experimental.pallas import tpu as pltpu
from jax.sharding import Mesh
from jax.sharding import PartitionSpec as P

DP = ("z", "x", "y")
ALL = ("seq", "z", "x", "y")
DP_SEQ = ("z", "x", "y", "seq")
ORDER = (("z", "x", "y"), ("x", "y", "z"), ("y", "z", "x"))
REM = (("z", "x"), ("y", "x"), ("y", "z"))
MESH_ID = pl.DeviceIdType.MESH
EPS = 1e-05
f32 = jnp.float32
bf16 = jnp.bfloat16

ROWS_FIRST = (("y", "s", "z", "x"), "rows")
CHANNELS = (("y", "z", "x", "s"), "cols")
VECTORS = (("s", "z", "x", "y"), "one")
SPECS = (ROWS_FIRST, ROWS_FIRST, CHANNELS, CHANNELS, VECTORS)
HEAD_AT = 80
SIZES = {"y": 4, "z": 4, "x": 4, "s": 2}


def dot(a, b, dims=((1,), (0,))):
    return lax.dot_general(a, b, (dims, ((), ())), preferred_element_type=f32)


def neighbours():
    pos = {a: lax.axis_index(a) for a in DP}
    right = {a: lax.rem(pos[a] + 1, 4) for a in DP}
    left = {a: lax.rem(pos[a] + 3, 4) for a in DP}
    opp = {a: lax.rem(pos[a] + 2, 4) for a in DP}
    return pos, right, left, opp


def chip_row():
    core, y = lax.axis_index("seq"), lax.axis_index("y")
    return [(lax.rem(core + c, 2), lax.rem(y + d, 4)) for c in range(2) for d in range(4)]


def greet(right, left, opp):
    barrier = pltpu.get_barrier_semaphore()

    def signal(device_id):
        pl.semaphore_signal(barrier, inc=1, device_id=device_id, device_id_type=MESH_ID)

    for a in ("z", "x"):
        signal({a: right[a]})
        signal({a: left[a]})
        signal({a: opp[a]})
    for core, y in chip_row()[1:]:
        signal({"seq": core, "y": y})


def met(count):
    pl.semaphore_wait(pltpu.get_barrier_semaphore(), count)


def cuts(spec):
    return range(1 if spec[1] == "one" else 3)


def third(shape, split, a):
    rows, cols = shape[-2:]
    if split == "one":
        return (slice(None), slice(None))
    if split == "rows":
        return (pl.ds(rows // 3 * a, rows // 3), slice(None))
    return (slice(None), pl.ds(cols // 3 * a, cols // 3))


def third_shape(shape, split):
    rows, cols = shape[-2:]
    return {"one": (rows, cols), "rows": (rows // 3, cols), "cols": (rows, cols // 3)}[split]


def region(ref, spec, free, fixed, a, s=None):
    order, split = spec
    ix = []
    for d in order:
        if d == "s":
            ix.append(slice(None) if s is None else s)
        else:
            ix.append(slice(None) if d in free else fixed[d])
    return ref.at[tuple(ix) + third(ref.shape, split, a)]


def roll(v, by, axis):
    by = by % v.shape[axis]
    return pltpu.roll(v, by, axis) if by else v


def lanes(shape):
    return lax.broadcasted_iota(jnp.int32, shape, len(shape) - 1)


def moved(v, at, to, width):
    lane = lanes(v.shape)
    return jnp.where((lane >= to) & (lane < to + width), roll(v, to - at, 1), 0.0)


def gather_kernel(in_ref, gu_ref, router_ref, rows_ref, *refs):
    specs, n = SPECS, len(SPECS)
    vec_refs, outs, blocks = refs[:5], refs[5 : 5 + n], refs[5 + n : 5 + 2 * n]
    pin, pout, bin_, bout, wide, vec, send0, recv0, send, recv, loc = refs[5 + 2 * n :]
    pos, right, left, opp = neighbours()
    row = chip_row()
    (core, y) = row[0]
    greet(right, left, opp)
    wide[...] = jnp.zeros_like(wide)
    wide[0, :12, :48] = in_ref[:, 6400:].astype(f32)
    wide[1, :12, :64] = router_ref[...].astype(f32)
    at = 0
    for v in vec_refs:
        wide[2, at : at + v.shape[0], : v.shape[1]] = v[...].astype(f32)
        at += v.shape[0]
    vec[...] = wide[2].astype(bf16)
    bc = [in_ref[:, 6144 + 128 * k : 6272 + 128 * k].astype(f32) for k in range(2)]
    steps, router = wide[0, :12], wide[1, :12]
    for c in range(2):
        for j in range(4):
            k, at = 4 * c + j, c * 1536 + j * 384
            misc = (
                moved(bc[j // 2], 64 * (j % 2), 0, 64)
                + moved(router, 16 * j, 64, 16)
                + moved(steps, 24 * c + 6 * j, HEAD_AT, 6)
            )
            pin[k, :12, :384] = in_ref[:, at : at + 384]
            pin[k, :12, 384:768] = in_ref[:, 3072 + at : 3456 + at]
            pin[k, :12, 768:896] = misc.astype(bf16)
            pin[k, :12, 896:1024] = gu_ref[:, 128 * k : 128 * k + 128]
            pin[k, :12, 1024:] = gu_ref[:, 1024 + 128 * k : 1152 + 128 * k]
    for j in range(4):
        pout[j] = rows_ref[:, 384 * j : 384 * j + 384]
    met(13)
    sends, first = [], []

    def push(src, dst, k, device_id):
        c = pltpu.make_async_remote_copy(
            src_ref=src,
            dst_ref=dst,
            send_sem=send0.at[k],
            recv_sem=recv0.at[k],
            device_id=device_id,
            device_id_type=MESH_ID,
        )
        c.start()
        sends.append(c)
        first.append(c)

    for k, (c, d) in enumerate(row):
        if k:
            push(pin.at[4 * c + d], bin_.at[4 * core + y], k, {"seq": c, "y": d})
    for k, (_, d) in enumerate(row[:4]):
        if k:
            push(pout.at[d], bout.at[y], 8 + k, {"y": d})
    push(vec, blocks[4].at[core], 0, {"seq": 1 - core})
    blocks[4][core] = vec[...]
    bin_[4 * core + y] = pin[4 * core + y]
    bout[y] = pout[y]
    for c in first:
        c.wait_recv()
    for c in range(2):
        v = jnp.concatenate([bin_[4 * c + d].astype(f32)[:12] for d in range(4)], axis=0)
        blocks[0][c] = v[:, :896].astype(bf16)
        blocks[1][c] = v[:, 896:].astype(bf16)
    v = [bout[d].astype(f32) for d in range(4)]
    for h in range(2):
        blocks[2][h] = jnp.concatenate([v[2 * h][:24], v[2 * h + 1][:24]], axis=0).astype(bf16)
        blocks[3][h] = jnp.concatenate([v[2 * h][24:], v[2 * h + 1][24:]], axis=0).astype(bf16)

    own = []
    for i in range(n):
        ix = tuple(slice(None) if d == "s" else pos[d] for d in specs[i][0])
        c = pltpu.make_async_copy(blocks[i], outs[i].at[ix], loc.at[i])
        c.start()
        own.append(c)

    def remote(i, st, a, k, src, dst, ax, to):
        c = pltpu.make_async_remote_copy(
            src_ref=src,
            dst_ref=dst,
            send_sem=send.at[i, st, a, k],
            recv_sem=recv.at[i, st, a, k],
            device_id={ax: to},
            device_id_type=MESH_ID,
        )
        c.start()
        sends.append(c)
        return c

    every = [(i, a) for i in range(n) for a in cuts(specs[i])]
    first, later = {}, {}

    def begin(i, a, st):
        ax, free = ORDER[a][st], ORDER[a][:st]
        dst = region(outs[i], specs[i], free, pos, a)
        src = dst
        if st == 0:
            src = blocks[i].at[(slice(None),) + third(blocks[i].shape, specs[i][1], a)]
        for d, to in enumerate((right[ax], left[ax])):
            first[i, a, d] = remote(i, st, a, d, src, dst, ax, to)
        if st == 0:
            later[i, a, 0] = remote(i, st, a, 2, src, dst, ax, opp[ax])

    for i, a in every:
        begin(i, a, 0)
    for c in own:
        c.wait()
    for st in range(3):
        for i, a in every:
            ax, free = ORDER[a][st], ORDER[a][:st]
            for d, (to, frm) in enumerate(((right[ax], left[ax]), (left[ax], right[ax]))):
                first[i, a, d].wait_recv()
                if st:
                    r = region(outs[i], specs[i], free, {**pos, ax: frm}, a, s=d)
                    later[i, a, d] = remote(i, st, a, 2 + d, r, r, ax, to)
        for i, a in every:
            for d in range(2 if st else 1):
                later[i, a, d].wait_recv()
            if st < 2:
                begin(i, a, st + 1)
    for c in sends:
        c.wait_send()


def gather(in_proj, gate_up, router, rows, vectors):
    n = len(SPECS)
    blocks = [(2, 48, 896), (2, 48, 256), (2, 48, 384), (2, 16, 384), (2, 16, 128)]
    outs = [
        jax.ShapeDtypeStruct(tuple(SIZES[d] for d in spec[0]) + v[1:], bf16)
        for v, spec in zip(blocks, SPECS)
    ]
    total = sum(int(np.prod(o.shape)) for o in outs) * 2
    return pl.pallas_call(
        gather_kernel,
        out_shape=outs,
        in_specs=[pl.BlockSpec(memory_space=pltpu.VMEM)] * 9,
        out_specs=[pl.BlockSpec(memory_space=pl.ANY)] * n,
        scratch_shapes=[pltpu.VMEM(v, bf16) for v in blocks]
        + [
            pltpu.VMEM((8, 16, 1152), bf16),
            pltpu.VMEM((4, 32, 384), bf16),
            pltpu.VMEM((8, 16, 1152), bf16),
            pltpu.VMEM((4, 32, 384), bf16),
            pltpu.VMEM((3, 16, 128), f32),
            pltpu.VMEM((16, 128), bf16),
            pltpu.SemaphoreType.DMA((12,)),
            pltpu.SemaphoreType.DMA((12,)),
            pltpu.SemaphoreType.DMA((n, 3, 3, 4)),
            pltpu.SemaphoreType.DMA((n, 3, 3, 4)),
            pltpu.SemaphoreType.DMA((n,)),
        ],
        compiler_params=pltpu.CompilerParams(
            collective_id=1, has_side_effects=True, vmem_limit_bytes=60 * 2**20
        ),
        cost_estimate=pl.CostEstimate(flops=0, bytes_accessed=2 * total, transcendentals=0),
        name="gather_weights",
    )(in_proj, gate_up, router, rows, *vectors)


def each(lead, fn):
    @pl.loop(0, int(np.prod(lead)))
    def _(i):
        ix = []
        for d in reversed(lead):
            ix.append(lax.rem(i, d))
            i = lax.div(i, d)
        fn(tuple(reversed(ix)))


def scatter_kernel(*refs):
    specs, n = SPECS, len(SPECS)
    gs, (bin_, bout, small_out) = refs[:n], refs[n : n + 3]
    outs, refs = refs[n + 3 : 2 * n + 3], refs[2 * n + 3 :]
    held, got = refs[:n], [refs[n + 3 * i : n + 3 * i + 3] for i in range(n)]
    pin, pout, other, send0, recv0, send, recv, loc = refs[4 * n :]
    pos, right, left, opp = neighbours()
    row = chip_row()
    (core, y) = row[0]

    def source(i, st, a, idx, s):
        ax = ORDER[a][2 - st]
        if st == 0:
            return region(gs[i], specs[i], [d for d in DP if d != ax], {ax: idx}, a, s)
        part = held[i].at[a, 2 + s]
        if st == 1:
            return part.at[:, idx] if REM[a][1] == ax else part.at[idx]
        me = pos[ORDER[a][1]]
        return part.at[me, idx] if REM[a][1] == ax else part.at[idx, me]

    local = {}
    for i in range(n):
        for a in cuts(specs[i]):
            ax = ORDER[a][2]
            for k, (idx, s) in enumerate(((right[ax], 0), (left[ax], 1), (pos[ax], 0), (pos[ax], 1))):
                c = pltpu.make_async_copy(source(i, 0, a, idx, s), held[i].at[a, k], loc.at[i, a, k])
                c.start()
                local[i, a, k] = c
    greet(right, left, opp)
    met(13)
    sends = []

    def remote(i, st, a, k, src, ax, to):
        c = pltpu.make_async_remote_copy(
            src_ref=src,
            dst_ref=got[i][st].at[a, k],
            send_sem=send.at[i, st, a, k],
            recv_sem=recv.at[i, st, a, k],
            device_id={ax: to},
            device_id_type=MESH_ID,
        )
        c.start()
        sends.append(c)
        return c

    every = [(i, a) for i in range(n) for a in cuts(specs[i])]
    cp = {}

    def begin(i, a, st):
        ax = ORDER[a][2 - st]
        if st == 2:
            for k, to in enumerate((opp[ax], right[ax], left[ax])):
                for s in range(2):
                    cp[i, a, 2 * k + s] = remote(i, st, a, 2 * k + s, source(i, st, a, to, s), ax, to)
            return
        cp[i, a, 0] = remote(i, st, a, 0, source(i, st, a, opp[ax], 0), ax, right[ax])
        cp[i, a, 1] = remote(i, st, a, 1, source(i, st, a, opp[ax], 1), ax, left[ax])
        if st:
            direct(i, a, st)

    def direct(i, a, st):
        ax = ORDER[a][2 - st]
        cp[i, a, 2] = remote(i, st, a, 2, source(i, st, a, right[ax], 1), ax, right[ax])
        cp[i, a, 3] = remote(i, st, a, 3, source(i, st, a, left[ax], 0), ax, left[ax])

    for i, a in every:
        begin(i, a, 0)
    for i, a in every:
        direct(i, a, 0)
    for st in range(2):
        lead = ((4, 4), (4,))[st]
        for i, a in every:
            ax = ORDER[a][2 - st]
            for d, to in enumerate((right[ax], left[ax])):
                cp[i, a, d].wait_recv()
                if st == 0:
                    local[i, a, d].wait()
                    acc = held[i].at[a, d]
                else:
                    acc = source(i, st, a, to, d)
                more = got[i][st].at[a, d]

                def add(ix, acc=acc, more=more):
                    acc[ix] = (acc[ix].astype(f32) + more[ix].astype(f32)).astype(acc.dtype)

                each(lead, add)
                cp[i, a, 4 + d] = remote(i, st, a, 4 + d, acc, ax, to)
        for i, a in every:
            ax = ORDER[a][2 - st]
            if st == 0:
                local[i, a, 2].wait()
                local[i, a, 3].wait()
            for s, (p, q) in enumerate(((4, 3), (2, 5))):
                cp[i, a, p].wait_recv()
                cp[i, a, q].wait_recv()
                acc = held[i].at[a, 2 + s] if st == 0 else source(i, st, a, pos[ax], s)
                one, two = got[i][st].at[a, p], got[i][st].at[a, q]

                def close(ix, acc=acc, one=one, two=two):
                    total = acc[ix].astype(f32) + one[ix].astype(f32) + two[ix].astype(f32)
                    acc[ix] = total.astype(acc.dtype)

                each(lead, close)
            begin(i, a, st + 1)
    for i, a in every:
        ax = ORDER[a][0]
        for s in range(2):
            total = source(i, 2, a, pos[ax], s)[...].astype(f32)
            for k in range(3):
                cp[i, a, 2 * k + s].wait_recv()
                total = total + got[i][2][a, 2 * k + s].astype(f32)
            outs[i][(s,) + third(outs[i].shape, specs[i][1], a)] = total

    for k in range(8):
        c, d = divmod(k, 4)
        pin[k, :12, :896] = outs[0][c, 12 * d : 12 * d + 12, :]
        pin[k, :12, 896:] = outs[1][c, 12 * d : 12 * d + 12, :]
    for d in range(4):
        h, at = divmod(d, 2)
        pout[d, :24] = outs[2][h, 24 * at : 24 * at + 24, :]
        pout[d, 24:] = outs[3][h, 8 * at : 8 * at + 8, :]
    last = []

    def push(src, dst, k, device_id):
        c = pltpu.make_async_remote_copy(
            src_ref=src,
            dst_ref=dst,
            send_sem=send0.at[k],
            recv_sem=recv0.at[k],
            device_id=device_id,
            device_id_type=MESH_ID,
        )
        c.start()
        sends.append(c)
        last.append(c)

    for k, (c, d) in enumerate(row):
        if k:
            push(pin.at[4 * c + d], bin_.at[4 * core + y], k, {"seq": c, "y": d})
    for k, (_, d) in enumerate(row[:4]):
        if k:
            push(pout.at[d], bout.at[y], 8 + k, {"y": d})
    push(outs[4].at[1 - core], other, 0, {"seq": 1 - core})
    bin_[4 * core + y] = pin[4 * core + y]
    bout[y] = pout[y]
    for c in last:
        c.wait_recv()
    small_out[...] = outs[4][core] + other[...]
    for c in sends:
        c.wait_send()


def finish_kernel(bin_, bout, small, in_out, router_out, gu_out, out_out, down_out, heads_out, taps_out, *vecs):
    misc = []
    for k in range(8):
        got_k = bin_[k]
        in_out[:, 384 * k : 384 * k + 384] = got_k[:12, :384]
        in_out[:, 3072 + 384 * k : 3456 + 384 * k] = got_k[:12, 384:768]
        gu_out[:, 128 * k : 128 * k + 128] = got_k[:12, 896:1024]
        gu_out[:, 1024 + 128 * k : 1152 + 128 * k] = got_k[:12, 1024:]
        misc.append(got_k[:, 768:896])
    both = [misc[j] + misc[4 + j] for j in range(4)]
    for h in range(2):
        pair = moved(both[2 * h], 0, 0, 64) + moved(both[2 * h + 1], 0, 64, 64)
        in_out[:, 6144 + 128 * h : 6272 + 128 * h] = pair[:12]
    steps = sum(moved(misc[k], HEAD_AT, 6 * k, 6) for k in range(8))
    in_out[:, 6400:] = steps[:12, :48]
    router = sum(moved(both[j], 64, 16 * j, 16) for j in range(4))
    router_out[...] = router[:12, :64]
    for j in range(4):
        out_out[:, 384 * j : 384 * j + 384] = bout[j, :24]
        down_out[:, 384 * j : 384 * j + 384] = bout[j, 24:]
    heads_out[...] = moved(small[...], 64, 0, 48)[:3, :48]
    taps_out[...] = jnp.concatenate([small[...]] * 16, axis=0).T[:26, 3:7]
    for v, at in zip(vecs, (0, 1, 2, 7)):
        v[...] = small[at : at + 1, : v.shape[1]]


def finish(bin_, bout, small):
    results = [(12, 6448), (12, 64), (12, 2048), (24, 1536), (8, 1536), (3, 48), (26, 4)]
    results += [(1, 12), (1, 12), (1, 24), (1, 26)]
    return pl.pallas_call(
        finish_kernel,
        out_shape=[jax.ShapeDtypeStruct(v, f32) for v in results],
        in_specs=[pl.BlockSpec(memory_space=pltpu.VMEM)] * 3,
        out_specs=[pl.BlockSpec(memory_space=pltpu.VMEM)] * len(results),
        name="finish_grads",
    )(bin_, bout, small)


def scatter(arrays):
    n = len(arrays)
    results = [(8, 16, 1152), (4, 32, 384), (8, 128)]
    pieces = [(third_shape(v.shape, spec[1]), v.dtype) for v, spec in zip(arrays, SPECS)]
    cut = [len(cuts(spec)) for spec in SPECS]
    return pl.pallas_call(
        scatter_kernel,
        out_shape=[jax.ShapeDtypeStruct(v, f32) for v in results],
        in_specs=[pl.BlockSpec(memory_space=pl.ANY)] * n,
        out_specs=[pl.BlockSpec(memory_space=pltpu.VMEM)] * len(results),
        scratch_shapes=[pltpu.VMEM((2,) + v.shape[4:], f32) for v in arrays]
        + [pltpu.VMEM((k, 4, 4, 4) + p, t) for k, (p, t) in zip(cut, pieces)]
        + [
            pltpu.VMEM((k, 6) + lead + p, t)
            for k, (p, t) in zip(cut, pieces)
            for lead in ((4, 4), (4,), ())
        ]
        + [
            pltpu.VMEM((8, 16, 1152), f32),
            pltpu.VMEM((4, 32, 384), f32),
            pltpu.VMEM((8, 128), f32),
            pltpu.SemaphoreType.DMA((12,)),
            pltpu.SemaphoreType.DMA((12,)),
            pltpu.SemaphoreType.DMA((n, 3, 3, 6)),
            pltpu.SemaphoreType.DMA((n, 3, 3, 6)),
            pltpu.SemaphoreType.DMA((n, 3, 4)),
        ],
        compiler_params=pltpu.CompilerParams(
            collective_id=2, has_side_effects=True, vmem_limit_bytes=56 * 2**20
        ),
        cost_estimate=pl.CostEstimate(flops=0, bytes_accessed=0, transcendentals=0),
        name="scatter_grads",
    )(*arrays)


def expert_kernel(rows_ref, grad_ref, gu_ref, down_ref, pick_ref, back_ref, act_ref, wact_ref, wgu_ref):
    for at in range(0, rows_ref.shape[0], 256):
        part = pl.ds(at, 256)
        e_gu = dot(rows_ref[part, :1536], gu_ref[...])
        d_act = dot(grad_ref[part, :], down_ref[...], ((1,), (1,)))
        eg, eu = e_gu[:, :512], e_gu[:, 512:]
        sig = jax.nn.sigmoid(eg)
        silu = eg * sig
        act32 = silu * eu
        act = act32.astype(bf16)
        slot_gate = jnp.sum(rows_ref[part, 1536:].astype(f32) * pick_ref[...], axis=1, keepdims=True)
        d_gate = jnp.sum(act.astype(f32) * d_act, axis=1, keepdims=True)
        d_eg = d_act * eu * (sig + silu * (1.0 - sig))
        d_eu = d_act * silu
        d_gu = jnp.concatenate([d_eg.astype(bf16), d_eu.astype(bf16)], axis=1)
        back_ref[part, :1536] = dot(d_gu, gu_ref[...], ((1,), (1,))).astype(bf16)
        hi = d_gate.astype(bf16).astype(f32)
        lane = lanes((256, 128))
        tail = jnp.where(lane == 0, hi, jnp.where(lane == 1, d_gate - hi, 0.0))
        back_ref[part, 1536:] = tail.astype(bf16)
        act_ref[part, :] = act
        wact_ref[part, :] = (act32 * slot_gate).astype(bf16)
        wgu_ref[part, :512] = (d_eg * slot_gate).astype(bf16)
        wgu_ref[part, 512:] = (d_eu * slot_gate).astype(bf16)


def expert_grads(rows, grad_rows, gate_up, down, pick):
    n, block = rows.shape[0], 512
    widths = (1664, 512, 512, 1024)

    def blocked(w):
        return pl.BlockSpec((block, w), lambda i: (i, 0))

    def whole(v):
        return pl.BlockSpec(v.shape, lambda i: (0, 0))

    return pl.pallas_call(
        expert_kernel,
        grid=(n // block,),
        out_shape=[jax.ShapeDtypeStruct((n, w), bf16) for w in widths],
        in_specs=[blocked(1664), blocked(1536), whole(gate_up), whole(down), whole(pick)],
        out_specs=[blocked(w) for w in widths],
        compiler_params=pltpu.CompilerParams(vmem_limit_bytes=48 * 2**20),
        cost_estimate=pl.CostEstimate(
            flops=2 * n * 1536 * (1024 + 512 + 1024), bytes_accessed=26 * 2**20, transcendentals=0
        ),
        name="expert_grads",
    )(rows, grad_rows, gate_up, down, pick)


def split3(v):
    hi = v.astype(bf16)
    rest = v - hi.astype(f32)
    mid = rest.astype(bf16)
    return hi, mid, (rest - mid.astype(f32)).astype(bf16)


def taps_pre(v, marks, w):
    total = w[4:5] + w[3:4] * v
    for d in (1, 2, 3):
        total = total + w[3 - d : 4 - d] * (roll(v, d, 0) * marks[:, d : d + 1])
    return total


def taps_back(d_pre, v, marks, w):
    d_v = w[3:4] * d_pre
    d_w = [jnp.sum(d_pre * v, axis=0, keepdims=True)]
    for d in (1, 2, 3):
        masked = d_pre * marks[:, d : d + 1]
        d_w.insert(0, jnp.sum(masked * roll(v, d, 0), axis=0, keepdims=True))
        d_v = d_v + w[3 - d : 4 - d] * roll(masked, 256 - d, 0)
    zero = jnp.zeros((3, v.shape[1]), f32)
    return d_v, jnp.concatenate(d_w + [jnp.sum(d_pre, axis=0, keepdims=True), zero], axis=0)


def joined(first, second):
    return jnp.where(lanes(first.shape) < 64, first, roll(second, 64, 1))


def bc_raw(proj_ref, k):
    return joined(
        proj_ref[2 * k, :, 768:896].astype(f32), proj_ref[2 * k + 1, :, 768:896].astype(f32)
    )


def head_steps(proj_ref, hp_ref, j, tri):
    raw = proj_ref[j, :, 768:896].astype(f32) + hp_ref[j, 1:2]
    step = jnp.maximum(raw, 0.0) + jnp.log1p(jnp.exp(-jnp.abs(raw)))
    rate = -step * hp_ref[j, 0:1]
    cum = sum(dot(tri, part) for part in split3(rate))
    return raw, step, rate, cum


def triangle():
    t = lax.broadcasted_iota(jnp.int32, (256, 256), 0)
    return t >= lanes((256, 256))


def pair_of(cols, p):
    at = HEAD_AT + 2 * p
    first = jnp.broadcast_to(cols[:, at : at + 1], (256, 128))
    return jnp.where(lanes((256, 128)) < 64, first, cols[:, at + 1 : at + 2])


def fade_of(cum, cum_rows, h, inside):
    at = HEAD_AT + h
    return jnp.exp(jnp.where(inside, cum[:, at : at + 1] - cum_rows[at : at + 1], -1e30))


def forward_kernel(
    x_ref, g_ref, w_in_ref, w_out_ref, cx_ref, cbc_ref, hp_ref, marks_ref, seg_ref,
    normed_ref, proj_ref, y_ref, scaled_ref, part_ref, squares_ref, scores_ref,
):
    i = pl.program_id(0)

    @pl.when(i == 0)
    def _():
        x = x_ref[...].astype(f32)
        normed_ref[...] = (x * rms(x) * g_ref[0:1]).astype(bf16)

    @pl.when(i < 4)
    def _():
        proj_ref[i] = dot(normed_ref[...], w_in_ref[0]).astype(bf16)

    @pl.when(i == 4)
    def _():
        marks = marks_ref[...]
        b_mat, c_mat = [jax.nn.silu(taps_pre(bc_raw(proj_ref, k), marks, cbc_ref[k])) for k in (0, 1)]
        scores_ref[...] = dot(c_mat.astype(bf16), b_mat.astype(bf16), ((1,), (1,)))
        part_ref[...] = jnp.zeros_like(part_ref)
        squares_ref[...] = jnp.zeros_like(squares_ref)

    @pl.when(i >= 4)
    def _():
        j = i - 4
        marks, cx = marks_ref[...], cx_ref[j]
        causal = triangle()
        inside = causal & (marks[:, 4:5] == seg_ref[0:1])
        _, step, _, cum = head_steps(proj_ref, hp_ref, j, causal.astype(bf16))
        cum_rows = cum.T
        x = jax.nn.silu(taps_pre(proj_ref[j, :, 384:768].astype(f32), marks, cx))
        scores = scores_ref[...]
        ys = []
        for p in range(3):
            xp = x[:, 128 * p : 128 * p + 128]
            xs = (xp * pair_of(step, p)).astype(bf16)
            y0, y1 = [
                dot((fade_of(cum, cum_rows, 2 * p + k, inside) * scores).astype(bf16), xs)
                for k in (0, 1)
            ]
            ys.append(jnp.where(lanes((256, 128)) < 64, y0, y1))
        y = jnp.concatenate(ys, axis=1) + cx[5:6] * x
        z = proj_ref[j, :, :384].astype(f32)
        gated = y * jax.nn.silu(z)
        scaled = (gated * cx[6:7]).astype(bf16)
        y_ref[j] = y
        scaled_ref[j] = scaled
        squares_ref[...] += jnp.broadcast_to(
            jnp.sum(gated * gated, axis=1, keepdims=True), squares_ref.shape
        )
        for c in range(4):
            part_ref[:, c * 384 : c * 384 + 384] += dot(scaled, w_out_ref[c])


def fixed(v):
    return pl.BlockSpec(v.shape, lambda i: (0,) * len(v.shape))


def mixer_forward(x, g, w_in, w_out, cx, cbc, hp, marks, seg):
    outs = [
        jax.ShapeDtypeStruct((256, 1536), bf16),
        jax.ShapeDtypeStruct((4, 256, 896), bf16),
        jax.ShapeDtypeStruct((4, 256, 384), f32),
        jax.ShapeDtypeStruct((4, 256, 384), bf16),
        jax.ShapeDtypeStruct((256, 1536), f32),
        jax.ShapeDtypeStruct((256, 128), f32),
    ]
    return pl.pallas_call(
        forward_kernel,
        grid=(8,),
        out_shape=outs,
        in_specs=[
            fixed(x),
            fixed(g),
            pl.BlockSpec((1, 1536, 896), lambda i: (jnp.minimum(i, 3), 0, 0)),
            pl.BlockSpec((4, 384, 384), lambda i: (0, jnp.maximum(i - 4, 0), 0)),
            *[fixed(v) for v in (cx, cbc, hp, marks, seg)],
        ],
        out_specs=[fixed(o) for o in outs],
        scratch_shapes=[pltpu.VMEM((256, 256), f32)],
        compiler_params=pltpu.CompilerParams(vmem_limit_bytes=48 * 2**20),
        cost_estimate=pl.CostEstimate(
            flops=2 * 256 * 1536 * (3584 + 1536), bytes_accessed=22 * 2**20, transcendentals=2**21
        ),
        name="mixer_forward",
    )(x, g, w_in, w_out, cx, cbc, hp, marks, seg)


def backward_kernel(
    dm_ref, kappa_ref, w_out_ref, w_in_ref, normed_ref, ffn_ref, drout_ref, proj_ref, y_ref,
    scaled_ref, cx_ref, cbc_ref, hp_ref, marks_ref, seg_ref, x_ref,
    gout_ref, gin_ref, dn_ref, gcx_ref, gcbc_ref, gheads_ref, gnorm_ref,
    dproj_ref, scores_ref, dscores_ref, bc_ref, w_ref, fetched,
):
    i = pl.program_id(0)

    def fetch(j):
        return pltpu.make_async_copy(w_in_ref.at[j], w_ref.at[j], fetched.at[j])

    @pl.when(i == 0)
    def _():
        for j in range(4):
            fetch(j).start()
        marks = marks_ref[...]
        for k in (0, 1):
            bc_ref[k] = jax.nn.silu(taps_pre(bc_raw(proj_ref, k), marks, cbc_ref[k])).astype(bf16)
        scores_ref[...] = dot(bc_ref[1], bc_ref[0], ((1,), (1,)))
        dscores_ref[...] = jnp.zeros_like(dscores_ref)

    @pl.when(i < 4)
    def _():
        j = i
        marks, cx = marks_ref[...], cx_ref[j]
        scaled = scaled_ref[0]
        d_scaled = jnp.zeros((256, 384), f32)
        for c in range(4):
            dm = dm_ref[:, c * 384 : c * 384 + 384]
            d_scaled = d_scaled + dot(dm, w_out_ref[c], ((1,), (1,)))
            gout_ref[c] = dot(scaled, dm, ((0,), (0,))).astype(bf16)
        y = y_ref[0]
        z = proj_ref[j, :, :384].astype(f32)
        sig = jax.nn.sigmoid(z)
        gate = z * sig
        gated = y * gate
        d_gated = d_scaled * cx[6:7] - kappa_ref[:, 0:1] * gated
        dy = d_gated * gate
        dproj_ref[j, :, :384] = (d_gated * y * (sig + gate * (1.0 - sig))).astype(bf16)
        norm_grad = jnp.sum(d_scaled * gated, axis=0, keepdims=True)

        causal = triangle()
        inside = causal & (marks[:, 4:5] == seg_ref[0:1])
        raw, step, rate, cum = head_steps(proj_ref, hp_ref, j, causal.astype(bf16))
        cum_rows = cum.T
        x_raw = proj_ref[j, :, 384:768].astype(f32)
        x_pre = taps_pre(x_raw, marks, cx)
        x_sig = jax.nn.sigmoid(x_pre)
        x = x_pre * x_sig
        scores = scores_ref[...]
        d_scores = dscores_ref[...]
        lane = lanes((256, 128))
        low_half = lane < 64
        row = lax.broadcasted_iota(jnp.int32, (128, 256), 0)
        d_cum = jnp.zeros((256, 128), f32)
        d_cum_rows = jnp.zeros((128, 256), f32)
        d_step = jnp.zeros((256, 128), f32)
        dxs = []
        for p in range(3):
            xp = x[:, 128 * p : 128 * p + 128]
            dyp = dy[:, 128 * p : 128 * p + 128]
            steps = pair_of(step, p)
            xs = (xp * steps).astype(bf16)
            dy_low = dyp.astype(bf16)
            back = []
            for k in (0, 1):
                at = HEAD_AT + 2 * p + k
                fade = fade_of(cum, cum_rows, 2 * p + k, inside)
                mine = jnp.where(low_half if k == 0 else ~low_half, dyp, 0.0).astype(bf16)
                pair = dot(mine, xs, ((1,), (1,)))
                mixing = fade * scores
                w = mixing * pair
                d_scores = d_scores + fade * pair
                d_cum = jnp.where(lane == at, jnp.sum(w, axis=1, keepdims=True), d_cum)
                d_cum_rows = jnp.where(row == at, jnp.sum(w, axis=0, keepdims=True), d_cum_rows)
                back.append(dot(mixing.astype(bf16), dy_low, ((0,), (0,))))
            d_xs = jnp.where(low_half, back[0], back[1])
            prod = xp * d_xs
            first = jnp.sum(jnp.where(low_half, prod, 0.0), axis=1, keepdims=True)
            second = jnp.sum(jnp.where(low_half, 0.0, prod), axis=1, keepdims=True)
            at = HEAD_AT + 2 * p
            d_step = jnp.where(lane == at, first, jnp.where(lane == at + 1, second, d_step))
            dxs.append(d_xs * steps)
        dscores_ref[...] = d_scores
        dx = jnp.concatenate(dxs, axis=1) + cx[5:6] * dy
        skip_grad = jnp.sum(x * dy, axis=0, keepdims=True)
        d_x_pre = dx * (x_sig + x * (1.0 - x_sig))
        d_x_raw, conv_grad = taps_back(d_x_pre, x_raw, marks, cx)
        dproj_ref[j, :, 384:768] = d_x_raw.astype(bf16)
        rowid = lax.broadcasted_iota(jnp.int32, (8, 384), 0)
        gcx_ref[j] = jnp.where(rowid == 5, skip_grad, jnp.where(rowid == 6, norm_grad, conv_grad))
        d_cum = d_cum - d_cum_rows.T
        d_rate = sum(dot(causal.astype(bf16), part, ((0,), (0,))) for part in split3(d_cum))
        d_raw = (d_step - d_rate * hp_ref[j, 0:1]) * jax.nn.sigmoid(raw)
        dproj_ref[j, :, 768:896] = d_raw.astype(bf16)
        rowid = lax.broadcasted_iota(jnp.int32, (8, 128), 0)
        gheads_ref[j] = jnp.where(
            rowid == 0,
            jnp.sum(d_rate * rate, axis=0, keepdims=True),
            jnp.where(rowid == 1, jnp.sum(d_raw, axis=0, keepdims=True), 0.0),
        )

    @pl.when(i == 4)
    def _():
        marks = marks_ref[...]
        d_scores = dscores_ref[...].astype(bf16)
        d_bc = (dot(d_scores, bc_ref[1], ((0,), (0,))), dot(d_scores, bc_ref[0]))
        low_half = lanes((256, 128)) < 64
        for k in (0, 1):
            raw = bc_raw(proj_ref, k)
            pre = taps_pre(raw, marks, cbc_ref[k])
            sig = jax.nn.sigmoid(pre)
            d_pre = d_bc[k] * (sig + pre * sig * (1.0 - sig))
            d_raw, conv_grad = taps_back(d_pre, raw, marks, cbc_ref[k])
            gcbc_ref[k] = conv_grad
            for h, moved in enumerate((d_raw, roll(d_raw, 64, 1))):
                steps = dproj_ref[2 * k + h, :, 768:896].astype(f32)
                dproj_ref[2 * k + h, :, 768:896] = jnp.where(low_half, moved, steps).astype(bf16)
        dn_ref[...] = jnp.zeros_like(dn_ref)

    @pl.when(i >= 4)
    def _():
        j = i - 4
        d_proj = dproj_ref[j]
        fetch(j).wait()
        dn_ref[...] += dot(d_proj, w_ref[j], ((1,), (1,)))
        gin_ref[0, :, :768] = dot(normed_ref[...], d_proj[:, :768], ((0,), (0,))).astype(bf16)
        last = dot(normed_ref[...], d_proj[:, 768:], ((0,), (0,)))
        last = last + dot(ffn_ref[...], drout_ref[j], ((0,), (0,)))
        gin_ref[0, :, 768:] = last.astype(bf16)

    @pl.when(i == 7)
    def _():
        x = x_ref[...].astype(f32)
        total = jnp.sum(dn_ref[...] * x * rms(x), axis=0, keepdims=True)
        gnorm_ref[...] = jnp.broadcast_to(total, gnorm_ref.shape)


def mixer_backward(dm, kappa, w_out, w_in, normed, ffn_in, drout, proj, y, scaled, *rest):
    def late(i):
        return jnp.maximum(i - 4, 0)

    def early(i):
        return jnp.minimum(i, 3)

    small = [
        jax.ShapeDtypeStruct((256, 1536), f32),
        jax.ShapeDtypeStruct((4, 8, 384), f32),
        jax.ShapeDtypeStruct((2, 8, 128), f32),
        jax.ShapeDtypeStruct((4, 8, 128), f32),
        jax.ShapeDtypeStruct((8, 1536), f32),
    ]
    w_out_spec = pl.BlockSpec((4, 384, 384), lambda i: (0, early(i), 0))
    w_in_spec = pl.BlockSpec((1, 1536, 896), lambda i: (late(i), 0, 0))
    return pl.pallas_call(
        backward_kernel,
        grid=(8,),
        out_shape=[
            jax.ShapeDtypeStruct((4, 1536, 384), bf16),
            jax.ShapeDtypeStruct((4, 1536, 896), bf16),
            *small,
        ],
        in_specs=[
            fixed(dm),
            fixed(kappa),
            w_out_spec,
            pl.BlockSpec(memory_space=pl.ANY),
            *[fixed(v) for v in (normed, ffn_in, drout, proj)],
            *[pl.BlockSpec((1, 256, 384), lambda i: (early(i), 0, 0))] * 2,
            *[fixed(v) for v in rest],
        ],
        out_specs=[w_out_spec, w_in_spec, *[fixed(o) for o in small]],
        scratch_shapes=[
            pltpu.VMEM((4, 256, 896), bf16),
            pltpu.VMEM((256, 256), f32),
            pltpu.VMEM((256, 256), f32),
            pltpu.VMEM((2, 256, 128), bf16),
            pltpu.VMEM((4, 1536, 896), bf16),
            pltpu.SemaphoreType.DMA((4,)),
        ],
        compiler_params=pltpu.CompilerParams(vmem_limit_bytes=56 * 2**20),
        cost_estimate=pl.CostEstimate(
            flops=0, bytes_accessed=0, transcendentals=0
        ),
        name="mixer_backward",
    )(dm, kappa, w_out, w_in, normed, ffn_in, drout, proj, y, scaled, *rest)


def swap(v):
    return lax.ppermute(v, "seq", [(0, 1), (1, 0)])


def both_halves(own, other, s):
    first = jnp.where(s == 0, own, other)
    second = jnp.where(s == 0, other, own)
    return jnp.concatenate([first, second], axis=0)


def halves(v, s):
    rows = v.shape[0] // 2
    return (
        lax.dynamic_slice_in_dim(v, s * rows, rows, 0),
        lax.dynamic_slice_in_dim(v, (1 - s) * rows, rows, 0),
    )


def hi_lo(v):
    hi = v.astype(bf16)
    return hi, (v - hi.astype(f32)).astype(bf16)


def rms(v):
    return lax.rsqrt(jnp.mean(v * v, axis=-1, keepdims=True) + EPS)


def silu_grad(v):
    sig = jax.nn.sigmoid(v)
    return sig * (1.0 + v * (1.0 - sig))


def local(
    tokens,
    out_grad,
    lengths,
    routes,
    in_norm,
    in_proj,
    conv_weight,
    conv_bias,
    head_params,
    mixer_norm,
    out_proj,
    ffn_norm,
    router,
    shared_gate_up,
    shared_down,
    expert_gate_up,
    expert_down,
):
    s = lax.axis_index("seq")
    dp = lax.axis_index(DP)
    experts, slots = 64, 24
    n_slots = experts * slots

    other_tokens = swap(tokens)
    other_grad = swap(out_grad)
    other_gate_up = swap(expert_gate_up[0])
    other_down = swap(expert_down[0])
    w_in, w_sgu, w_out, w_sdown, vecs = gather(
        in_proj,
        shared_gate_up,
        router,
        jnp.concatenate([out_proj, shared_down], axis=0),
        (in_norm[None], ffn_norm[None], mixer_norm[None], conv_weight.T, conv_bias[None]),
    )
    w_in = w_in.reshape(4, 1536, 896)
    w_sgu = w_sgu.reshape(4, 1536, 256)
    w_out = w_out.reshape(4, 1536, 384)
    w_sdown = w_sdown.reshape(4, 512, 384)

    vecs = vecs.reshape(128, 16, 128).astype(f32)
    g_in = vecs[:, 0, :12].reshape(1, 1536)
    g_ffn = vecs[:, 1, :12].reshape(1536)
    g_mix = lax.dynamic_slice_in_dim(vecs[:, 2, :24].reshape(1, 3072), s * 1536, 1536, 1)
    conv = vecs[:, 3:8, :26].transpose(1, 0, 2).reshape(5, 3328)
    heads = lax.dynamic_slice_in_dim(head_params.astype(f32), s * 24, 24, 1)
    cx = jnp.concatenate(
        [
            lax.dynamic_slice_in_dim(conv[:, :3072], s * 1536, 1536, 1),
            jnp.broadcast_to(heads[2][:, None], (24, 64)).reshape(1, 1536),
            g_mix,
            jnp.zeros((1, 1536), f32),
        ],
        axis=0,
    )
    cx = cx.reshape(8, 4, 384).transpose(1, 0, 2)
    cbc = jnp.pad(conv[:, 3072:], ((0, 3), (0, 0))).reshape(8, 2, 128).transpose(1, 0, 2)
    hp = jnp.stack([jnp.exp(heads[0]), heads[1]]).reshape(2, 4, 6).transpose(1, 0, 2)
    hp = jnp.pad(hp, ((0, 0), (0, 6), (HEAD_AT, 122 - HEAD_AT)))
    w_eg = both_halves(expert_gate_up[0], other_gate_up, s)
    w_ed = both_halves(expert_down[0], other_down, s)

    ids = jnp.arange(experts, dtype=jnp.int32)
    named = jnp.sum((routes[:, :, None] == ids).astype(f32), axis=1)
    t128 = jnp.arange(128)
    before = (t128[:, None] > t128[None, :]).astype(bf16)
    rank = dot(before, named.astype(bf16))
    slot = jnp.arange(n_slots, dtype=jnp.int32)
    spread = (slot[None, :] // slots == ids[:, None]).astype(bf16)
    is_named = dot(named.astype(bf16), spread) > 0.5
    in_slot = dot(rank.astype(bf16), spread) == (slot % slots).astype(f32)[None, :]
    place = (is_named & in_slot).astype(bf16)

    def to_slots(v):
        return dot(place, v, ((0,), (0,))).astype(bf16).reshape(experts, slots, v.shape[1])

    grad_slots, w_in = lax.optimization_barrier((to_slots(out_grad), w_in))
    grad_rows = lax.all_to_all(grad_slots, DP, 0, 0, tiled=True).reshape(n_slots, 1536)

    ends = jnp.cumsum(lengths[0])
    t256 = jnp.arange(256, dtype=jnp.int32)
    segment = jnp.sum((t256[:, None] >= ends[None, :]).astype(jnp.int32), axis=1)
    seg = segment.astype(f32)
    same = [
        (jnp.pad(segment, (d, 0), constant_values=-1)[:256] == segment).astype(f32)
        for d in range(4)
    ]
    marks = jnp.pad(jnp.stack(same + [seg], axis=1), ((0, 0), (0, 123)))
    seg = jnp.broadcast_to(seg, (8, 256))
    x_full = both_halves(tokens, other_tokens, s)
    normed, proj, y, scaled, part, squares = mixer_forward(
        x_full, jnp.broadcast_to(g_in, (8, 1536)), w_in, w_out, cx, cbc, hp, marks, seg
    )
    squares = squares[:, :1]
    part_own, part_other = halves(part, s)
    sq_own, sq_other = halves(squares, s)
    part = part_own + swap(part_other)
    q = lax.rsqrt((sq_own + swap(sq_other)) / 3072.0 + EPS)
    residual = tokens.astype(f32) + q * part

    r = rms(residual)
    ffn_in = (residual * r * g_ffn).astype(bf16)
    w_router = w_in[:, :, 832:848].transpose(1, 0, 2).reshape(1536, 64)
    logits = dot(ffn_in, w_router)
    logits = jnp.where(named > 0.5, logits, -1e30)
    top = jnp.max(logits, axis=1, keepdims=True)
    weights = jnp.where(named > 0.5, jnp.exp(logits - top), 0.0)
    gating = weights / jnp.sum(weights, axis=1, keepdims=True)
    gate_hi, gate_lo = hi_lo(gating)
    sent = to_slots(jnp.concatenate([ffn_in, gate_hi, gate_lo], axis=1))
    sent, grad_rows = lax.optimization_barrier((sent, grad_rows))
    arrived = lax.all_to_all(sent, DP, 0, 0, tiled=True).reshape(n_slots, 1664)

    ffn_full = both_halves(ffn_in, swap(ffn_in), s)
    og_full = both_halves(out_grad, other_grad, s)
    sgu = jnp.stack([dot(ffn_full, w_sgu[j]) for j in range(4)])
    sg, su = sgu[..., :128], sgu[..., 128:]
    s_act = (jax.nn.silu(sg) * su).astype(bf16)
    s_flat = s_act.transpose(1, 0, 2).reshape(256, 512)
    s_out = jnp.concatenate([dot(s_flat, w_sdown[j]) for j in range(4)], axis=1)
    s_own, s_other = halves(s_out, s)
    s_out = s_own + swap(s_other.astype(bf16)).astype(f32)
    og_cols = og_full.reshape(256, 4, 384).transpose(1, 0, 2)
    d_s_act = sum(dot(og_cols[j], w_sdown[j], ((1,), (1,))) for j in range(4))
    d_s_act = d_s_act.reshape(256, 4, 128).transpose(1, 0, 2)
    d_sgu = jnp.concatenate([d_s_act * su * silu_grad(sg), d_s_act * jax.nn.silu(sg)], axis=-1)
    d_sgu = d_sgu.astype(bf16)
    grad_sdown = jnp.stack([dot(s_flat, og_cols[j], ((0,), (0,))) for j in range(4)]).astype(bf16)
    grad_sgu = jnp.stack([dot(ffn_full, d_sgu[j], ((0,), (0,))) for j in range(4)]).astype(bf16)
    d_ffn = sum(dot(d_sgu[j], w_sgu[j], ((1,), (1,))) for j in range(4))
    df_own, df_other = halves(d_ffn, s)
    d_ffn = df_own + swap(df_other.astype(bf16)).astype(f32)

    lane = jnp.arange(128, dtype=jnp.int32) % 64
    pick = (lane == dp).astype(f32)[None, :]
    d_rows, e_act, w_act, w_gu = expert_grads(arrived, grad_rows, w_eg, w_ed, pick)
    d_back = lax.all_to_all(d_rows.reshape(experts, slots, 1664), DP, 0, 0, tiled=True)
    e_out = dot(e_act, w_ed).astype(bf16)
    grad_ed = dot(w_act, grad_rows, ((0,), (0,)))
    grad_eg = dot(arrived[:, :1536], w_gu, ((0,), (0,)))
    ge_own, ge_other = halves(grad_eg, s)
    grad_eg = ge_own + swap(ge_other.astype(bf16)).astype(f32)
    gd_own, gd_other = halves(grad_ed, s)
    grad_ed = gd_own + swap(gd_other.astype(bf16)).astype(f32)
    e_out, d_back, grad_eg, grad_ed, d_ffn, grad_sgu, grad_sdown = lax.optimization_barrier(
        (e_out, d_back, grad_eg, grad_ed, d_ffn, grad_sgu, grad_sdown)
    )
    d_back = d_back.reshape(n_slots, 1664)
    out_back = lax.all_to_all(e_out.reshape(experts, slots, 1536), DP, 0, 0, tiled=True)
    out_back = out_back.reshape(n_slots, 1536)

    wide_gate = dot(gate_hi, spread) + dot(gate_lo, spread)
    weighted = (place.astype(f32) * wide_gate).astype(bf16)
    d_route = dot(weighted, d_back[:, :1536])
    dg = d_back[:, 1536:1538].T
    d_gating = dot(place * dg[0:1], spread, ((1,), (1,))) + dot(
        place * dg[1:2], spread, ((1,), (1,))
    )
    d_logits = gating * (d_gating - jnp.sum(gating * d_gating, axis=1, keepdims=True))
    d_logits_low = d_logits.astype(bf16)
    d_ffn = d_ffn + dot(d_logits_low, w_router, ((1,), (1,))) + d_route
    ffn_norm_grad = jnp.sum(d_ffn * residual * r, axis=0)
    u = d_ffn * g_ffn
    d_residual = (
        out_grad.astype(f32)
        + r * u
        - r * r * r * residual * jnp.mean(u * residual, axis=1, keepdims=True)
    )

    d_mixed = (q * d_residual).astype(bf16)
    kappa = q * q / 3072.0 * jnp.sum(d_mixed.astype(f32) * part, axis=1, keepdims=True)
    d_mixed_full = both_halves(d_mixed, swap(d_mixed), s)
    kappa = both_halves(kappa, swap(kappa), s)
    drout = jnp.pad(d_logits_low.reshape(128, 4, 16).transpose(1, 0, 2), ((0, 0), (0, 0), (64, 48)))
    grad_out, grad_in, d_normed, g_cx, g_cbc, g_heads, in_norm_grad = mixer_backward(
        d_mixed_full, kappa, w_out, w_in, normed, ffn_in, drout, proj, y, scaled, cx, cbc, hp, marks, seg, x_full
    )
    conv_x_grad = g_cx[:, :5].transpose(1, 0, 2).reshape(5, 1536)
    conv_bc_grad = g_cbc[:, :5].transpose(1, 0, 2).reshape(5, 256)
    mixer_norm_grad = g_cx[:, 6].reshape(1536)
    head_grad = g_heads[:, :2, HEAD_AT : HEAD_AT + 6].transpose(1, 0, 2).reshape(2, 24)
    d_skip = jnp.sum(g_cx[:, 5].reshape(24, 64), axis=1)
    head_grad = jnp.concatenate([head_grad, d_skip[None]], axis=0)
    dn_own, dn_other = halves(d_normed, s)
    dn_other = swap(dn_other.astype(bf16))

    conv_grad = lax.dynamic_update_slice(
        jnp.zeros((5, 3328), f32), conv_x_grad, (0, s * 1536)
    )
    conv_grad = lax.dynamic_update_slice(conv_grad, conv_bc_grad, (0, 3072))
    mixer_norm_grad = lax.dynamic_update_slice(
        jnp.zeros((128, 24), f32), mixer_norm_grad.reshape(64, 24), (s * 64, 0)
    )
    head_grad = lax.dynamic_update_slice(jnp.zeros((3, 48), f32), head_grad, (0, s * 24))
    def rows_of(v, width):
        return jnp.pad(v.reshape(128, 1, width), ((0, 0), (0, 0), (0, 64 - width)))

    conv_grad = conv_grad.reshape(5, 128, 26).transpose(1, 0, 2)
    small = jnp.concatenate(
        [
            rows_of(in_norm_grad[0], 12),
            rows_of(ffn_norm_grad, 12),
            rows_of(mixer_norm_grad, 24),
            jnp.pad(conv_grad, ((0, 0), (0, 0), (0, 38))),
        ],
        axis=1,
    )
    head_rows = jnp.broadcast_to(jnp.pad(head_grad, ((0, 5), (0, 16)))[None], (128, 8, 64))
    small = jnp.concatenate([small, head_rows], axis=2).reshape(2, 4, 4, 4, 8, 128)
    sums = scatter(
        (
            grad_in.reshape(4, 2, 4, 4, 48, 896),
            grad_sgu.reshape(4, 2, 4, 4, 48, 256),
            grad_out.reshape(4, 4, 4, 2, 48, 384),
            grad_sdown.reshape(4, 4, 4, 2, 16, 384),
            small,
        )
    )
    weighted_late, dn_own, sums = lax.optimization_barrier((weighted, dn_own, tuple(sums)))
    routed = dot(weighted_late, out_back)
    block_out = (residual + s_out + routed).astype(bf16)
    d_normed = dn_own + dn_other.astype(f32)
    x_own = tokens.astype(f32)
    p = rms(x_own)
    v = d_normed * g_in
    token_grad = (
        d_residual + p * v - p * p * p * x_own * jnp.mean(v * x_own, axis=1, keepdims=True)
    ).astype(bf16)
    (
        in_proj_grad, router_grad, sgu_grad, out_proj_grad, sdown_grad, head_grad, conv_grad,
        in_norm_grad, ffn_norm_grad, mixer_norm_grad, conv_bias_grad,
    ) = finish(*sums)
    return (
        block_out,
        token_grad,
        in_norm_grad[0],
        in_proj_grad,
        conv_grad,
        conv_bias_grad[0],
        head_grad,
        mixer_norm_grad[0],
        out_proj_grad,
        ffn_norm_grad[0],
        router_grad,
        sgu_grad,
        sdown_grad,
        grad_eg[None],
        grad_ed[None],
    )


def solution(mesh):
    finer = Mesh(mesh.devices.reshape(2, 4, 4, 4), ALL)
    placed = (
        P(DP_SEQ, None),
        P(DP_SEQ, None),
        P(DP, None),
        P(DP_SEQ, None),
        P(ALL),
        P(ALL, None),
        P(ALL, None),
        P(ALL),
        P(),
        P(ALL),
        P(ALL, None),
        P(ALL),
        P(ALL, None),
        P(ALL, None),
        P(ALL, None),
        P(DP, "seq", None),
        P(DP, "seq", None),
    )
    return jax.shard_map(
        local,
        mesh=finer,
        in_specs=placed,
        out_specs=(
            P(DP_SEQ, None),
            P(DP_SEQ, None),
            P(ALL),
            P(ALL, None),
            P(ALL, None),
            P(ALL),
            P(),
            P(ALL),
            P(ALL, None),
            P(ALL),
            P(ALL, None),
            P(ALL, None),
            P(ALL, None),
            P(DP, "seq", None),
            P(DP, "seq", None),
        ),
        check_vma=False,
    )
```
